32 devices in a mesh: dp: 4 (over z), ctx: 2 (over x), mp: 4 (over y, core).
Axes of the slice: x: 2, y: 2, z: 4, core: 2. Of those that a mesh axis runs over, the one named last changes fastest.
Arguments:
- tokens: bfloat16 [5632, 2304], P(('dp', 'ctx', 'mp')), may hold values from -6 to 6
- w_query: bfloat16 [2304, 2304], P(('dp', 'ctx'), 'mp'), may hold values from -0.125 to 0.125
- w_key: bfloat16 [2304, 2304], P(('dp', 'ctx'), 'mp'), may hold values from -0.125 to 0.125
- w_value: bfloat16 [2304, 2304], P(('dp', 'ctx'), 'mp'), may hold values from -0.125 to 0.125
- w_out: bfloat16 [2304, 2304], P('mp', ('dp', 'ctx')), may hold values from -3 to 3
- gain_attn: bfloat16 [2304], replicated, may hold values from 0.099609375 to 1.8984375
- w_gate: bfloat16 [2304, 5760], P(('dp', 'ctx'), 'mp'), may hold values from -0.125 to 0.125
- w_up: bfloat16 [2304, 5760], P(('dp', 'ctx'), 'mp'), may hold values from -0.125 to 0.125
- w_down: bfloat16 [5760, 2304], P('mp', ('dp', 'ctx')), may hold values from -0.625 to 0.625
- gain_mlp: bfloat16 [2304], replicated, may hold values from 0.099609375 to 1.8984375
- cotangent: bfloat16 [5632, 2304], P(('dp', 'ctx', 'mp')), may hold values from -6 to 6
- lineage: int32 [3, 5632], P(None, 'dp'), may hold values from 0 to 7, as said below
- padding: int32 [5632], P('dp'), may hold values from 0 to 1, as said below
- positions: int32 [5632], P('dp'), may hold values from 0 to 959, as said below
Outputs:
- output: bfloat16 [5632, 2304], P(('dp', 'ctx', 'mp'))
- input_grad: bfloat16 [5632, 2304], P(('dp', 'ctx', 'mp'))
- grad_query: float32 [2304, 2304], P(('dp', 'ctx'), 'mp')
- grad_key: float32 [2304, 2304], P(('dp', 'ctx'), 'mp')
- grad_value: float32 [2304, 2304], P(('dp', 'ctx'), 'mp')
- grad_out: float32 [2304, 2304], P('mp', ('dp', 'ctx'))
- grad_gain_attn: float32 [2304], replicated
- grad_gate: float32 [2304, 5760], P(('dp', 'ctx'), 'mp')
- grad_up: float32 [2304, 5760], P(('dp', 'ctx'), 'mp')
- grad_down: float32 [5760, 2304], P('mp', ('dp', 'ctx'))
- grad_gain_mlp: float32 [2304], replicated
The draws below stay inside these ranges and needn't reach their ends.
Inputs may be any that keep to these rules, and one draw needn't show every extreme that they name: `lineage`: each tree's slot of 1408 tokens holds a trunk of 768 tokens first, two branches of 128 tokens whose parent is the trunk, two leaves of 64 tokens under each branch, and one run of 128 padding tokens; every segment lies in consecutive tokens after its parent. Within a tree the seven segments carry distinct numbers 0 to 6; padding tokens carry 7 in all three rows. The trunk's parent and grandparent are the trunk itself, a branch's grandparent is the trunk. Exactly 128 padding tokens in each tree's slot, in one run after the trunk. `positions`: trunk tokens count 0 to 767, branch tokens continue from 768, leaf tokens from 896; padding tokens count from 0.
All inputs are finite; a program needn't handle non-finite values.
Results may differ from the reference program's by a relative error of at most 0.019.
Values may be sent and summed in bfloat16 or wider, within the bound.
No kernel may reach another device: no remote copies, remote signals or barrier semaphores. Data moves between devices by JAX's collectives and lax.ppermute only.
A program may use at most 192 MiB of HBM per device.

```python
import math
import jax
import jax.numpy as jnp
import numpy as np
from jax import lax

D = 2304
HEADS = 36
HEAD_DIM = 64
FF = 5760
TRUNK = 768
BRANCH = 128
LEAF = 64
PAD = 128
SLOT = 1408
TREES = 4
TOKENS = 5632


def layout_tables():
    unit_sizes = [TRUNK, BRANCH, BRANCH, LEAF, LEAF, LEAF, LEAF, PAD]
    leaf_start = TRUNK + BRANCH
    depth_start = [0, TRUNK, TRUNK, leaf_start, leaf_start, leaf_start, leaf_start, 0]
    role_rows = []
    place_rows = []
    for unit_order in ([1, 3, 4, 2, 5, 6], [1, 2, 3, 4, 5, 6], [2, 5, 6, 1, 3, 4], [2, 1, 5, 6, 3, 4]):
        for pad_spot in range(7):
            unit_seq = [0] + unit_order[:pad_spot] + [7] + unit_order[pad_spot:]
            role_line = []
            place_line = []
            for unit_id in unit_seq:
                role_line = role_line + [unit_id] * unit_sizes[unit_id]
                place_line = place_line + list(range(depth_start[unit_id], depth_start[unit_id] + unit_sizes[unit_id]))
            role_rows.append(role_line)
            place_rows.append(place_line)
    return (np.array(role_rows, dtype=np.int32), np.array(place_rows, dtype=np.int32))


def tree_layout(key):
    role_table, place_table = layout_tables()
    layout_pick = jax.random.randint(jax.random.fold_in(key, 11), (TREES,), 0, role_table.shape[0])
    label_keys = jax.random.split(jax.random.fold_in(key, 12), TREES)
    labels = jax.vmap(lambda label_key: jax.random.permutation(label_key, 7))(label_keys).astype(jnp.int32)
    labels = jnp.concatenate([labels, jnp.full((TREES, 1), 7, jnp.int32)], axis=1)
    roles_drawn = jnp.asarray(role_table)[layout_pick]
    places_drawn = jnp.asarray(place_table)[layout_pick]
    return (roles_drawn, places_drawn, labels)


def draw_lineage(key, part):
    roles_drawn, places_drawn, labels = tree_layout(key)
    parent_role = jnp.array([0, 0, 0, 1, 1, 2, 2, 7], jnp.int32)
    grand_role = jnp.array([0, 0, 0, 0, 0, 0, 0, 7], jnp.int32)
    own_label = jnp.take_along_axis(labels, roles_drawn, axis=1)
    parent_label = jnp.take_along_axis(labels, parent_role[roles_drawn], axis=1)
    grand_label = jnp.take_along_axis(labels, grand_role[roles_drawn], axis=1)
    return jnp.stack([own_label, parent_label, grand_label]).reshape(3, TOKENS).astype(jnp.int32)


def draw_padding(key, part):
    roles_drawn, places_drawn, labels = tree_layout(key)
    return (roles_drawn == 7).astype(jnp.int32).reshape(TOKENS)


def draw_positions(key, part):
    roles_drawn, places_drawn, labels = tree_layout(key)
    return places_drawn.reshape(TOKENS).astype(jnp.int32)


def levels(own_key, dims, cuts, low, high):
    factor_of, own = 1.0, jax.random.fold_in(own_key, 6)
    for dim, parts in cuts:
        draws = jnp.exp(jax.random.uniform(jax.random.fold_in(own, dim), (parts,), jnp.float32, low / len(cuts), high / len(cuts)))
        factor_of = factor_of * jnp.repeat(draws, dims[dim] // parts).reshape([-1 if axis == dim else 1 for axis in range(len(dims))])
    return factor_of


def bell_draw(stream_key, dims, spread, limit, cuts=(), kind=jnp.bfloat16):
    values = jax.random.normal(stream_key, dims, jnp.float32) * spread
    if len(cuts) > 0:
        values = levels(stream_key, dims, cuts, -0.22, 0.18) * values
    return jnp.clip(values, min=-limit, max=limit).astype(kind)


def setup_inputs(seed: int = 0) -> dict:
    keys = jax.random.split(jax.random.key(seed), 15)
    tokens = bell_draw(keys[0], (TOKENS, D), 1.0, 6.0, ((0, 32),))
    w_query = bell_draw(keys[1], (D, D), D ** -0.5, 0.125, ((0, 8), (1, 4)))
    w_key = bell_draw(keys[2], (D, D), D ** -0.5, 0.125, ((0, 8), (1, 4)))
    w_value = bell_draw(keys[3], (D, D), D ** -0.5, 0.125, ((0, 8), (1, 4)))
    w_out = bell_draw(keys[4], (D, D), (max(1, D // 512)) ** -0.5, 3.0, ((0, 4), (1, 8)))
    gain_attn = jnp.clip(1.0 + 0.18 * jax.random.normal(keys[5], (D,), jnp.float32), 0.099609375, 1.8984375).astype(jnp.bfloat16)
    w_gate = bell_draw(keys[6], (D, FF), D ** -0.5, 0.125, ((0, 8), (1, 4)))
    w_up = bell_draw(keys[7], (D, FF), D ** -0.5, 0.125, ((0, 8), (1, 4)))
    w_down = bell_draw(keys[8], (FF, D), (max(1, FF // 64)) ** -0.5, 0.625, ((0, 4), (1, 8)))
    gain_mlp = jnp.clip(1.0 + 0.18 * jax.random.normal(keys[9], (D,), jnp.float32), 0.099609375, 1.8984375).astype(jnp.bfloat16)
    cotangent = bell_draw(keys[10], (TOKENS, D), 1.0, 6.0, ((0, 32),))
    lineage = draw_lineage(jax.random.fold_in(keys[14], 71), 0)
    padding = draw_padding(jax.random.fold_in(keys[14], 71), 0)
    positions = draw_positions(jax.random.fold_in(keys[14], 71), 0)
    return {"tokens": tokens, "w_query": w_query, "w_key": w_key, "w_value": w_value, "w_out": w_out, "gain_attn": gain_attn, "w_gate": w_gate, "w_up": w_up, "w_down": w_down, "gain_mlp": gain_mlp, "cotangent": cotangent, "lineage": lineage, "padding": padding, "positions": positions}


@jax.custom_vjp
def low(v):
    return lax.optimization_barrier(v.astype(jnp.bfloat16)).astype(jnp.float32)

@jax.custom_vjp
def low_back(v):
    return v

def low_keep(v):
    return (low(v), None)

def low_pass(kept, grad):
    return (grad,)

def back_keep(v):
    return (v, None)

def back_low(kept, grad):
    return (low(grad),)
low.defvjp(low_keep, low_pass)
low_back.defvjp(back_keep, back_low)
eps = 1e-05
branch_scale = 1.4 / math.sqrt(40.0)
rope_base = 10000.0
masked_value = -1e+30
top_precision = lax.Precision.HIGHEST

def product(left, right):
    return jnp.dot(left, right, precision=top_precision, preferred_element_type=jnp.float32)

def normalize(field):
    return field * lax.rsqrt(lax.optimization_barrier(jnp.mean(field * field, axis=-1, keepdims=True)) + eps)

def rope_tables(places):
    half_dim = HEAD_DIM // 2
    inv_freq = rope_base ** (-2.0 * jnp.arange(half_dim, dtype=jnp.float32) / HEAD_DIM)
    angles = places.astype(jnp.float32)[:, None] * inv_freq[None, :]
    return (jnp.cos(angles)[:, None, :], jnp.sin(angles)[:, None, :])

def rotate(field, cosine_table, sine_table):
    half_dim = field.shape[-1] // 2
    first_half = field[..., :half_dim]
    second_half = field[..., half_dim:]
    return jnp.concatenate([first_half * cosine_table - second_half * sine_table, second_half * cosine_table + first_half * sine_table], axis=-1)

def visible(tree_lineage, tree_padding):
    token_index = jnp.arange(SLOT, dtype=jnp.int32)
    own_seg = tree_lineage[0]
    related = (own_seg[None, :] == tree_lineage[0][:, None]) | (own_seg[None, :] == tree_lineage[1][:, None]) | (own_seg[None, :] == tree_lineage[2][:, None])
    live_mask = tree_padding == 0
    earlier = token_index[None, :] < token_index[:, None]
    return (token_index[None, :] == token_index[:, None]) | related & earlier & live_mask[:, None] & live_mask[None, :]

def block_forward(inputs, weights, allowed, cosine_table, sine_table):
    w_query, w_key, w_value, w_out, gain_attn, w_gate, w_up, w_down, gain_mlp = weights
    normed = low(normalize(inputs) * gain_attn)
    query_rows = low_back(product(normed, w_query)).reshape(SLOT, HEADS, HEAD_DIM)
    key_rows = low_back(product(normed, w_key)).reshape(SLOT, HEADS, HEAD_DIM)
    value_rows = low(low_back(product(normed, w_value))).reshape(SLOT, HEADS, HEAD_DIM)
    query_rows = low(rotate(query_rows, cosine_table, sine_table))
    key_rows = low(rotate(key_rows, cosine_table, sine_table))
    score_scale = HEAD_DIM ** (-0.5)

    def one_head(pieces):
        query_head, key_head, value_head = pieces
        scores = low_back(jnp.dot(query_head, key_head.T, precision=top_precision) * score_scale)
        scores = jnp.where(allowed, scores, masked_value)
        row_max = lax.optimization_barrier(jnp.max(scores, axis=1, keepdims=True))
        exp_scores = jnp.exp(scores - row_max)
        probs = low(exp_scores / lax.optimization_barrier(jnp.sum(exp_scores, axis=1, keepdims=True)))
        return jnp.dot(probs, value_head, precision=top_precision)
    mixed_heads = lax.map(jax.checkpoint(one_head), (query_rows.transpose(1, 0, 2), key_rows.transpose(1, 0, 2), value_rows.transpose(1, 0, 2)))
    mixed_heads = low(low_back(mixed_heads.transpose(1, 0, 2).reshape(SLOT, D)))
    residual = inputs + branch_scale * low_back(product(mixed_heads, w_out))
    normed_mlp = low(normalize(residual) * gain_mlp)
    gate_proj = low_back(product(normed_mlp, w_gate))
    up_proj = low_back(product(normed_mlp, w_up))
    hidden = low(jax.nn.silu(gate_proj) * up_proj)
    return residual + branch_scale * low_back(product(hidden, w_down))

def reference(tokens, w_query, w_key, w_value, w_out, gain_attn, w_gate, w_up, w_down, gain_mlp, cotangent, lineage, padding, positions):
    weights = tuple((weight.astype(jnp.float32) for weight in (w_query, w_key, w_value, w_out, gain_attn, w_gate, w_up, w_down, gain_mlp)))
    tree_inputs = tokens.reshape(TREES, SLOT, D)
    tree_cotangents = cotangent.reshape(TREES, SLOT, D)
    tree_lineages = lineage.reshape(3, TREES, SLOT).transpose(1, 0, 2)
    tree_paddings = padding.reshape(TREES, SLOT)
    tree_places = positions.reshape(TREES, SLOT)

    def one_tree(totals, tree_item):
        tree_input, tree_cot, tree_lineage, tree_padding, tree_place = tree_item
        allowed = visible(tree_lineage, tree_padding)
        cosine_table, sine_table = rope_tables(tree_place)

        def forward(inputs, *params):
            return block_forward(inputs, params, allowed, cosine_table, sine_table)
        tree_out, pullback = jax.vjp(forward, tree_input.astype(jnp.float32), *weights)
        grads = pullback(tree_cot.astype(jnp.float32))
        totals = tuple((left + right for left, right in zip(totals, grads[1:])))
        return (totals, (tree_out.astype(jnp.bfloat16), grads[0].astype(jnp.bfloat16)))
    zeros = tuple((jnp.zeros(weight.shape, jnp.float32) for weight in weights))
    totals, (outputs, input_grads) = lax.scan(one_tree, zeros, (tree_inputs, tree_cotangents, tree_lineages, tree_paddings, tree_places))
    return (outputs.reshape(TOKENS, D), input_grads.reshape(TOKENS, D), totals[0], totals[1], totals[2], totals[3], totals[4], totals[5], totals[6], totals[7], totals[8])
```

```python
import functools
import math

import jax
import jax.numpy as jnp
from jax import lax
from jax.experimental import pallas as pl
from jax.experimental.pallas import tpu as pltpu
from jax.sharding import PartitionSpec as P

HEAD_DIM = 64
LANES = 128
PAIRS = 2
TILE = 128

eps = 1e-05
branch_scale = 1.4 / math.sqrt(40.0)
rope_base = 10000.0
masked_value = -1e30

f32 = jnp.float32
bf16 = jnp.bfloat16

NN = (((1,), (0,)), ((), ()))
NT = (((1,), (1,)), ((), ()))
TN = (((0,), (0,)), ((), ()))


def dot(left, right, dims=NN):
    return lax.dot_general(left, right, dims, preferred_element_type=f32)


def normalize(field):
    return field * lax.rsqrt(jnp.mean(field * field, axis=-1, keepdims=True) + eps)


def norm_back(field, gain_f32, incoming):
    inverse = lax.rsqrt(jnp.mean(field * field, axis=-1, keepdims=True) + eps)
    scaled = gain_f32 * incoming
    along = jnp.mean(field * scaled, axis=-1, keepdims=True)
    return (
        inverse * scaled - field * inverse**3 * along,
        jnp.sum(incoming * field * inverse, axis=0),
    )


def flip_x(field):
    return lax.ppermute(field, "ctx", [(0, 1), (1, 0)])


def flip_y(field):
    return lax.ppermute(field, "mp", [(0, 2), (2, 0), (1, 3), (3, 1)])


def flip_core(field):
    return lax.ppermute(field, "mp", [(0, 1), (1, 0), (2, 3), (3, 2)])


def gather_rows(own):
    half = own.shape[0] // 2
    from_x, from_y = flip_x(own), flip_y(own)
    corner = jnp.concatenate([flip_y(from_x[:half]), flip_x(from_y[half:])], axis=0)
    near = jnp.concatenate([own, from_y, from_x, corner], axis=0)
    return jnp.concatenate([near, flip_core(near)], axis=0)


def sum_rows(left, right, dims):
    count = left.shape[0] // 2
    block = count // 4
    half = block // 2
    away = flip_core(dot(left[count:], right, dims).astype(bf16))
    total = dot(left[:count], right, dims) + away.astype(f32)
    total = total.reshape(2, 2, block, total.shape[-1])
    got_x = flip_x(total[1, :, :half].astype(bf16)).astype(f32)
    got_y = flip_y(total[:, 1, half:].astype(bf16)).astype(f32)
    upper = total[0, :, :half] + got_x
    lower = total[:, 0, half:] + got_y
    upper = upper[0] + flip_y(upper[1].astype(bf16)).astype(f32)
    lower = lower[0] + flip_x(lower[1].astype(bf16)).astype(f32)
    return jnp.concatenate([upper, lower], axis=0)


def sum_all(field):
    total = flip_core(field) + field
    total = flip_y(total) + total
    total = flip_x(total) + total
    count, step = lax.axis_size("dp"), 1
    if count & (count - 1):
        return lax.psum(total, "dp")
    while step < count:
        total = lax.ppermute(total, "dp", [(i, i ^ step) for i in range(count)]) + total
        step *= 2
    return total


def lane_mask(rows, upper):
    lane = lax.broadcasted_iota(jnp.int32, (rows, LANES), 1)
    return lane >= HEAD_DIM if upper else lane < HEAD_DIM


def swap_halves(field):
    lane = lax.broadcasted_iota(jnp.int32, field.shape, 1)
    return jnp.where(
        lane % HEAD_DIM < HEAD_DIM // 2,
        pltpu.roll(field, LANES - HEAD_DIM // 2, 1),
        pltpu.roll(field, HEAD_DIM // 2, 1),
    )


def two_heads(block):
    zero = jnp.zeros_like(block)
    return jnp.concatenate(
        [
            jnp.where(lane_mask(block.shape[0], False), block, zero),
            jnp.where(lane_mask(block.shape[0], True), block, zero),
        ],
        axis=0,
    )


def forward_kernel(
    info, qkv_ref, cos_ref, sin_ref, bias_ref, rot_ref, mixed_ref, lse_ref, s_ref, e_ref, vt_ref, o_ref
):
    slot = qkv_ref.shape[0]
    rows = slot // 8
    tiles = slot // TILE
    for n in range(8):
        here = pl.ds(n * rows, rows)
        there = pl.ds(pl.multiple_of(info[n] * rows, 16), rows)
        cosine, sine = cos_ref[here, :], sin_ref[here, :]
        for g in (0, 1, 2, 3, 6):
            lanes = pl.ds(g * LANES, LANES)
            field = qkv_ref[there, lanes]
            field = field * cosine + swap_halves(field) * sine
            if g < 2:
                field = field * (HEAD_DIM**-0.5)
            if g == 6:
                field = jnp.where(lane_mask(rows, False), field * (HEAD_DIM**-0.5), field)
            rot_ref[here, lanes] = field.astype(bf16)
        for g in (4, 5):
            lanes = pl.ds(g * LANES, LANES)
            rot_ref[here, lanes] = qkv_ref[there, lanes].astype(bf16)
        lanes = pl.ds(7 * LANES, LANES)
        field = qkv_ref[there, lanes]
        rot_ref[here, lanes] = jnp.where(lane_mask(rows, False), field, 0.0).astype(bf16)

    def softmax_block(count, width, keys, queries, biases):
        top = jnp.full((8, width), masked_value, f32)
        for t in range(count):
            scores = dot(keys(t), queries, NT) + biases(t)
            s_ref[pl.ds(t * TILE, TILE), pl.ds(0, width)] = scores
            top = jnp.maximum(top, jnp.max(scores.reshape(TILE // 8, 8, width), axis=0))
        top = jnp.max(top, axis=0, keepdims=True)
        total = jnp.zeros((8, width), f32)
        for t in range(count):
            weights = jnp.exp(s_ref[pl.ds(t * TILE, TILE), pl.ds(0, width)] - top)
            total = total + jnp.sum(weights.reshape(TILE // 8, 8, width), axis=0)
            e_ref[pl.ds(t * TILE, TILE), pl.ds(0, width)] = weights.astype(bf16)
        total = jnp.sum(total, axis=0, keepdims=True)
        depth = count * TILE
        product = dot(vt_ref[:, pl.ds(0, depth)], e_ref[pl.ds(0, depth), pl.ds(0, width)])
        return product / total, top + jnp.log(total)

    def pair(g, carry):
        q_lanes = pl.ds(pl.multiple_of(g * LANES, LANES), LANES)
        k_lanes = pl.ds(pl.multiple_of((PAIRS + g) * LANES, LANES), LANES)
        v_lanes = pl.ds(pl.multiple_of((2 * PAIRS + g) * LANES, LANES), LANES)
        o_lanes = pl.ds(pl.multiple_of((1 + g) * LANES, LANES), LANES)
        vt_ref[...] = rot_ref[:, v_lanes].T
        for i in range(tiles):
            cols = pl.ds(i * TILE, TILE)

            def biases(t):
                bias = bias_ref[pl.ds(t * TILE, TILE), cols]
                return jnp.concatenate([bias, bias], axis=1)

            product, log_total = softmax_block(
                i + 1,
                2 * TILE,
                lambda t: rot_ref[pl.ds(t * TILE, TILE), k_lanes],
                two_heads(rot_ref[cols, q_lanes]),
                biases,
            )
            lse_ref[g, :, pl.ds(i * 2 * TILE, 2 * TILE)] = jnp.broadcast_to(log_total, (8, 2 * TILE))
            out = jnp.concatenate([product[:HEAD_DIM, :TILE], product[HEAD_DIM:, TILE:]], axis=0)
            o_ref[cols, o_lanes] = out.T.astype(bf16)
        return carry

    lax.fori_loop(0, PAIRS, pair, 0)
    o_ref[:, pl.ds(0, LANES)] = jnp.zeros((slot, LANES), bf16)
    vt_ref[...] = rot_ref[:, pl.ds(7 * LANES, LANES)].T
    for j in range((tiles + 1) // 2):
        which = 2 * j + info[8]

        @pl.when(which < tiles)
        def _():
            cols = pl.ds(pl.multiple_of(which * TILE, TILE), TILE)
            queries = pltpu.roll(rot_ref[cols, pl.ds(6 * LANES, LANES)].astype(f32), HEAD_DIM, 1)
            queries = jnp.where(lane_mask(TILE, True), queries, 0.0).astype(bf16)
            product, log_total = softmax_block(
                min(2 * j + 2, tiles),
                TILE,
                lambda t: rot_ref[pl.ds(t * TILE, TILE), pl.ds(6 * LANES, LANES)],
                queries,
                lambda t: bias_ref[pl.ds(t * TILE, TILE), cols],
            )
            lse_ref[PAIRS, :, pl.ds(j * TILE, TILE)] = jnp.broadcast_to(log_total, (8, TILE))
            out = jnp.concatenate([jnp.zeros((HEAD_DIM, TILE), f32), product[:HEAD_DIM]], axis=0)
            o_ref[cols, pl.ds(0, LANES)] = out.T.astype(bf16)

    for n in range(8):
        there = pl.ds(pl.multiple_of(info[n] * rows, 16), rows)
        mixed_ref[there, :] = o_ref[pl.ds(n * rows, rows), :]


def backward_kernel(
    info, rot_ref, cos_ref, sin_ref, bias_ref, mixed_ref, dmix_ref, lse_ref, out_ref,
    d_ref, p_ref, ds_ref, kt_ref, dk_ref, dv_ref, dq_ref,
):
    slot = rot_ref.shape[0]
    rows = slot // 8
    tiles = slot // TILE
    for n in range(8):
        here = pl.ds(n * rows, rows)
        there = pl.ds(pl.multiple_of(info[n] * rows, 16), rows)
        d_rows = dmix_ref[there, :]
        d_ref[here, :] = d_rows
        p_ref[here, :] = d_rows.astype(f32) * mixed_ref[there, :].astype(f32)

    def row_sums(cols, lanes, upper):
        product = p_ref[cols, lanes]
        high = product.astype(bf16)
        low = (product - high.astype(f32)).astype(bf16)
        ones = jnp.where(lane_mask(8, upper), 1.0, 0.0).astype(bf16)
        return dot(ones, high, NT) + dot(ones, low, NT)

    def score_block(count, width, keys, values, queries, d_rows, biases, lse, centre):
        for t in range(count):
            here = pl.ds(t * TILE, TILE)
            probs = jnp.exp(dot(keys(t), queries, NT) + biases(t) - lse)
            d_probs = dot(values(t), d_rows, NT)
            d_scores = (probs * (d_probs - centre)).astype(bf16)
            ds_ref[here, pl.ds(0, width)] = d_scores
            dk_ref[here, :] += dot(d_scores, queries)
            dv_ref[here, :] += dot(probs.astype(bf16), d_rows)
        depth = count * TILE
        return dot(kt_ref[:, pl.ds(0, depth)], ds_ref[pl.ds(0, depth), pl.ds(0, width)]) * (HEAD_DIM**-0.5)

    def place(field_of, lanes, turned):
        for n in range(8):
            here = pl.ds(n * rows, rows)
            there = pl.ds(pl.multiple_of(info[n] * rows, 16), rows)
            field = field_of(here)
            if turned:
                field = field * cos_ref[here, :] - swap_halves(field) * sin_ref[here, :]
            out_ref[there, lanes] = field.astype(bf16)

    def pair(g, carry):
        q_lanes = pl.ds(pl.multiple_of(g * LANES, LANES), LANES)
        k_lanes = pl.ds(pl.multiple_of((PAIRS + g) * LANES, LANES), LANES)
        v_lanes = pl.ds(pl.multiple_of((2 * PAIRS + g) * LANES, LANES), LANES)
        o_lanes = pl.ds(pl.multiple_of((1 + g) * LANES, LANES), LANES)
        kt_ref[...] = rot_ref[:, k_lanes].T
        dk_ref[...] = jnp.zeros_like(dk_ref)
        dv_ref[...] = jnp.zeros_like(dv_ref)
        for i in range(tiles):
            cols = pl.ds(i * TILE, TILE)

            def biases(t):
                bias = bias_ref[pl.ds(t * TILE, TILE), cols]
                return jnp.concatenate([bias, bias], axis=1)

            centre = jnp.concatenate([row_sums(cols, o_lanes, False), row_sums(cols, o_lanes, True)], axis=1)
            d_query = score_block(
                i + 1,
                2 * TILE,
                lambda t: rot_ref[pl.ds(t * TILE, TILE), k_lanes],
                lambda t: rot_ref[pl.ds(t * TILE, TILE), v_lanes],
                two_heads(rot_ref[cols, q_lanes]),
                two_heads(d_ref[cols, o_lanes]),
                biases,
                lse_ref[g, pl.ds(0, 1), pl.ds(i * 2 * TILE, 2 * TILE)],
                centre[0:1],
            )
            out = jnp.concatenate([d_query[:HEAD_DIM, :TILE], d_query[HEAD_DIM:, TILE:]], axis=0)
            dq_ref[cols, :] = out.T
        place(lambda here: dq_ref[here, :], q_lanes, True)
        place(lambda here: dk_ref[here, :], k_lanes, True)
        place(lambda here: dv_ref[here, :], v_lanes, False)
        return carry

    lax.fori_loop(0, PAIRS, pair, 0)
    k_lanes, v_lanes = pl.ds(6 * LANES, LANES), pl.ds(7 * LANES, LANES)
    kt_ref[...] = rot_ref[:, k_lanes].T
    dk_ref[...] = jnp.zeros_like(dk_ref)
    dv_ref[...] = jnp.zeros_like(dv_ref)
    dq_ref[...] = jnp.zeros_like(dq_ref)
    for j in range((tiles + 1) // 2):
        which = 2 * j + info[8]

        @pl.when(which < tiles)
        def _():
            cols = pl.ds(pl.multiple_of(which * TILE, TILE), TILE)
            queries = pltpu.roll(rot_ref[cols, k_lanes].astype(f32), HEAD_DIM, 1)
            queries = jnp.where(lane_mask(TILE, True), queries, 0.0).astype(bf16)
            d_rows = pltpu.roll(d_ref[cols, pl.ds(0, LANES)].astype(f32), HEAD_DIM, 1)
            d_rows = jnp.where(lane_mask(TILE, False), d_rows, 0.0).astype(bf16)
            d_query = score_block(
                min(2 * j + 2, tiles),
                TILE,
                lambda t: rot_ref[pl.ds(t * TILE, TILE), k_lanes],
                lambda t: rot_ref[pl.ds(t * TILE, TILE), v_lanes],
                queries,
                d_rows,
                lambda t: bias_ref[pl.ds(t * TILE, TILE), cols],
                lse_ref[PAIRS, pl.ds(0, 1), pl.ds(j * TILE, TILE)],
                row_sums(cols, pl.ds(0, LANES), True)[0:1],
            )
            out = jnp.concatenate([d_query[HEAD_DIM:], jnp.zeros((HEAD_DIM, TILE), f32)], axis=0)
            dq_ref[cols, :] = out.T

    place(lambda here: dq_ref[here, :] + dk_ref[here, :], k_lanes, True)
    place(lambda here: dv_ref[here, :], v_lanes, False)


SMEM_SPEC = pl.BlockSpec(memory_space=pltpu.SMEM)
VMEM_SPEC = pl.BlockSpec(memory_space=pltpu.VMEM)


def attention_forward(info, qkv, cosine, sine, bias):
    slot = qkv.shape[0]
    pieces = slot // TILE
    return pl.pallas_call(
        forward_kernel,
        out_shape=(
            jax.ShapeDtypeStruct((slot, 8 * LANES), bf16),
            jax.ShapeDtypeStruct((slot, 3 * LANES), bf16),
            jax.ShapeDtypeStruct((PAIRS + 1, 8, pieces * 2 * TILE), f32),
        ),
        in_specs=[SMEM_SPEC] + [VMEM_SPEC] * 4,
        out_specs=(VMEM_SPEC,) * 3,
        scratch_shapes=[
            pltpu.VMEM((slot, 2 * TILE), f32),
            pltpu.VMEM((slot, 2 * TILE), bf16),
            pltpu.VMEM((LANES, slot), bf16),
            pltpu.VMEM((slot, 3 * LANES), bf16),
        ],
        compiler_params=pltpu.CompilerParams(vmem_limit_bytes=48 << 20),
        cost_estimate=pl.CostEstimate(
            flops=20 * slot * slot * 128, bytes_accessed=24 << 20, transcendentals=3 * slot * slot
        ),
        name="attention_forward",
    )(info, qkv, cosine, sine, bias)


def attention_backward(info, rotated, cosine, sine, bias, mixed, d_mixed, log_total):
    slot = rotated.shape[0]
    return pl.pallas_call(
        backward_kernel,
        out_shape=jax.ShapeDtypeStruct((slot, 8 * LANES), bf16),
        in_specs=[SMEM_SPEC] + [VMEM_SPEC] * 7,
        out_specs=VMEM_SPEC,
        scratch_shapes=[
            pltpu.VMEM((slot, 3 * LANES), bf16),
            pltpu.VMEM((slot, 3 * LANES), f32),
            pltpu.VMEM((slot, 2 * TILE), bf16),
            pltpu.VMEM((LANES, slot), bf16),
            pltpu.VMEM((slot, LANES), f32),
            pltpu.VMEM((slot, LANES), f32),
            pltpu.VMEM((slot, LANES), f32),
        ],
        compiler_params=pltpu.CompilerParams(vmem_limit_bytes=48 << 20),
        cost_estimate=pl.CostEstimate(
            flops=50 * slot * slot * 128, bytes_accessed=24 << 20, transcendentals=3 * slot * slot
        ),
        name="attention_backward",
    )(info, rotated, cosine, sine, bias, mixed, d_mixed, log_total)


def shards(
    tokens,
    w_query,
    w_key,
    w_value,
    w_out,
    gain_attn,
    w_gate,
    w_up,
    w_down,
    gain_mlp,
    cotangent,
    lineage,
    padding,
    positions,
):
    slot = lineage.shape[1]
    on_x, on_mp = lax.axis_index("ctx"), lax.axis_index("mp")
    on_y, on_core = on_mp // 2, on_mp % 2
    lower_x = on_x == 0
    heads = w_query.shape[1] // HEAD_DIM
    own_cols = heads // 2 * HEAD_DIM
    ff_half = w_gate.shape[1] // 2
    ff_pad = -(-ff_half // LANES) * LANES

    info = []
    for n in range(8):
        d_x, d_y, d_core = on_x ^ (n // 4), on_y ^ (n // 2 % 2), on_core ^ (n % 2)
        info.append(d_core * 4 + d_x * 2 + d_y)
    info = jnp.stack(info + [on_x] + [jnp.zeros_like(on_x)] * 7).astype(jnp.int32)

    gain_a = gain_attn.astype(f32)
    gain_m = gain_mlp.astype(f32)
    inputs = tokens.astype(f32)
    grad_rows = cotangent.astype(f32)

    def both_x(mine, theirs):
        got = flip_x(theirs)
        return jnp.where(lower_x, jnp.concatenate([mine, got], 0), jnp.concatenate([got, mine], 0))

    out_t = w_out.T
    a_cols = [w[:, :own_cols] for w in (w_query, w_key, w_value, out_t)]
    b_cols = [w[:, own_cols : 2 * own_cols] for w in (w_query, w_key, w_value, out_t)]
    s_cols = [w[:, 2 * own_cols :] for w in (w_query, w_key, w_value, out_t)]

    def pack(cols):
        return jnp.concatenate(cols[:3] + s_cols + cols[3:], axis=1)

    attn_a, attn_b = pack(a_cols), pack(b_cols)
    attn_part = both_x(jnp.where(lower_x, attn_a, attn_b), jnp.where(lower_x, attn_b, attn_a))

    def halves(weight):
        fill = ((0, 0), (0, ff_pad - ff_half))
        first, second = jnp.pad(weight[:, :ff_half], fill), jnp.pad(weight[:, ff_half:], fill)
        return jnp.where(lower_x, first, second), jnp.where(lower_x, second, first)

    gate_mine, gate_theirs = halves(w_gate)
    up_mine, up_theirs = halves(w_up)
    down_mine, down_theirs = halves(w_down.T)
    gu_part = both_x(
        jnp.concatenate([gate_mine, up_mine], 1), jnp.concatenate([gate_theirs, up_theirs], 1)
    )
    down_part = both_x(down_mine, down_theirs)

    attn_w = lax.all_gather(attn_part, "dp", axis=0, tiled=True)
    gu_w = lax.all_gather(gu_part, "dp", axis=0, tiled=True)
    down_w = lax.all_gather(down_part, "dp", axis=0, tiled=True)
    qkv_w = attn_w[:, : 8 * LANES]
    out_w = attn_w[:, 7 * LANES :]

    index = jnp.arange(slot, dtype=jnp.int32)
    own_seg = lineage[0]
    related = (
        (own_seg[:, None] == lineage[0][None, :])
        | (own_seg[:, None] == lineage[1][None, :])
        | (own_seg[:, None] == lineage[2][None, :])
    )
    live = padding == 0
    allowed = (index[:, None] == index[None, :]) | (
        related & live[:, None] & live[None, :] & (index[:, None] < index[None, :])
    )
    bias = jnp.where(allowed, 0.0, masked_value).astype(f32)
    half_dim = HEAD_DIM // 2
    inv_freq = rope_base ** (-2.0 * jnp.arange(half_dim, dtype=f32) / HEAD_DIM)
    angles = positions.astype(f32)[:, None] * inv_freq[None, :]
    cos, sin = jnp.cos(angles), jnp.sin(angles)
    cosine = jnp.concatenate([cos, cos, cos, cos], axis=1)
    sine = jnp.concatenate([-sin, sin, -sin, sin], axis=1)

    normed_a = gather_rows((normalize(inputs) * gain_a).astype(bf16))
    qkv = dot(normed_a, qkv_w)
    rotated, mixed, log_total = attention_forward(info, qkv, cosine, sine, bias)
    residual = inputs + branch_scale * sum_rows(mixed, out_w, NT)
    normed_m = gather_rows((normalize(residual) * gain_m).astype(bf16))
    gate_up = dot(normed_m, gu_w)
    gate, up = gate_up[:, :ff_pad], gate_up[:, ff_pad:]
    sigmoid_gate = jax.nn.sigmoid(gate)
    hidden = (gate * sigmoid_gate * up).astype(bf16)
    output = residual + branch_scale * sum_rows(hidden, down_w, NT)

    d_mlp = gather_rows((branch_scale * grad_rows).astype(bf16))
    grad_down = lax.psum_scatter(
        dot(d_mlp, hidden, TN).astype(bf16), "dp", scatter_dimension=0, tiled=True
    )
    d_hidden = dot(d_mlp, down_w)
    d_gate = (d_hidden * up * sigmoid_gate * (1.0 + gate * (1.0 - sigmoid_gate))).astype(bf16)
    d_up = (d_hidden * (gate * sigmoid_gate)).astype(bf16)
    d_gate_up = jnp.concatenate([d_gate, d_up], axis=1)
    d_normed_mlp = sum_rows(d_gate_up, gu_w, NT)
    grad_gu = lax.psum_scatter(
        dot(normed_m, d_gate_up, TN).astype(bf16), "dp", scatter_dimension=0, tiled=True
    )
    back_mlp, gain_mlp_part = norm_back(residual, gain_m, d_normed_mlp)
    d_residual = grad_rows + back_mlp

    d_attn = gather_rows((branch_scale * d_residual).astype(bf16))
    d_mixed = dot(d_attn, out_w).astype(bf16)
    grad_o = lax.psum_scatter(
        dot(d_attn, mixed, TN).astype(bf16), "dp", scatter_dimension=0, tiled=True
    )
    d_qkv = attention_backward(info, rotated, cosine, sine, bias, mixed, d_mixed, log_total)
    grad_qkv = lax.psum_scatter(
        dot(normed_a, d_qkv, TN).astype(bf16), "dp", scatter_dimension=0, tiled=True
    )
    d_normed_attn = sum_rows(d_qkv, qkv_w, NT)
    back_attn, gain_attn_part = norm_back(inputs, gain_a, d_normed_attn)
    input_grad = d_residual + back_attn
    gains = sum_all(jnp.stack([gain_attn_part, gain_mlp_part]))

    def rows_of_x(field):
        rows = field.shape[0] // 2
        mine = jnp.where(lower_x, field[:rows], field[rows:])
        got = flip_x(jnp.where(lower_x, field[rows:], field[:rows]))
        return mine.astype(f32), got.astype(f32)

    def join(mine, got):
        return jnp.where(lower_x, jnp.concatenate([mine, got], 1), jnp.concatenate([got, mine], 1))

    def join_heads(mine, got, at, shared_at):
        whole = join(mine[:, at : at + own_cols], got[:, at : at + own_cols])
        last = slice(shared_at, shared_at + HEAD_DIM)
        return jnp.concatenate([whole, mine[:, last] + got[:, last]], axis=1)

    mine, got = rows_of_x(grad_gu)
    grad_gate = join(mine[:, :ff_half], got[:, :ff_half])
    grad_up = join(mine[:, ff_pad : ff_pad + ff_half], got[:, ff_pad : ff_pad + ff_half])
    mine, got = rows_of_x(grad_down)
    grad_down = join(mine[:, :ff_half], got[:, :ff_half]).T
    mine, got = rows_of_x(grad_o)
    grad_out = join_heads(mine, got, LANES, HEAD_DIM).T
    mine, got = rows_of_x(grad_qkv)
    grad_query = join_heads(mine, got, 0, 6 * LANES)
    grad_key = join_heads(mine, got, 2 * LANES, 6 * LANES + HEAD_DIM)
    grad_value = join_heads(mine, got, 4 * LANES, 7 * LANES)

    return (
        output.astype(bf16),
        input_grad.astype(bf16),
        grad_query,
        grad_key,
        grad_value,
        grad_out,
        gains[0],
        grad_gate,
        grad_up,
        grad_down,
        gains[1],
    )


def solution(mesh):
    placed = (
        P(("dp", "ctx", "mp"), None),
        P(("dp", "ctx"), "mp"),
        P(("dp", "ctx"), "mp"),
        P(("dp", "ctx"), "mp"),
        P("mp", ("dp", "ctx")),
        P(),
        P(("dp", "ctx"), "mp"),
        P(("dp", "ctx"), "mp"),
        P("mp", ("dp", "ctx")),
        P(),
        P(("dp", "ctx", "mp"), None),
        P(None, "dp"),
        P("dp"),
        P("dp"),
    )
    return jax.shard_map(
        shards,
        mesh=mesh,
        in_specs=placed,
        out_specs=(
            P(("dp", "ctx", "mp"), None),
            P(("dp", "ctx", "mp"), None),
            P(("dp", "ctx"), "mp"),
            P(("dp", "ctx"), "mp"),
            P(("dp", "ctx"), "mp"),
            P("mp", ("dp", "ctx")),
            P(),
            P(("dp", "ctx"), "mp"),
            P(("dp", "ctx"), "mp"),
            P("mp", ("dp", "ctx")),
            P(),
        ),
        check_vma=False,
    )
```

```python
import functools
import math

import jax
import jax.numpy as jnp
from jax import lax
from jax.experimental import pallas as pl
from jax.experimental.pallas import tpu as pltpu
from jax.sharding import PartitionSpec as P

HEAD_DIM = 64
LANES = 128
PAIRS = 2
TILE = 128

eps = 1e-05
branch_scale = 1.4 / math.sqrt(40.0)
rope_base = 10000.0
masked_value = -1e30

f32 = jnp.float32
bf16 = jnp.bfloat16

NN = (((1,), (0,)), ((), ()))
NT = (((1,), (1,)), ((), ()))
TN = (((0,), (0,)), ((), ()))


def dot(left, right, dims=NN):
    return lax.dot_general(left, right, dims, preferred_element_type=f32)


def after(*fields):
    return lax.optimization_barrier(fields)


def normalize(field):
    return field * lax.rsqrt(jnp.mean(field * field, axis=-1, keepdims=True) + eps)


def norm_back(field, gain_f32, incoming):
    inverse = lax.rsqrt(jnp.mean(field * field, axis=-1, keepdims=True) + eps)
    scaled = gain_f32 * incoming
    along = jnp.mean(field * scaled, axis=-1, keepdims=True)
    return (
        inverse * scaled - field * inverse**3 * along,
        jnp.sum(incoming * field * inverse, axis=0),
    )


def flip_x(field):
    return lax.ppermute(field, "ctx", [(0, 1), (1, 0)])


def flip_y(field):
    return lax.ppermute(field, "mp", [(0, 2), (2, 0), (1, 3), (3, 1)])


def flip_core(field):
    return lax.ppermute(field, "mp", [(0, 1), (1, 0), (2, 3), (3, 2)])


def gather_near(own, other=None):
    half = own.shape[0] // 2
    from_x, from_y = flip_x(own), flip_y(own)
    if other is not None:
        from_x, from_y, other = after(from_x, from_y, other)
    corner = jnp.concatenate([flip_y(from_x[:half]), flip_x(from_y[half:])], axis=0)
    near = jnp.concatenate([own, from_y, from_x, corner], axis=0)
    return near if other is None else (near, other)


def gather_rows(own):
    near = gather_near(own)
    return near, flip_core(near)


def sum_rows(left, right, dims, other=None):
    count = left.shape[0] // 2
    block = count // 4
    half = block // 2
    away = flip_core(dot(left[count:], right, dims).astype(bf16))
    total = dot(left[:count], right, dims) + away.astype(f32)
    total = total.reshape(2, 2, block, total.shape[-1])
    got_x = flip_x(total[1, :, :half].astype(bf16)).astype(f32)
    got_y = flip_y(total[:, 1, half:].astype(bf16)).astype(f32)
    upper = total[0, :, :half] + got_x
    lower = total[:, 0, half:] + got_y
    if other is not None:
        upper, other = after(upper, other)
    upper = upper[0] + flip_y(upper[1].astype(bf16)).astype(f32)
    lower = lower[0] + flip_x(lower[1].astype(bf16)).astype(f32)
    total = jnp.concatenate([upper, lower], axis=0)
    return total if other is None else (total, other)


def sum_all(field):
    total = flip_core(field) + field
    total = flip_y(total) + total
    total = flip_x(total) + total
    count, step = lax.axis_size("dp"), 1
    if count & (count - 1):
        return lax.psum(total, "dp")
    while step < count:
        total = lax.ppermute(total, "dp", [(i, i ^ step) for i in range(count)]) + total
        step *= 2
    return total


def lane_mask(rows, upper):
    lane = lax.broadcasted_iota(jnp.int32, (rows, LANES), 1)
    return lane >= HEAD_DIM if upper else lane < HEAD_DIM


def swap_halves(field):
    lane = lax.broadcasted_iota(jnp.int32, field.shape, 1)
    return jnp.where(
        lane % HEAD_DIM < HEAD_DIM // 2,
        pltpu.roll(field, LANES - HEAD_DIM // 2, 1),
        pltpu.roll(field, HEAD_DIM // 2, 1),
    )


def two_heads(block):
    zero = jnp.zeros_like(block)
    return jnp.concatenate(
        [
            jnp.where(lane_mask(block.shape[0], False), block, zero),
            jnp.where(lane_mask(block.shape[0], True), block, zero),
        ],
        axis=0,
    )


def forward_kernel(
    info, qkv_ref, cos_ref, sin_ref, bias_ref, rot_ref, mixed_ref, lse_ref, s_ref, e_ref, vt_ref, o_ref
):
    slot = qkv_ref.shape[0]
    rows = slot // 8
    tiles = slot // TILE
    for n in range(8):
        here = pl.ds(n * rows, rows)
        there = pl.ds(pl.multiple_of(info[n] * rows, 16), rows)
        cosine, sine = cos_ref[here, :], sin_ref[here, :]
        for g in (0, 1, 2, 3, 6):
            lanes = pl.ds(g * LANES, LANES)
            field = qkv_ref[there, lanes]
            field = field * cosine + swap_halves(field) * sine
            if g < 2:
                field = field * (HEAD_DIM**-0.5)
            if g == 6:
                field = jnp.where(lane_mask(rows, False), field * (HEAD_DIM**-0.5), field)
            rot_ref[here, lanes] = field.astype(bf16)
        for g in (4, 5):
            lanes = pl.ds(g * LANES, LANES)
            rot_ref[here, lanes] = qkv_ref[there, lanes].astype(bf16)
        lanes = pl.ds(7 * LANES, LANES)
        field = qkv_ref[there, lanes]
        rot_ref[here, lanes] = jnp.where(lane_mask(rows, False), field, 0.0).astype(bf16)

    def softmax_block(count, width, keys, queries, biases):
        top = jnp.full((8, width), masked_value, f32)
        for t in range(count):
            scores = dot(keys(t), queries, NT) + biases(t)
            s_ref[pl.ds(t * TILE, TILE), pl.ds(0, width)] = scores
            top = jnp.maximum(top, jnp.max(scores.reshape(TILE // 8, 8, width), axis=0))
        top = jnp.max(top, axis=0, keepdims=True)
        total = jnp.zeros((8, width), f32)
        for t in range(count):
            weights = jnp.exp(s_ref[pl.ds(t * TILE, TILE), pl.ds(0, width)] - top)
            total = total + jnp.sum(weights.reshape(TILE // 8, 8, width), axis=0)
            e_ref[pl.ds(t * TILE, TILE), pl.ds(0, width)] = weights.astype(bf16)
        total = jnp.sum(total, axis=0, keepdims=True)
        depth = count * TILE
        product = dot(vt_ref[:, pl.ds(0, depth)], e_ref[pl.ds(0, depth), pl.ds(0, width)])
        return product / total, top + jnp.log(total)

    def pair(g, carry):
        q_lanes = pl.ds(pl.multiple_of(g * LANES, LANES), LANES)
        k_lanes = pl.ds(pl.multiple_of((PAIRS + g) * LANES, LANES), LANES)
        v_lanes = pl.ds(pl.multiple_of((2 * PAIRS + g) * LANES, LANES), LANES)
        o_lanes = pl.ds(pl.multiple_of((1 + g) * LANES, LANES), LANES)
        vt_ref[...] = rot_ref[:, v_lanes].T
        for i in range(tiles):
            cols = pl.ds(i * TILE, TILE)

            def biases(t):
                bias = bias_ref[pl.ds(t * TILE, TILE), cols]
                return jnp.concatenate([bias, bias], axis=1)

            product, log_total = softmax_block(
                i + 1,
                2 * TILE,
                lambda t: rot_ref[pl.ds(t * TILE, TILE), k_lanes],
                two_heads(rot_ref[cols, q_lanes]),
                biases,
            )
            lse_ref[g, :, pl.ds(i * 2 * TILE, 2 * TILE)] = jnp.broadcast_to(log_total, (8, 2 * TILE))
            out = jnp.concatenate([product[:HEAD_DIM, :TILE], product[HEAD_DIM:, TILE:]], axis=0)
            o_ref[cols, o_lanes] = out.T.astype(bf16)
        return carry

    lax.fori_loop(0, PAIRS, pair, 0)
    o_ref[:, pl.ds(0, LANES)] = jnp.zeros((slot, LANES), bf16)
    vt_ref[...] = rot_ref[:, pl.ds(7 * LANES, LANES)].T
    for j in range((tiles + 1) // 2):
        which = 2 * j + info[8]

        @pl.when(which < tiles)
        def _():
            cols = pl.ds(pl.multiple_of(which * TILE, TILE), TILE)
            queries = pltpu.roll(rot_ref[cols, pl.ds(6 * LANES, LANES)].astype(f32), HEAD_DIM, 1)
            queries = jnp.where(lane_mask(TILE, True), queries, 0.0).astype(bf16)
            product, log_total = softmax_block(
                min(2 * j + 2, tiles),
                TILE,
                lambda t: rot_ref[pl.ds(t * TILE, TILE), pl.ds(6 * LANES, LANES)],
                queries,
                lambda t: bias_ref[pl.ds(t * TILE, TILE), cols],
            )
            lse_ref[PAIRS, :, pl.ds(j * TILE, TILE)] = jnp.broadcast_to(log_total, (8, TILE))
            out = jnp.concatenate([jnp.zeros((HEAD_DIM, TILE), f32), product[:HEAD_DIM]], axis=0)
            o_ref[cols, pl.ds(0, LANES)] = out.T.astype(bf16)

    for n in range(8):
        there = pl.ds(pl.multiple_of(info[n] * rows, 16), rows)
        mixed_ref[there, :] = o_ref[pl.ds(n * rows, rows), :]


def backward_kernel(
    info, rot_ref, cos_ref, sin_ref, bias_ref, mixed_ref, near_ref, far_ref, lse_ref, out_ref,
    d_ref, p_ref, ds_ref, kt_ref, dk_ref, dv_ref, dq_ref,
):
    slot = rot_ref.shape[0]
    rows = slot // 8
    tiles = slot // TILE
    for r in range(8):
        here = pl.ds(r * rows, rows)
        there = pl.ds(pl.multiple_of(info[9 + r] * rows, 16), rows)
        d_rows = (near_ref if r < 4 else far_ref)[pl.ds(r % 4 * rows, rows), :]
        d_ref[there, :] = d_rows
        p_ref[there, :] = d_rows.astype(f32) * mixed_ref[here, :].astype(f32)

    def row_sums(cols, lanes, upper):
        product = p_ref[cols, lanes]
        high = product.astype(bf16)
        low = (product - high.astype(f32)).astype(bf16)
        ones = jnp.where(lane_mask(8, upper), 1.0, 0.0).astype(bf16)
        return dot(ones, high, NT) + dot(ones, low, NT)

    def score_block(count, width, keys, values, queries, d_rows, biases, lse, centre):
        for t in range(count):
            here = pl.ds(t * TILE, TILE)
            probs = jnp.exp(dot(keys(t), queries, NT) + biases(t) - lse)
            d_probs = dot(values(t), d_rows, NT)
            d_scores = (probs * (d_probs - centre)).astype(bf16)
            ds_ref[here, pl.ds(0, width)] = d_scores
            dk_ref[here, :] += dot(d_scores, queries)
            dv_ref[here, :] += dot(probs.astype(bf16), d_rows)
        depth = count * TILE
        return dot(kt_ref[:, pl.ds(0, depth)], ds_ref[pl.ds(0, depth), pl.ds(0, width)]) * (HEAD_DIM**-0.5)

    def place(field_of, lanes, turned):
        for n in range(8):
            here = pl.ds(n * rows, rows)
            there = pl.ds(pl.multiple_of(info[n] * rows, 16), rows)
            field = field_of(here)
            if turned:
                field = field * cos_ref[here, :] - swap_halves(field) * sin_ref[here, :]
            out_ref[there, lanes] = field.astype(bf16)

    def pair(g, carry):
        q_lanes = pl.ds(pl.multiple_of(g * LANES, LANES), LANES)
        k_lanes = pl.ds(pl.multiple_of((PAIRS + g) * LANES, LANES), LANES)
        v_lanes = pl.ds(pl.multiple_of((2 * PAIRS + g) * LANES, LANES), LANES)
        o_lanes = pl.ds(pl.multiple_of((1 + g) * LANES, LANES), LANES)
        kt_ref[...] = rot_ref[:, k_lanes].T
        dk_ref[...] = jnp.zeros_like(dk_ref)
        dv_ref[...] = jnp.zeros_like(dv_ref)
        for i in range(tiles):
            cols = pl.ds(i * TILE, TILE)

            def biases(t):
                bias = bias_ref[pl.ds(t * TILE, TILE), cols]
                return jnp.concatenate([bias, bias], axis=1)

            centre = jnp.concatenate([row_sums(cols, o_lanes, False), row_sums(cols, o_lanes, True)], axis=1)
            d_query = score_block(
                i + 1,
                2 * TILE,
                lambda t: rot_ref[pl.ds(t * TILE, TILE), k_lanes],
                lambda t: rot_ref[pl.ds(t * TILE, TILE), v_lanes],
                two_heads(rot_ref[cols, q_lanes]),
                two_heads(d_ref[cols, o_lanes]),
                biases,
                lse_ref[g, pl.ds(0, 1), pl.ds(i * 2 * TILE, 2 * TILE)],
                centre[0:1],
            )
            out = jnp.concatenate([d_query[:HEAD_DIM, :TILE], d_query[HEAD_DIM:, TILE:]], axis=0)
            dq_ref[cols, :] = out.T
        place(lambda here: dq_ref[here, :], q_lanes, True)
        place(lambda here: dk_ref[here, :], k_lanes, True)
        place(lambda here: dv_ref[here, :], v_lanes, False)
        return carry

    lax.fori_loop(0, PAIRS, pair, 0)
    k_lanes, v_lanes = pl.ds(6 * LANES, LANES), pl.ds(7 * LANES, LANES)
    kt_ref[...] = rot_ref[:, k_lanes].T
    dk_ref[...] = jnp.zeros_like(dk_ref)
    dv_ref[...] = jnp.zeros_like(dv_ref)
    dq_ref[...] = jnp.zeros_like(dq_ref)
    for j in range((tiles + 1) // 2):
        which = 2 * j + info[8]

        @pl.when(which < tiles)
        def _():
            cols = pl.ds(pl.multiple_of(which * TILE, TILE), TILE)
            queries = pltpu.roll(rot_ref[cols, k_lanes].astype(f32), HEAD_DIM, 1)
            queries = jnp.where(lane_mask(TILE, True), queries, 0.0).astype(bf16)
            d_rows = pltpu.roll(d_ref[cols, pl.ds(0, LANES)].astype(f32), HEAD_DIM, 1)
            d_rows = jnp.where(lane_mask(TILE, False), d_rows, 0.0).astype(bf16)
            d_query = score_block(
                min(2 * j + 2, tiles),
                TILE,
                lambda t: rot_ref[pl.ds(t * TILE, TILE), k_lanes],
                lambda t: rot_ref[pl.ds(t * TILE, TILE), v_lanes],
                queries,
                d_rows,
                lambda t: bias_ref[pl.ds(t * TILE, TILE), cols],
                lse_ref[PAIRS, pl.ds(0, 1), pl.ds(j * TILE, TILE)],
                row_sums(cols, pl.ds(0, LANES), True)[0:1],
            )
            out = jnp.concatenate([d_query[HEAD_DIM:], jnp.zeros((HEAD_DIM, TILE), f32)], axis=0)
            dq_ref[cols, :] = out.T

    place(lambda here: dq_ref[here, :] + dk_ref[here, :], k_lanes, True)
    place(lambda here: dv_ref[here, :], v_lanes, False)


SMEM_SPEC = pl.BlockSpec(memory_space=pltpu.SMEM)
VMEM_SPEC = pl.BlockSpec(memory_space=pltpu.VMEM)


def attention_forward(info, qkv, cosine, sine, bias):
    slot = qkv.shape[0]
    pieces = slot // TILE
    return pl.pallas_call(
        forward_kernel,
        out_shape=(
            jax.ShapeDtypeStruct((slot, 8 * LANES), bf16),
            jax.ShapeDtypeStruct((slot, 3 * LANES), bf16),
            jax.ShapeDtypeStruct((PAIRS + 1, 8, pieces * 2 * TILE), f32),
        ),
        in_specs=[SMEM_SPEC] + [VMEM_SPEC] * 4,
        out_specs=(VMEM_SPEC,) * 3,
        scratch_shapes=[
            pltpu.VMEM((slot, 2 * TILE), f32),
            pltpu.VMEM((slot, 2 * TILE), bf16),
            pltpu.VMEM((LANES, slot), bf16),
            pltpu.VMEM((slot, 3 * LANES), bf16),
        ],
        compiler_params=pltpu.CompilerParams(vmem_limit_bytes=48 << 20),
        cost_estimate=pl.CostEstimate(flops=0, bytes_accessed=1024, transcendentals=0),
        name="attention_forward",
    )(info, qkv, cosine, sine, bias)


def attention_backward(info, rotated, cosine, sine, bias, mixed, near, far, log_total):
    slot = rotated.shape[0]
    return pl.pallas_call(
        backward_kernel,
        out_shape=jax.ShapeDtypeStruct((slot, 8 * LANES), bf16),
        in_specs=[SMEM_SPEC] + [VMEM_SPEC] * 8,
        out_specs=VMEM_SPEC,
        scratch_shapes=[
            pltpu.VMEM((slot, 3 * LANES), bf16),
            pltpu.VMEM((slot, 3 * LANES), f32),
            pltpu.VMEM((slot, 2 * TILE), bf16),
            pltpu.VMEM((LANES, slot), bf16),
            pltpu.VMEM((slot, LANES), f32),
            pltpu.VMEM((slot, LANES), f32),
            pltpu.VMEM((slot, LANES), f32),
        ],
        compiler_params=pltpu.CompilerParams(vmem_limit_bytes=48 << 20),
        cost_estimate=pl.CostEstimate(flops=0, bytes_accessed=1024, transcendentals=0),
        name="attention_backward",
    )(info, rotated, cosine, sine, bias, mixed, near, far, log_total)


def whole(shape):
    return pl.BlockSpec(shape, lambda i: (0,) * len(shape), pipeline_mode=pl.Buffered(1))


FREE = pl.CostEstimate(flops=0, bytes_accessed=1024, transcendentals=0)
ROOMY = pltpu.CompilerParams(vmem_limit_bytes=52 << 20)


def gate_kernel(rows_ref, w_ref, *refs):
    gate_up_ref, hidden_ref = refs[-2:]
    width = hidden_ref.shape[1]
    gate_up = dot(rows_ref[...], w_ref[...])
    gate_up_ref[...] = gate_up
    gate, up = gate_up[:, :width], gate_up[:, width:]
    hidden_ref[...] = (gate * jax.nn.sigmoid(gate) * up).astype(bf16)


def gate_half(rows, gu_w, width, earlier):
    count, depth = rows.shape
    tile = count // 4
    at = 4 if earlier else 0
    return pl.pallas_call(
        gate_kernel,
        grid=(4,),
        out_shape=(
            jax.ShapeDtypeStruct((2 * count, 2 * width), f32),
            jax.ShapeDtypeStruct((2 * count, width), bf16),
        ),
        in_specs=[pl.BlockSpec((tile, depth), lambda i: (i, 0)), whole((depth, 2 * width))]
        + [pl.BlockSpec(memory_space=pl.ANY)] * len(earlier),
        out_specs=(
            pl.BlockSpec((tile, 2 * width), lambda i: (i + at, 0)),
            pl.BlockSpec((tile, width), lambda i: (i + at, 0)),
        ),
        input_output_aliases={2: 0, 3: 1} if earlier else {},
        compiler_params=ROOMY,
        cost_estimate=FREE,
        name="gate_half",
    )(rows, gu_w, *earlier)


def hidden_back_kernel(rows_ref, w_ref, gate_up_ref, out_ref):
    width = w_ref.shape[1]
    d_hidden = dot(rows_ref[...], w_ref[...])
    gate, up = gate_up_ref[:, :width], gate_up_ref[:, width:]
    sigmoid_gate = jax.nn.sigmoid(gate)
    d_gate = d_hidden * up * sigmoid_gate * (1.0 + gate * (1.0 - sigmoid_gate))
    out_ref[:, :width] = d_gate.astype(bf16)
    out_ref[:, width:] = (d_hidden * (gate * sigmoid_gate)).astype(bf16)


def hidden_back(rows, down_w, gate_up):
    count, depth = rows.shape
    width = gate_up.shape[1] // 2
    tile = count // 8
    return pl.pallas_call(
        hidden_back_kernel,
        grid=(8,),
        out_shape=jax.ShapeDtypeStruct((count, 2 * width), bf16),
        in_specs=[
            pl.BlockSpec((tile, depth), lambda i: (i, 0)),
            whole((depth, width)),
            pl.BlockSpec((tile, 2 * width), lambda i: (i, 0)),
        ],
        out_specs=pl.BlockSpec((tile, 2 * width), lambda i: (i, 0)),
        compiler_params=ROOMY,
        cost_estimate=FREE,
        name="hidden_back",
    )(rows, down_w, gate_up)


def rows_kernel(dims, rows_ref, w_ref, out_ref):
    out_ref[...] = dot(rows_ref[...], w_ref[...], dims).astype(out_ref.dtype)


def project(rows, weight, cols, kind):
    count, depth = rows.shape
    tile = count // 8
    return pl.pallas_call(
        functools.partial(rows_kernel, NN),
        grid=(8,),
        out_shape=jax.ShapeDtypeStruct((count, cols), kind),
        in_specs=[
            pl.BlockSpec((tile, depth), lambda i: (i, 0)),
            pl.BlockSpec((depth, cols), lambda i: (0, 0), pipeline_mode=pl.Buffered(1)),
        ],
        out_specs=pl.BlockSpec((tile, cols), lambda i: (i, 0)),
        compiler_params=ROOMY,
        cost_estimate=FREE,
        name="project",
    )(rows, weight)


def grads_kernel(place, *refs):
    out_ref = refs[-1]
    products = []
    for near_ref, far_ref, right_ref in zip(refs[0:-1:3], refs[1:-1:3], refs[2:-1:3]):
        left = jnp.concatenate([near_ref[...], far_ref[...]], axis=0)
        products.append(dot(left, right_ref[...], TN))
    place(out_ref, *products)


def place_one(out_ref, product):
    out_ref[...] = product.astype(bf16)


def place_heads(out_ref, first, second):
    start = first.shape[1] - LANES
    out_ref[:, :start] = first[:, :start].astype(bf16)
    out_ref[:, start : start + LANES] = (first[:, start:] + second[:, :LANES]).astype(bf16)
    out_ref[:, start + LANES :] = second[:, LANES:].astype(bf16)


def weight_grads(place, cols, *triples):
    depth = triples[0][0].shape[1]
    specs, operands = [], []
    for near, far, right in triples:
        specs += [
            pl.BlockSpec((near.shape[0], 2 * LANES), lambda i: (0, i)),
            pl.BlockSpec((far.shape[0], 2 * LANES), lambda i: (0, i)),
            whole(right.shape),
        ]
        operands += [near, far, right]
    return pl.pallas_call(
        functools.partial(grads_kernel, place),
        grid=(depth // (2 * LANES),),
        out_shape=jax.ShapeDtypeStruct((depth, cols), bf16),
        in_specs=specs,
        out_specs=pl.BlockSpec((2 * LANES, cols), lambda i: (i, 0)),
        compiler_params=ROOMY,
        cost_estimate=FREE,
        name="weight_grads",
    )(*operands)


def shards(
    tokens,
    w_query,
    w_key,
    w_value,
    w_out,
    gain_attn,
    w_gate,
    w_up,
    w_down,
    gain_mlp,
    cotangent,
    lineage,
    padding,
    positions,
):
    slot = lineage.shape[1]
    on_x, on_mp = lax.axis_index("ctx"), lax.axis_index("mp")
    on_y, on_core = on_mp // 2, on_mp % 2
    lower_x = on_x == 0
    heads = w_query.shape[1] // HEAD_DIM
    own_cols = heads // 2 * HEAD_DIM
    ff_half = w_gate.shape[1] // 2
    ff_pad = -(-ff_half // LANES) * LANES

    info, back = [], []
    for n in range(8):
        d_x, d_y, d_core = on_x ^ (n // 4), on_y ^ (n // 2 % 2), on_core ^ (n % 2)
        info.append(d_core * 4 + d_x * 2 + d_y)
        from_x, from_y, from_core = on_x ^ (n // 2 % 2), on_y ^ (n % 2), on_core ^ (n // 4)
        back.append(from_x * 4 + from_y * 2 + from_core)
    info = jnp.stack(info + [on_x] + back).astype(jnp.int32)

    gain_a = gain_attn.astype(f32)
    gain_m = gain_mlp.astype(f32)
    inputs = tokens.astype(f32)
    grad_rows = cotangent.astype(f32)

    def both_x(mine, theirs):
        got = flip_x(theirs)
        return jnp.where(lower_x, jnp.concatenate([mine, got], 0), jnp.concatenate([got, mine], 0))

    out_t = w_out.T
    a_cols = [w[:, :own_cols] for w in (w_query, w_key, w_value, out_t)]
    b_cols = [w[:, own_cols : 2 * own_cols] for w in (w_query, w_key, w_value, out_t)]
    s_cols = [w[:, 2 * own_cols :] for w in (w_query, w_key, w_value, out_t)]

    def pack(cols):
        return jnp.concatenate(cols[:3] + s_cols + cols[3:], axis=1)

    attn_a, attn_b = pack(a_cols), pack(b_cols)
    attn_part = both_x(jnp.where(lower_x, attn_a, attn_b), jnp.where(lower_x, attn_b, attn_a))

    def halves(weight):
        fill = ((0, 0), (0, ff_pad - ff_half))
        first, second = jnp.pad(weight[:, :ff_half], fill), jnp.pad(weight[:, ff_half:], fill)
        return jnp.where(lower_x, first, second), jnp.where(lower_x, second, first)

    index = jnp.arange(slot, dtype=jnp.int32)
    own_seg = lineage[0]
    related = (
        (own_seg[:, None] == lineage[0][None, :])
        | (own_seg[:, None] == lineage[1][None, :])
        | (own_seg[:, None] == lineage[2][None, :])
    )
    live = padding == 0
    allowed = (index[:, None] == index[None, :]) | (
        related & live[:, None] & live[None, :] & (index[:, None] < index[None, :])
    )
    bias = jnp.where(allowed, 0.0, masked_value).astype(f32)
    half_dim = HEAD_DIM // 2
    inv_freq = rope_base ** (-2.0 * jnp.arange(half_dim, dtype=f32) / HEAD_DIM)
    angles = positions.astype(f32)[:, None] * inv_freq[None, :]
    cos, sin = jnp.cos(angles), jnp.sin(angles)
    cosine = jnp.concatenate([cos, cos, cos, cos], axis=1)
    sine = jnp.concatenate([-sin, sin, -sin, sin], axis=1)

    attn_part, own_rows, grad_rows = after(attn_part, normalize(inputs) * gain_a, grad_rows)
    near_a = gather_near(own_rows.astype(bf16))
    near_a, w_gate, w_up, w_down, grad_rows = after(near_a, w_gate, w_up, w_down, grad_rows)
    far_a = flip_core(near_a)
    near_d, far_d = gather_rows((branch_scale * grad_rows).astype(bf16))
    gate_mine, gate_theirs = halves(w_gate)
    up_mine, up_theirs = halves(w_up)
    down_mine, down_theirs = halves(w_down.T)
    gu_part = both_x(
        jnp.concatenate([gate_mine, up_mine], 1), jnp.concatenate([gate_theirs, up_theirs], 1)
    )
    down_part = both_x(down_mine, down_theirs)
    normed_a = jnp.concatenate([near_a, far_a], axis=0)
    d_mlp = jnp.concatenate([near_d, far_d], axis=0)
    attn_w = lax.all_gather(attn_part, "dp", axis=0, tiled=True)
    attn_w, normed_a, gu_part, down_part, d_mlp, bias, cosine, sine = after(
        attn_w, normed_a, gu_part, down_part, d_mlp, bias, cosine, sine
    )
    gu_w = lax.all_gather(gu_part, "dp", axis=0, tiled=True)
    down_w = lax.all_gather(down_part, "dp", axis=0, tiled=True)
    qkv_w = attn_w[:, : 8 * LANES]
    out_w = attn_w[:, 7 * LANES :]
    qkv = project(normed_a, attn_w, 8 * LANES, f32)
    rotated, mixed, log_total = attention_forward(info, qkv, cosine, sine, bias)
    mixed_rows, gu_w = sum_rows(mixed, out_w, NT, gu_w)
    residual = inputs + branch_scale * mixed_rows
    near_m = gather_near((normalize(residual) * gain_m).astype(bf16))
    far_m = flip_core(near_m)
    gate_up, hidden = gate_half(far_m, gu_w, ff_pad, gate_half(near_m, gu_w, ff_pad, ()))

    grad_down = weight_grads(place_one, ff_pad, (near_d, far_d, hidden))
    gate_up, grad_down = after(gate_up, grad_down)
    grad_down = lax.psum_scatter(grad_down, "dp", scatter_dimension=0, tiled=True)
    d_gate_up = hidden_back(d_mlp, down_w, gate_up)
    grad_gu = weight_grads(place_one, 2 * ff_pad, (near_m, far_m, d_gate_up))
    d_gate_up, grad_gu = after(d_gate_up, grad_gu)
    grad_gu = lax.psum_scatter(grad_gu, "dp", scatter_dimension=0, tiled=True)
    d_normed_mlp, grad_down = sum_rows(d_gate_up, gu_w, NT, grad_down)
    back_mlp, gain_mlp_part = norm_back(residual, gain_m, d_normed_mlp)
    d_residual = grad_rows + back_mlp

    near_o, far_o = gather_rows((branch_scale * d_residual).astype(bf16))
    d_mixed_near, d_mixed_far = dot(near_o, out_w).astype(bf16), dot(far_o, out_w).astype(bf16)
    d_qkv = attention_backward(
        info, rotated, cosine, sine, bias, mixed, d_mixed_near, d_mixed_far, log_total
    )
    grad_attn = weight_grads(
        place_heads, 10 * LANES, (near_a, far_a, d_qkv), (near_o, far_o, mixed)
    )
    grad_attn, grad_gu, d_qkv, hidden = after(grad_attn, grad_gu, d_qkv, hidden)
    grad_attn = lax.psum_scatter(grad_attn, "dp", scatter_dimension=0, tiled=True)
    d_normed_attn = sum_rows(d_qkv, qkv_w, NT)
    back_attn, gain_attn_part = norm_back(inputs, gain_a, d_normed_attn)
    input_grad = d_residual + back_attn
    gains = sum_all(jnp.stack([gain_attn_part, gain_mlp_part]))
    output = residual + branch_scale * sum_rows(hidden, down_w, NT)

    def rows_of_x(field):
        rows = field.shape[0] // 2
        mine = jnp.where(lower_x, field[:rows], field[rows:])
        got = flip_x(jnp.where(lower_x, field[rows:], field[:rows]))
        return mine.astype(f32), got.astype(f32)

    def join(mine, got):
        return jnp.where(lower_x, jnp.concatenate([mine, got], 1), jnp.concatenate([got, mine], 1))

    def join_heads(mine, got, at, shared_at):
        whole = join(mine[:, at : at + own_cols], got[:, at : at + own_cols])
        last = slice(shared_at, shared_at + HEAD_DIM)
        return jnp.concatenate([whole, mine[:, last] + got[:, last]], axis=1)

    mine, got = rows_of_x(grad_gu)
    grad_gate = join(mine[:, :ff_half], got[:, :ff_half])
    grad_up = join(mine[:, ff_pad : ff_pad + ff_half], got[:, ff_pad : ff_pad + ff_half])
    mine, got = rows_of_x(grad_down)
    grad_down = join(mine[:, :ff_half], got[:, :ff_half]).T
    mine, got = rows_of_x(grad_attn)
    grad_query = join_heads(mine, got, 0, 6 * LANES)
    grad_key = join_heads(mine, got, 2 * LANES, 6 * LANES + HEAD_DIM)
    grad_value = join_heads(mine, got, 4 * LANES, 7 * LANES)
    grad_out = join_heads(mine, got, 8 * LANES, 7 * LANES + HEAD_DIM).T

    return (
        output.astype(bf16),
        input_grad.astype(bf16),
        grad_query,
        grad_key,
        grad_value,
        grad_out,
        gains[0],
        grad_gate,
        grad_up,
        grad_down,
        gains[1],
    )


def solution(mesh):
    placed = (
        P(("dp", "ctx", "mp"), None),
        P(("dp", "ctx"), "mp"),
        P(("dp", "ctx"), "mp"),
        P(("dp", "ctx"), "mp"),
        P("mp", ("dp", "ctx")),
        P(),
        P(("dp", "ctx"), "mp"),
        P(("dp", "ctx"), "mp"),
        P("mp", ("dp", "ctx")),
        P(),
        P(("dp", "ctx", "mp"), None),
        P(None, "dp"),
        P("dp"),
        P("dp"),
    )
    return jax.shard_map(
        shards,
        mesh=mesh,
        in_specs=placed,
        out_specs=(
            P(("dp", "ctx", "mp"), None),
            P(("dp", "ctx", "mp"), None),
            P(("dp", "ctx"), "mp"),
            P(("dp", "ctx"), "mp"),
            P(("dp", "ctx"), "mp"),
            P("mp", ("dp", "ctx")),
            P(),
            P(("dp", "ctx"), "mp"),
            P(("dp", "ctx"), "mp"),
            P("mp", ("dp", "ctx")),
            P(),
        ),
        check_vma=False,
    )
```

```python
import functools
import math

import jax
import jax.numpy as jnp
from jax import lax
from jax.experimental import pallas as pl
from jax.experimental.pallas import tpu as pltpu
from jax.sharding import PartitionSpec as P

HEAD_DIM = 64
LANES = 128
PAIRS = 2
TILE = 128

eps = 1e-05
branch_scale = 1.4 / math.sqrt(40.0)
rope_base = 10000.0
masked_value = -1e30

f32 = jnp.float32
bf16 = jnp.bfloat16

NN = (((1,), (0,)), ((), ()))
NT = (((1,), (1,)), ((), ()))
TN = (((0,), (0,)), ((), ()))


def dot(left, right, dims=NN):
    return lax.dot_general(left, right, dims, preferred_element_type=f32)


def after(*fields):
    return lax.optimization_barrier(fields)


def normalize(field):
    return field * lax.rsqrt(jnp.mean(field * field, axis=-1, keepdims=True) + eps)


def norm_back(field, gain_f32, incoming):
    inverse = lax.rsqrt(jnp.mean(field * field, axis=-1, keepdims=True) + eps)
    scaled = gain_f32 * incoming
    along = jnp.mean(field * scaled, axis=-1, keepdims=True)
    return (
        inverse * scaled - field * inverse**3 * along,
        jnp.sum(incoming * field * inverse, axis=0),
    )


def flip_x(field):
    return lax.ppermute(field, "ctx", [(0, 1), (1, 0)])


def flip_y(field):
    return lax.ppermute(field, "mp", [(0, 2), (2, 0), (1, 3), (3, 1)])


def flip_core(field, pieces=1):
    if pieces > 1:
        size = field.shape[0] // pieces
        parts = [flip_core(field[i * size : (i + 1) * size]) for i in range(pieces)]
        return jnp.concatenate(parts, axis=0)
    return lax.ppermute(field, "mp", [(0, 1), (1, 0), (2, 3), (3, 2)])


def gather_near(own, other=None):
    half = own.shape[0] // 2
    from_x, from_y = flip_x(own), flip_y(own)
    if other is not None:
        from_x, from_y, other = after(from_x, from_y, other)
    corner = jnp.concatenate([flip_y(from_x[:half]), flip_x(from_y[half:])], axis=0)
    near = jnp.concatenate([own, from_y, from_x, corner], axis=0)
    return near if other is None else (near, other)


def gather_rows(own):
    near = gather_near(own)
    return near, flip_core(near)


def sum_rows(left, right, dims, other=None, pieces=1):
    count = left.shape[0] // 2
    block = count // 4
    half = block // 2
    away = flip_core(dot(left[count:], right, dims).astype(bf16), pieces)
    total = dot(left[:count], right, dims) + away.astype(f32)
    total = total.reshape(2, 2, block, total.shape[-1])
    got_x = flip_x(total[1, :, :half].astype(bf16)).astype(f32)
    got_y = flip_y(total[:, 1, half:].astype(bf16)).astype(f32)
    upper = total[0, :, :half] + got_x
    lower = total[:, 0, half:] + got_y
    if other is not None:
        upper, other = after(upper, other)
    upper = upper[0] + flip_y(upper[1].astype(bf16)).astype(f32)
    lower = lower[0] + flip_x(lower[1].astype(bf16)).astype(f32)
    total = jnp.concatenate([upper, lower], axis=0)
    return total if other is None else (total, other)


def sum_all(field):
    total = flip_core(field) + field
    total = flip_y(total) + total
    total = flip_x(total) + total
    count, step = lax.axis_size("dp"), 1
    if count & (count - 1):
        return lax.psum(total, "dp")
    while step < count:
        total = lax.ppermute(total, "dp", [(i, i ^ step) for i in range(count)]) + total
        step *= 2
    return total


def lane_mask(rows, upper):
    lane = lax.broadcasted_iota(jnp.int32, (rows, LANES), 1)
    return lane >= HEAD_DIM if upper else lane < HEAD_DIM


def swap_halves(field):
    lane = lax.broadcasted_iota(jnp.int32, field.shape, 1)
    return jnp.where(
        lane % HEAD_DIM < HEAD_DIM // 2,
        pltpu.roll(field, LANES - HEAD_DIM // 2, 1),
        pltpu.roll(field, HEAD_DIM // 2, 1),
    )


def two_heads(block):
    zero = jnp.zeros_like(block)
    return jnp.concatenate(
        [
            jnp.where(lane_mask(block.shape[0], False), block, zero),
            jnp.where(lane_mask(block.shape[0], True), block, zero),
        ],
        axis=0,
    )


def forward_kernel(
    info, qkv_ref, cos_ref, sin_ref, bias_ref, rot_ref, mixed_ref, lse_ref, s_ref, e_ref, vt_ref, o_ref
):
    slot = qkv_ref.shape[0]
    rows = slot // 8
    tiles = slot // TILE
    for n in range(8):
        here = pl.ds(n * rows, rows)
        there = pl.ds(pl.multiple_of(info[n] * rows, 16), rows)
        cosine, sine = cos_ref[here, :], sin_ref[here, :]
        for g in (0, 1, 2, 3, 6):
            lanes = pl.ds(g * LANES, LANES)
            field = qkv_ref[there, lanes]
            field = field * cosine + swap_halves(field) * sine
            if g < 2:
                field = field * (HEAD_DIM**-0.5)
            if g == 6:
                field = jnp.where(lane_mask(rows, False), field * (HEAD_DIM**-0.5), field)
            rot_ref[here, lanes] = field.astype(bf16)
        for g in (4, 5):
            lanes = pl.ds(g * LANES, LANES)
            rot_ref[here, lanes] = qkv_ref[there, lanes].astype(bf16)
        lanes = pl.ds(7 * LANES, LANES)
        field = qkv_ref[there, lanes]
        rot_ref[here, lanes] = jnp.where(lane_mask(rows, False), field, 0.0).astype(bf16)

    def softmax_block(count, width, keys, queries, biases):
        top = jnp.full((8, width), masked_value, f32)
        for t in range(count):
            scores = dot(keys(t), queries, NT) + biases(t)
            s_ref[pl.ds(t * TILE, TILE), pl.ds(0, width)] = scores
            top = jnp.maximum(top, jnp.max(scores.reshape(TILE // 8, 8, width), axis=0))
        top = jnp.max(top, axis=0, keepdims=True)
        total = jnp.zeros((8, width), f32)
        for t in range(count):
            weights = jnp.exp(s_ref[pl.ds(t * TILE, TILE), pl.ds(0, width)] - top)
            total = total + jnp.sum(weights.reshape(TILE // 8, 8, width), axis=0)
            e_ref[pl.ds(t * TILE, TILE), pl.ds(0, width)] = weights.astype(bf16)
        total = jnp.sum(total, axis=0, keepdims=True)
        depth = count * TILE
        product = dot(vt_ref[:, pl.ds(0, depth)], e_ref[pl.ds(0, depth), pl.ds(0, width)])
        return product / total, top + jnp.log(total)

    def pair(g, carry):
        q_lanes = pl.ds(pl.multiple_of(g * LANES, LANES), LANES)
        k_lanes = pl.ds(pl.multiple_of((PAIRS + g) * LANES, LANES), LANES)
        v_lanes = pl.ds(pl.multiple_of((2 * PAIRS + g) * LANES, LANES), LANES)
        o_lanes = pl.ds(pl.multiple_of((1 + g) * LANES, LANES), LANES)
        vt_ref[...] = rot_ref[:, v_lanes].T
        for i in range(tiles):
            cols = pl.ds(i * TILE, TILE)

            def biases(t):
                bias = bias_ref[pl.ds(t * TILE, TILE), cols]
                return jnp.concatenate([bias, bias], axis=1)

            product, log_total = softmax_block(
                i + 1,
                2 * TILE,
                lambda t: rot_ref[pl.ds(t * TILE, TILE), k_lanes],
                two_heads(rot_ref[cols, q_lanes]),
                biases,
            )
            lse_ref[g, :, pl.ds(i * 2 * TILE, 2 * TILE)] = jnp.broadcast_to(log_total, (8, 2 * TILE))
            out = jnp.concatenate([product[:HEAD_DIM, :TILE], product[HEAD_DIM:, TILE:]], axis=0)
            o_ref[cols, o_lanes] = out.T.astype(bf16)
        return carry

    lax.fori_loop(0, PAIRS, pair, 0)
    o_ref[:, pl.ds(0, LANES)] = jnp.zeros((slot, LANES), bf16)
    vt_ref[...] = rot_ref[:, pl.ds(7 * LANES, LANES)].T
    for j in range((tiles + 1) // 2):
        which = 2 * j + info[8]

        @pl.when(which < tiles)
        def _():
            cols = pl.ds(pl.multiple_of(which * TILE, TILE), TILE)
            queries = pltpu.roll(rot_ref[cols, pl.ds(6 * LANES, LANES)].astype(f32), HEAD_DIM, 1)
            queries = jnp.where(lane_mask(TILE, True), queries, 0.0).astype(bf16)
            product, log_total = softmax_block(
                min(2 * j + 2, tiles),
                TILE,
                lambda t: rot_ref[pl.ds(t * TILE, TILE), pl.ds(6 * LANES, LANES)],
                queries,
                lambda t: bias_ref[pl.ds(t * TILE, TILE), cols],
            )
            lse_ref[PAIRS, :, pl.ds(j * TILE, TILE)] = jnp.broadcast_to(log_total, (8, TILE))
            out = jnp.concatenate([jnp.zeros((HEAD_DIM, TILE), f32), product[:HEAD_DIM]], axis=0)
            o_ref[cols, pl.ds(0, LANES)] = out.T.astype(bf16)

    for n in range(8):
        there = pl.ds(pl.multiple_of(info[n] * rows, 16), rows)
        mixed_ref[there, :] = o_ref[pl.ds(n * rows, rows), :]


def backward_kernel(
    info, rot_ref, cos_ref, sin_ref, bias_ref, mixed_ref, near_ref, far_ref, lse_ref, out_ref,
    d_ref, p_ref, ds_ref, kt_ref, dk_ref, dv_ref, dq_ref,
):
    slot = rot_ref.shape[0]
    rows = slot // 8
    tiles = slot // TILE
    for r in range(8):
        here = pl.ds(r * rows, rows)
        there = pl.ds(pl.multiple_of(info[9 + r] * rows, 16), rows)
        d_rows = (near_ref if r < 4 else far_ref)[pl.ds(r % 4 * rows, rows), :]
        d_ref[there, :] = d_rows
        p_ref[there, :] = d_rows.astype(f32) * mixed_ref[here, :].astype(f32)

    def row_sums(cols, lanes, upper):
        product = p_ref[cols, lanes]
        high = product.astype(bf16)
        low = (product - high.astype(f32)).astype(bf16)
        ones = jnp.where(lane_mask(8, upper), 1.0, 0.0).astype(bf16)
        return dot(ones, high, NT) + dot(ones, low, NT)

    def score_block(count, width, keys, values, queries, d_rows, biases, lse, centre):
        for t in range(count):
            here = pl.ds(t * TILE, TILE)
            probs = jnp.exp(dot(keys(t), queries, NT) + biases(t) - lse)
            d_probs = dot(values(t), d_rows, NT)
            d_scores = (probs * (d_probs - centre)).astype(bf16)
            ds_ref[here, pl.ds(0, width)] = d_scores
            dk_ref[here, :] += dot(d_scores, queries)
            dv_ref[here, :] += dot(probs.astype(bf16), d_rows)
        depth = count * TILE
        return dot(kt_ref[:, pl.ds(0, depth)], ds_ref[pl.ds(0, depth), pl.ds(0, width)]) * (HEAD_DIM**-0.5)

    def place(field_of, lanes, turned):
        for n in range(8):
            here = pl.ds(n * rows, rows)
            there = pl.ds(pl.multiple_of(info[n] * rows, 16), rows)
            field = field_of(here)
            if turned:
                field = field * cos_ref[here, :] - swap_halves(field) * sin_ref[here, :]
            out_ref[there, lanes] = field.astype(bf16)

    def pair(g, carry):
        q_lanes = pl.ds(pl.multiple_of(g * LANES, LANES), LANES)
        k_lanes = pl.ds(pl.multiple_of((PAIRS + g) * LANES, LANES), LANES)
        v_lanes = pl.ds(pl.multiple_of((2 * PAIRS + g) * LANES, LANES), LANES)
        o_lanes = pl.ds(pl.multiple_of((1 + g) * LANES, LANES), LANES)
        kt_ref[...] = rot_ref[:, k_lanes].T
        dk_ref[...] = jnp.zeros_like(dk_ref)
        dv_ref[...] = jnp.zeros_like(dv_ref)
        for i in range(tiles):
            cols = pl.ds(i * TILE, TILE)

            def biases(t):
                bias = bias_ref[pl.ds(t * TILE, TILE), cols]
                return jnp.concatenate([bias, bias], axis=1)

            centre = jnp.concatenate([row_sums(cols, o_lanes, False), row_sums(cols, o_lanes, True)], axis=1)
            d_query = score_block(
                i + 1,
                2 * TILE,
                lambda t: rot_ref[pl.ds(t * TILE, TILE), k_lanes],
                lambda t: rot_ref[pl.ds(t * TILE, TILE), v_lanes],
                two_heads(rot_ref[cols, q_lanes]),
                two_heads(d_ref[cols, o_lanes]),
                biases,
                lse_ref[g, pl.ds(0, 1), pl.ds(i * 2 * TILE, 2 * TILE)],
                centre[0:1],
            )
            out = jnp.concatenate([d_query[:HEAD_DIM, :TILE], d_query[HEAD_DIM:, TILE:]], axis=0)
            dq_ref[cols, :] = out.T
        place(lambda here: dq_ref[here, :], q_lanes, True)
        place(lambda here: dk_ref[here, :], k_lanes, True)
        place(lambda here: dv_ref[here, :], v_lanes, False)
        return carry

    lax.fori_loop(0, PAIRS, pair, 0)
    k_lanes, v_lanes = pl.ds(6 * LANES, LANES), pl.ds(7 * LANES, LANES)
    kt_ref[...] = rot_ref[:, k_lanes].T
    dk_ref[...] = jnp.zeros_like(dk_ref)
    dv_ref[...] = jnp.zeros_like(dv_ref)
    dq_ref[...] = jnp.zeros_like(dq_ref)
    for j in range((tiles + 1) // 2):
        which = 2 * j + info[8]

        @pl.when(which < tiles)
        def _():
            cols = pl.ds(pl.multiple_of(which * TILE, TILE), TILE)
            queries = pltpu.roll(rot_ref[cols, k_lanes].astype(f32), HEAD_DIM, 1)
            queries = jnp.where(lane_mask(TILE, True), queries, 0.0).astype(bf16)
            d_rows = pltpu.roll(d_ref[cols, pl.ds(0, LANES)].astype(f32), HEAD_DIM, 1)
            d_rows = jnp.where(lane_mask(TILE, False), d_rows, 0.0).astype(bf16)
            d_query = score_block(
                min(2 * j + 2, tiles),
                TILE,
                lambda t: rot_ref[pl.ds(t * TILE, TILE), k_lanes],
                lambda t: rot_ref[pl.ds(t * TILE, TILE), v_lanes],
                queries,
                d_rows,
                lambda t: bias_ref[pl.ds(t * TILE, TILE), cols],
                lse_ref[PAIRS, pl.ds(0, 1), pl.ds(j * TILE, TILE)],
                row_sums(cols, pl.ds(0, LANES), True)[0:1],
            )
            out = jnp.concatenate([d_query[HEAD_DIM:], jnp.zeros((HEAD_DIM, TILE), f32)], axis=0)
            dq_ref[cols, :] = out.T

    place(lambda here: dq_ref[here, :] + dk_ref[here, :], k_lanes, True)
    place(lambda here: dv_ref[here, :], v_lanes, False)


SMEM_SPEC = pl.BlockSpec(memory_space=pltpu.SMEM)
VMEM_SPEC = pl.BlockSpec(memory_space=pltpu.VMEM)


def attention_forward(info, qkv, cosine, sine, bias):
    slot = qkv.shape[0]
    pieces = slot // TILE
    return pl.pallas_call(
        forward_kernel,
        out_shape=(
            jax.ShapeDtypeStruct((slot, 8 * LANES), bf16),
            jax.ShapeDtypeStruct((slot, 3 * LANES), bf16),
            jax.ShapeDtypeStruct((PAIRS + 1, 8, pieces * 2 * TILE), f32),
        ),
        in_specs=[SMEM_SPEC] + [VMEM_SPEC] * 4,
        out_specs=(VMEM_SPEC,) * 3,
        scratch_shapes=[
            pltpu.VMEM((slot, 2 * TILE), f32),
            pltpu.VMEM((slot, 2 * TILE), bf16),
            pltpu.VMEM((LANES, slot), bf16),
            pltpu.VMEM((slot, 3 * LANES), bf16),
        ],
        compiler_params=pltpu.CompilerParams(vmem_limit_bytes=48 << 20),
        cost_estimate=pl.CostEstimate(flops=0, bytes_accessed=1024, transcendentals=0),
        name="attention_forward",
    )(info, qkv, cosine, sine, bias)


def attention_backward(info, rotated, cosine, sine, bias, mixed, near, far, log_total):
    slot = rotated.shape[0]
    return pl.pallas_call(
        backward_kernel,
        out_shape=jax.ShapeDtypeStruct((slot, 8 * LANES), bf16),
        in_specs=[SMEM_SPEC] + [VMEM_SPEC] * 8,
        out_specs=VMEM_SPEC,
        scratch_shapes=[
            pltpu.VMEM((slot, 3 * LANES), bf16),
            pltpu.VMEM((slot, 3 * LANES), f32),
            pltpu.VMEM((slot, 2 * TILE), bf16),
            pltpu.VMEM((LANES, slot), bf16),
            pltpu.VMEM((slot, LANES), f32),
            pltpu.VMEM((slot, LANES), f32),
            pltpu.VMEM((slot, LANES), f32),
        ],
        compiler_params=pltpu.CompilerParams(vmem_limit_bytes=48 << 20),
        cost_estimate=pl.CostEstimate(flops=0, bytes_accessed=1024, transcendentals=0),
        name="attention_backward",
    )(info, rotated, cosine, sine, bias, mixed, near, far, log_total)


def whole(shape):
    return pl.BlockSpec(shape, lambda i: (0,) * len(shape), pipeline_mode=pl.Buffered(1))


FREE = pl.CostEstimate(flops=0, bytes_accessed=1024, transcendentals=0)
ROOMY = pltpu.CompilerParams(vmem_limit_bytes=52 << 20)


def gate_kernel(rows_ref, w_ref, *refs):
    gate_up_ref, hidden_ref = refs[-2:]
    width = hidden_ref.shape[1]
    gate_up = dot(rows_ref[...], w_ref[...])
    gate_up_ref[...] = gate_up
    gate, up = gate_up[:, :width], gate_up[:, width:]
    hidden_ref[...] = (gate * jax.nn.sigmoid(gate) * up).astype(bf16)


def gate_half(rows, gu_w, width, earlier):
    count, depth = rows.shape
    tile = count // 4
    at = 4 if earlier else 0
    return pl.pallas_call(
        gate_kernel,
        grid=(4,),
        out_shape=(
            jax.ShapeDtypeStruct((2 * count, 2 * width), f32),
            jax.ShapeDtypeStruct((2 * count, width), bf16),
        ),
        in_specs=[pl.BlockSpec((tile, depth), lambda i: (i, 0)), whole((depth, 2 * width))]
        + [pl.BlockSpec(memory_space=pl.ANY)] * len(earlier),
        out_specs=(
            pl.BlockSpec((tile, 2 * width), lambda i: (i + at, 0)),
            pl.BlockSpec((tile, width), lambda i: (i + at, 0)),
        ),
        input_output_aliases={2: 0, 3: 1} if earlier else {},
        compiler_params=ROOMY,
        cost_estimate=FREE,
        name="gate_half",
    )(rows, gu_w, *earlier)


def hidden_back_kernel(rows_ref, w_ref, gate_up_ref, out_ref):
    width = w_ref.shape[1]
    d_hidden = dot(rows_ref[...], w_ref[...])
    gate, up = gate_up_ref[:, :width], gate_up_ref[:, width:]
    sigmoid_gate = jax.nn.sigmoid(gate)
    d_gate = d_hidden * up * sigmoid_gate * (1.0 + gate * (1.0 - sigmoid_gate))
    out_ref[:, :width] = d_gate.astype(bf16)
    out_ref[:, width:] = (d_hidden * (gate * sigmoid_gate)).astype(bf16)


def hidden_back(rows, down_w, gate_up):
    count, depth = rows.shape
    width = gate_up.shape[1] // 2
    tile = count // 8
    return pl.pallas_call(
        hidden_back_kernel,
        grid=(8,),
        out_shape=jax.ShapeDtypeStruct((count, 2 * width), bf16),
        in_specs=[
            pl.BlockSpec((tile, depth), lambda i: (i, 0)),
            whole((depth, width)),
            pl.BlockSpec((tile, 2 * width), lambda i: (i, 0)),
        ],
        out_specs=pl.BlockSpec((tile, 2 * width), lambda i: (i, 0)),
        compiler_params=ROOMY,
        cost_estimate=FREE,
        name="hidden_back",
    )(rows, down_w, gate_up)


def rows_kernel(rows_ref, w_ref, *refs):
    refs[-1][...] = dot(rows_ref[...], w_ref[...])


def project_half(rows, weight, cols, earlier):
    count, depth = rows.shape
    tile = count // 4
    at = 0 if earlier is None else 4
    earlier = () if earlier is None else (earlier,)
    return pl.pallas_call(
        rows_kernel,
        grid=(4,),
        out_shape=jax.ShapeDtypeStruct((2 * count, cols), f32),
        in_specs=[
            pl.BlockSpec((tile, depth), lambda i: (i, 0)),
            pl.BlockSpec((depth, cols), lambda i: (0, 0), pipeline_mode=pl.Buffered(1)),
        ]
        + [pl.BlockSpec(memory_space=pl.ANY)] * len(earlier),
        out_specs=pl.BlockSpec((tile, cols), lambda i: (i + at, 0)),
        input_output_aliases={2: 0} if earlier else {},
        compiler_params=ROOMY,
        cost_estimate=FREE,
        name="project_half",
    )(rows, weight, *earlier)


def grads_kernel(place, *refs):
    out_ref = refs[-1]
    products = []
    for near_ref, far_ref, right_ref in zip(refs[0:-1:3], refs[1:-1:3], refs[2:-1:3]):
        left = jnp.concatenate([near_ref[...], far_ref[...]], axis=0)
        products.append(dot(left, right_ref[...], TN))
    place(out_ref, *products)


def place_one(out_ref, product):
    out_ref[...] = product.astype(bf16)


def place_heads(out_ref, first, second):
    start = first.shape[1] - LANES
    out_ref[:, :start] = first[:, :start].astype(bf16)
    out_ref[:, start : start + LANES] = (first[:, start:] + second[:, :LANES]).astype(bf16)
    out_ref[:, start + LANES :] = second[:, LANES:].astype(bf16)


def weight_grads(place, cols, *triples):
    depth = triples[0][0].shape[1]
    specs, operands = [], []
    for near, far, right in triples:
        specs += [
            pl.BlockSpec((near.shape[0], 2 * LANES), lambda i: (0, i)),
            pl.BlockSpec((far.shape[0], 2 * LANES), lambda i: (0, i)),
            whole(right.shape),
        ]
        operands += [near, far, right]
    return pl.pallas_call(
        functools.partial(grads_kernel, place),
        grid=(depth // (2 * LANES),),
        out_shape=jax.ShapeDtypeStruct((depth, cols), bf16),
        in_specs=specs,
        out_specs=pl.BlockSpec((2 * LANES, cols), lambda i: (i, 0)),
        compiler_params=ROOMY,
        cost_estimate=FREE,
        name="weight_grads",
    )(*operands)


def shards(
    tokens,
    w_query,
    w_key,
    w_value,
    w_out,
    gain_attn,
    w_gate,
    w_up,
    w_down,
    gain_mlp,
    cotangent,
    lineage,
    padding,
    positions,
):
    slot = lineage.shape[1]
    on_x, on_mp = lax.axis_index("ctx"), lax.axis_index("mp")
    on_y, on_core = on_mp // 2, on_mp % 2
    lower_x = on_x == 0
    heads = w_query.shape[1] // HEAD_DIM
    own_cols = heads // 2 * HEAD_DIM
    ff_half = w_gate.shape[1] // 2
    ff_pad = -(-ff_half // LANES) * LANES

    info, back = [], []
    for n in range(8):
        d_x, d_y, d_core = on_x ^ (n // 4), on_y ^ (n // 2 % 2), on_core ^ (n % 2)
        info.append(d_core * 4 + d_x * 2 + d_y)
        from_x, from_y, from_core = on_x ^ (n // 2 % 2), on_y ^ (n % 2), on_core ^ (n // 4)
        back.append(from_x * 4 + from_y * 2 + from_core)
    info = jnp.stack(info + [on_x] + back).astype(jnp.int32)

    gain_a = gain_attn.astype(f32)
    gain_m = gain_mlp.astype(f32)
    inputs = tokens.astype(f32)
    grad_rows = cotangent.astype(f32)

    def both_x(mine, theirs):
        got = flip_x(theirs)
        return jnp.where(lower_x, jnp.concatenate([mine, got], 0), jnp.concatenate([got, mine], 0))

    out_t = w_out.T
    a_cols = [w[:, :own_cols] for w in (w_query, w_key, w_value, out_t)]
    b_cols = [w[:, own_cols : 2 * own_cols] for w in (w_query, w_key, w_value, out_t)]
    s_cols = [w[:, 2 * own_cols :] for w in (w_query, w_key, w_value, out_t)]

    def pack(cols):
        return jnp.concatenate(cols[:3] + s_cols + cols[3:], axis=1)

    attn_a, attn_b = pack(a_cols), pack(b_cols)
    attn_mine, attn_theirs = jnp.where(lower_x, attn_a, attn_b), jnp.where(lower_x, attn_b, attn_a)

    def halves(weight):
        fill = ((0, 0), (0, ff_pad - ff_half))
        first, second = jnp.pad(weight[:, :ff_half], fill), jnp.pad(weight[:, ff_half:], fill)
        return jnp.where(lower_x, first, second), jnp.where(lower_x, second, first)

    index = jnp.arange(slot, dtype=jnp.int32)
    own_seg = lineage[0]
    related = (
        (own_seg[:, None] == lineage[0][None, :])
        | (own_seg[:, None] == lineage[1][None, :])
        | (own_seg[:, None] == lineage[2][None, :])
    )
    live = padding == 0
    allowed = (index[:, None] == index[None, :]) | (
        related & live[:, None] & live[None, :] & (index[:, None] < index[None, :])
    )
    bias = jnp.where(allowed, 0.0, masked_value).astype(f32)
    half_dim = HEAD_DIM // 2
    inv_freq = rope_base ** (-2.0 * jnp.arange(half_dim, dtype=f32) / HEAD_DIM)
    angles = positions.astype(f32)[:, None] * inv_freq[None, :]
    cos, sin = jnp.cos(angles), jnp.sin(angles)
    cosine = jnp.concatenate([cos, cos, cos, cos], axis=1)
    sine = jnp.concatenate([-sin, sin, -sin, sin], axis=1)

    def rows_of_x(field):
        rows = field.shape[0] // 2
        mine = jnp.where(lower_x, field[:rows], field[rows:])
        return mine, flip_x(jnp.where(lower_x, field[rows:], field[:rows]))

    attn_got = flip_x(attn_theirs)
    count, on_dp = lax.axis_size("dp"), lax.axis_index("dp")

    def from_dp(field, k):
        return lax.ppermute(field, "dp", [(i, i ^ k) for i in range(count)])

    arrived = [from_dp(attn_mine, k) for k in range(1, count)]
    _, own_rows = after(attn_got, (normalize(inputs) * gain_a).astype(bf16))
    near_a, arrived[:2] = gather_near(own_rows, arrived[:2])
    near_a, arrived[2:], w_gate, w_up = after(near_a, arrived[2:], w_gate, w_up)
    gate_mine, gate_theirs = halves(w_gate)
    up_mine, up_theirs = halves(w_up)
    gu_part = both_x(
        jnp.concatenate([gate_mine, up_mine], 1), jnp.concatenate([gate_theirs, up_theirs], 1)
    )
    block = (1, 1) + attn_mine.shape
    attn_w = jnp.zeros((count, 2) + attn_mine.shape, bf16)
    for k, field in enumerate([attn_mine] + arrived):
        attn_w = lax.dynamic_update_slice(attn_w, field.reshape(block), (on_dp ^ k, on_x, 0, 0))
    attn_all = lax.all_gather(attn_got, "dp", axis=0, tiled=False)
    near_a, gu_part, attn_all, attn_w, bias, cosine, sine = after(
        near_a, gu_part, attn_all, attn_w, bias, cosine, sine
    )
    far_a = flip_core(near_a)
    attn_w = lax.dynamic_update_slice(attn_w, attn_all[:, None], (0, 1 - on_x, 0, 0))
    attn_w = attn_w.reshape(count * 2 * attn_mine.shape[0], attn_mine.shape[1])
    gu_w = lax.all_gather(gu_part, "dp", axis=0, tiled=True)
    qkv_w = attn_w[:, : 8 * LANES]
    out_w = attn_w[:, 7 * LANES :]
    qkv = project_half(far_a, attn_w, 8 * LANES, project_half(near_a, attn_w, 8 * LANES, None))
    qkv, w_down, grad_rows = after(qkv, w_down, grad_rows)
    near_d, far_d = gather_rows((branch_scale * grad_rows).astype(bf16))
    d_mlp = jnp.concatenate([near_d, far_d], axis=0)
    down_mine, down_theirs = halves(w_down.T)
    down_part = both_x(down_mine, down_theirs)
    rotated, mixed, log_total = attention_forward(info, qkv, cosine, sine, bias)
    residual = inputs + branch_scale * sum_rows(mixed, out_w, NT, pieces=4)
    near_m, (gu_w, d_mlp) = gather_near((normalize(residual) * gain_m).astype(bf16), (gu_w, d_mlp))
    down_w = lax.all_gather(down_part, "dp", axis=0, tiled=True)
    far_m = flip_core(near_m, 4)
    gate_up, hidden = gate_half(far_m, gu_w, ff_pad, gate_half(near_m, gu_w, ff_pad, ()))

    grad_down = weight_grads(place_one, ff_pad, (near_d, far_d, hidden))
    gate_up, grad_down = after(gate_up, grad_down)
    grad_down = lax.psum_scatter(grad_down, "dp", scatter_dimension=0, tiled=True)
    d_gate_up = hidden_back(d_mlp, down_w, gate_up)
    grad_gu = weight_grads(place_one, 2 * ff_pad, (near_m, far_m, d_gate_up))
    d_gate_up, grad_gu = after(d_gate_up, grad_gu)
    grad_gu = lax.psum_scatter(grad_gu, "dp", scatter_dimension=0, tiled=True)
    d_normed_mlp, grad_down = sum_rows(d_gate_up, gu_w, NT, grad_down)
    back_mlp, gain_mlp_part = norm_back(residual, gain_m, d_normed_mlp)
    d_residual = grad_rows + back_mlp

    near_o, far_o = gather_rows((branch_scale * d_residual).astype(bf16))
    d_mixed_near, d_mixed_far = dot(near_o, out_w).astype(bf16), dot(far_o, out_w).astype(bf16)
    d_qkv = attention_backward(
        info, rotated, cosine, sine, bias, mixed, d_mixed_near, d_mixed_far, log_total
    )
    grad_attn = weight_grads(
        place_heads, 10 * LANES, (near_a, far_a, d_qkv), (near_o, far_o, mixed)
    )
    grad_attn, grad_gu, d_qkv, hidden = after(grad_attn, grad_gu, d_qkv, hidden)
    grad_attn = lax.psum_scatter(grad_attn, "dp", scatter_dimension=0, tiled=True)
    gu_mine, gu_got = rows_of_x(grad_gu)
    gu_got, d_qkv, hidden = after(gu_got, d_qkv, hidden)
    d_normed_attn = sum_rows(d_qkv, qkv_w, NT, pieces=4)
    back_attn, gain_attn_part = norm_back(inputs, gain_a, d_normed_attn)
    input_grad = d_residual + back_attn
    gains, grad_attn = after(jnp.stack([gain_attn_part, gain_mlp_part]), grad_attn)
    gains = sum_all(gains)
    output = residual + branch_scale * sum_rows(hidden, down_w, NT, pieces=4)

    def join(mine, got):
        mine, got = mine.astype(f32), got.astype(f32)
        return jnp.where(lower_x, jnp.concatenate([mine, got], 1), jnp.concatenate([got, mine], 1))

    def join_heads(mine, got, at, shared_at):
        whole = join(mine[:, at : at + own_cols], got[:, at : at + own_cols])
        last = slice(shared_at, shared_at + HEAD_DIM)
        return jnp.concatenate([whole, mine[:, last].astype(f32) + got[:, last].astype(f32)], axis=1)

    mine, got = gu_mine, gu_got
    grad_gate = join(mine[:, :ff_half], got[:, :ff_half])
    grad_up = join(mine[:, ff_pad : ff_pad + ff_half], got[:, ff_pad : ff_pad + ff_half])
    mine, got = rows_of_x(grad_down)
    grad_down = join(mine[:, :ff_half], got[:, :ff_half]).T
    mine, got = rows_of_x(grad_attn)
    grad_query = join_heads(mine, got, 0, 6 * LANES)
    grad_key = join_heads(mine, got, 2 * LANES, 6 * LANES + HEAD_DIM)
    grad_value = join_heads(mine, got, 4 * LANES, 7 * LANES)
    grad_out = join_heads(mine, got, 8 * LANES, 7 * LANES + HEAD_DIM).T

    return (
        output.astype(bf16),
        input_grad.astype(bf16),
        grad_query,
        grad_key,
        grad_value,
        grad_out,
        gains[0],
        grad_gate,
        grad_up,
        grad_down,
        gains[1],
    )


def solution(mesh):
    placed = (
        P(("dp", "ctx", "mp"), None),
        P(("dp", "ctx"), "mp"),
        P(("dp", "ctx"), "mp"),
        P(("dp", "ctx"), "mp"),
        P("mp", ("dp", "ctx")),
        P(),
        P(("dp", "ctx"), "mp"),
        P(("dp", "ctx"), "mp"),
        P("mp", ("dp", "ctx")),
        P(),
        P(("dp", "ctx", "mp"), None),
        P(None, "dp"),
        P("dp"),
        P("dp"),
    )
    return jax.shard_map(
        shards,
        mesh=mesh,
        in_specs=placed,
        out_specs=(
            P(("dp", "ctx", "mp"), None),
            P(("dp", "ctx", "mp"), None),
            P(("dp", "ctx"), "mp"),
            P(("dp", "ctx"), "mp"),
            P(("dp", "ctx"), "mp"),
            P("mp", ("dp", "ctx")),
            P(),
            P(("dp", "ctx"), "mp"),
            P(("dp", "ctx"), "mp"),
            P("mp", ("dp", "ctx")),
            P(),
        ),
        check_vma=False,
    )
```

```python
import functools
import math

import jax
import jax.numpy as jnp
from jax import lax
from jax.experimental import pallas as pl
from jax.experimental.pallas import tpu as pltpu
from jax.sharding import PartitionSpec as P

HEAD_DIM = 64
LANES = 128
PAIRS = 2
TILE = 128

eps = 1e-05
branch_scale = 1.4 / math.sqrt(40.0)
rope_base = 10000.0
masked_value = -1e30

f32 = jnp.float32
bf16 = jnp.bfloat16

NN = (((1,), (0,)), ((), ()))
NT = (((1,), (1,)), ((), ()))
TN = (((0,), (0,)), ((), ()))


def dot(left, right, dims=NN):
    return lax.dot_general(left, right, dims, preferred_element_type=f32)


def after(*fields):
    return lax.optimization_barrier(fields)


def normalize(field):
    return field * lax.rsqrt(jnp.mean(field * field, axis=-1, keepdims=True) + eps)


def norm_back(field, gain_f32, incoming):
    inverse = lax.rsqrt(jnp.mean(field * field, axis=-1, keepdims=True) + eps)
    scaled = gain_f32 * incoming
    along = jnp.mean(field * scaled, axis=-1, keepdims=True)
    return (
        inverse * scaled - field * inverse**3 * along,
        jnp.sum(incoming * field * inverse, axis=0),
    )


def flip_x(field):
    return lax.ppermute(field, "ctx", [(0, 1), (1, 0)])


def flip_y(field):
    return lax.ppermute(field, "mp", [(0, 2), (2, 0), (1, 3), (3, 1)])


def flip_core(field, pieces=1):
    if pieces > 1:
        size = field.shape[0] // pieces
        parts = [flip_core(field[i * size : (i + 1) * size]) for i in range(pieces)]
        return jnp.concatenate(parts, axis=0)
    return lax.ppermute(field, "mp", [(0, 1), (1, 0), (2, 3), (3, 2)])


def gather_near(own, other=None):
    half = own.shape[0] // 2
    from_x, from_y = flip_x(own), flip_y(own)
    if other is not None:
        from_x, from_y, other = after(from_x, from_y, other)
    corner = jnp.concatenate([flip_y(from_x[:half]), flip_x(from_y[half:])], axis=0)
    near = jnp.concatenate([own, from_y, from_x, corner], axis=0)
    return near if other is None else (near, other)


def gather_rows(own):
    near = gather_near(own)
    return near, flip_core(near)


def sum_rows(left, right, dims, other=None, pieces=1):
    count = left.shape[0] // 2
    block = count // 4
    half = block // 2
    away = flip_core(dot(left[count:], right, dims).astype(bf16), pieces)
    total = dot(left[:count], right, dims) + away.astype(f32)
    total = total.reshape(2, 2, block, total.shape[-1])
    got_x = flip_x(total[1, :, :half].astype(bf16)).astype(f32)
    got_y = flip_y(total[:, 1, half:].astype(bf16)).astype(f32)
    upper = total[0, :, :half] + got_x
    lower = total[:, 0, half:] + got_y
    if other is not None:
        upper, other = after(upper, other)
    upper = upper[0] + flip_y(upper[1].astype(bf16)).astype(f32)
    lower = lower[0] + flip_x(lower[1].astype(bf16)).astype(f32)
    total = jnp.concatenate([upper, lower], axis=0)
    return total if other is None else (total, other)


def sum_all(field, other):
    total = flip_core(field) + field
    total = flip_y(total) + total
    total = flip_x(total) + total
    count, step = lax.axis_size("dp"), 1
    while step < count:
        if 2 * step >= count:
            total, other = after(total, other)
        total = lax.ppermute(total, "dp", [(i, i ^ step) for i in range(count)]) + total
        step *= 2
    return total, other


def lane_mask(rows, upper):
    lane = lax.broadcasted_iota(jnp.int32, (rows, LANES), 1)
    return lane >= HEAD_DIM if upper else lane < HEAD_DIM


def swap_halves(field):
    lane = lax.broadcasted_iota(jnp.int32, field.shape, 1)
    return jnp.where(
        lane % HEAD_DIM < HEAD_DIM // 2,
        pltpu.roll(field, LANES - HEAD_DIM // 2, 1),
        pltpu.roll(field, HEAD_DIM // 2, 1),
    )


def two_heads(block):
    zero = jnp.zeros_like(block)
    return jnp.concatenate(
        [
            jnp.where(lane_mask(block.shape[0], False), block, zero),
            jnp.where(lane_mask(block.shape[0], True), block, zero),
        ],
        axis=0,
    )


def forward_kernel(
    info, qkv_ref, cos_ref, sin_ref, bias_ref, rot_ref, mixed_ref, lse_ref, s_ref, e_ref, vt_ref, o_ref
):
    slot = qkv_ref.shape[0]
    rows = slot // 8
    tiles = slot // TILE
    for n in range(8):
        here = pl.ds(n * rows, rows)
        there = pl.ds(pl.multiple_of(info[n] * rows, 16), rows)
        cosine, sine = cos_ref[here, :], sin_ref[here, :]
        for g in (0, 1, 2, 3, 6):
            lanes = pl.ds(g * LANES, LANES)
            field = qkv_ref[there, lanes]
            field = field * cosine + swap_halves(field) * sine
            if g < 2:
                field = field * (HEAD_DIM**-0.5)
            if g == 6:
                field = jnp.where(lane_mask(rows, False), field * (HEAD_DIM**-0.5), field)
            rot_ref[here, lanes] = field.astype(bf16)
        for g in (4, 5):
            lanes = pl.ds(g * LANES, LANES)
            rot_ref[here, lanes] = qkv_ref[there, lanes].astype(bf16)
        lanes = pl.ds(7 * LANES, LANES)
        field = qkv_ref[there, lanes]
        rot_ref[here, lanes] = jnp.where(lane_mask(rows, False), field, 0.0).astype(bf16)

    def softmax_block(count, width, keys, queries, biases):
        top = jnp.full((8, width), masked_value, f32)
        for t in range(count):
            scores = dot(keys(t), queries, NT) + biases(t)
            s_ref[pl.ds(t * TILE, TILE), pl.ds(0, width)] = scores
            top = jnp.maximum(top, jnp.max(scores.reshape(TILE // 8, 8, width), axis=0))
        top = jnp.max(top, axis=0, keepdims=True)
        total = jnp.zeros((8, width), f32)
        for t in range(count):
            weights = jnp.exp(s_ref[pl.ds(t * TILE, TILE), pl.ds(0, width)] - top)
            total = total + jnp.sum(weights.reshape(TILE // 8, 8, width), axis=0)
            e_ref[pl.ds(t * TILE, TILE), pl.ds(0, width)] = weights.astype(bf16)
        total = jnp.sum(total, axis=0, keepdims=True)
        depth = count * TILE
        product = dot(vt_ref[:, pl.ds(0, depth)], e_ref[pl.ds(0, depth), pl.ds(0, width)])
        return product / total, top + jnp.log(total)

    def pair(g, carry):
        q_lanes = pl.ds(pl.multiple_of(g * LANES, LANES), LANES)
        k_lanes = pl.ds(pl.multiple_of((PAIRS + g) * LANES, LANES), LANES)
        v_lanes = pl.ds(pl.multiple_of((2 * PAIRS + g) * LANES, LANES), LANES)
        o_lanes = pl.ds(pl.multiple_of((1 + g) * LANES, LANES), LANES)
        vt_ref[...] = rot_ref[:, v_lanes].T
        for i in range(tiles):
            cols = pl.ds(i * TILE, TILE)

            def biases(t):
                bias = bias_ref[pl.ds(t * TILE, TILE), cols]
                return jnp.concatenate([bias, bias], axis=1)

            product, log_total = softmax_block(
                i + 1,
                2 * TILE,
                lambda t: rot_ref[pl.ds(t * TILE, TILE), k_lanes],
                two_heads(rot_ref[cols, q_lanes]),
                biases,
            )
            lse_ref[g, :, pl.ds(i * 2 * TILE, 2 * TILE)] = jnp.broadcast_to(log_total, (8, 2 * TILE))
            out = jnp.concatenate([product[:HEAD_DIM, :TILE], product[HEAD_DIM:, TILE:]], axis=0)
            o_ref[cols, o_lanes] = out.T.astype(bf16)
        return carry

    lax.fori_loop(0, PAIRS, pair, 0)
    o_ref[:, pl.ds(0, LANES)] = jnp.zeros((slot, LANES), bf16)
    vt_ref[...] = rot_ref[:, pl.ds(7 * LANES, LANES)].T
    for j in range((tiles + 1) // 2):
        which = 2 * j + info[8]

        @pl.when(which < tiles)
        def _():
            cols = pl.ds(pl.multiple_of(which * TILE, TILE), TILE)
            queries = pltpu.roll(rot_ref[cols, pl.ds(6 * LANES, LANES)].astype(f32), HEAD_DIM, 1)
            queries = jnp.where(lane_mask(TILE, True), queries, 0.0).astype(bf16)
            product, log_total = softmax_block(
                min(2 * j + 2, tiles),
                TILE,
                lambda t: rot_ref[pl.ds(t * TILE, TILE), pl.ds(6 * LANES, LANES)],
                queries,
                lambda t: bias_ref[pl.ds(t * TILE, TILE), cols],
            )
            lse_ref[PAIRS, :, pl.ds(j * TILE, TILE)] = jnp.broadcast_to(log_total, (8, TILE))
            out = jnp.concatenate([jnp.zeros((HEAD_DIM, TILE), f32), product[:HEAD_DIM]], axis=0)
            o_ref[cols, pl.ds(0, LANES)] = out.T.astype(bf16)

    for n in range(8):
        there = pl.ds(pl.multiple_of(info[n] * rows, 16), rows)
        mixed_ref[there, :] = o_ref[pl.ds(n * rows, rows), :]


def backward_kernel(
    info, rot_ref, cos_ref, sin_ref, bias_ref, mixed_ref, near_ref, far_ref, lse_ref, out_ref,
    d_ref, p_ref, ds_ref, kt_ref, dk_ref, dv_ref, dq_ref,
):
    slot = rot_ref.shape[0]
    rows = slot // 8
    tiles = slot // TILE
    for r in range(8):
        here = pl.ds(r * rows, rows)
        there = pl.ds(pl.multiple_of(info[9 + r] * rows, 16), rows)
        d_rows = (near_ref if r < 4 else far_ref)[pl.ds(r % 4 * rows, rows), :]
        d_ref[there, :] = d_rows
        p_ref[there, :] = d_rows.astype(f32) * mixed_ref[here, :].astype(f32)

    def row_sums(cols, lanes, upper):
        product = p_ref[cols, lanes]
        high = product.astype(bf16)
        low = (product - high.astype(f32)).astype(bf16)
        ones = jnp.where(lane_mask(8, upper), 1.0, 0.0).astype(bf16)
        return dot(ones, high, NT) + dot(ones, low, NT)

    def score_block(count, width, keys, values, queries, d_rows, biases, lse, centre):
        here = pl.ds(0, count * TILE)
        probs = jnp.exp(dot(keys(here), queries, NT) + biases(here) - lse)
        d_probs = dot(values(here), d_rows, NT)
        d_scores = (probs * (d_probs - centre)).astype(bf16)
        ds_ref[here, pl.ds(0, width)] = d_scores
        dk_ref[here, :] += dot(d_scores, queries)
        dv_ref[here, :] += dot(probs.astype(bf16), d_rows)
        return dot(kt_ref[:, here], ds_ref[here, pl.ds(0, width)]) * (HEAD_DIM**-0.5)

    def place(field_of, lanes, turned):
        for n in range(8):
            here = pl.ds(n * rows, rows)
            there = pl.ds(pl.multiple_of(info[n] * rows, 16), rows)
            field = field_of(here)
            if turned:
                field = field * cos_ref[here, :] - swap_halves(field) * sin_ref[here, :]
            out_ref[there, lanes] = field.astype(bf16)

    def pair(g, carry):
        q_lanes = pl.ds(pl.multiple_of(g * LANES, LANES), LANES)
        k_lanes = pl.ds(pl.multiple_of((PAIRS + g) * LANES, LANES), LANES)
        v_lanes = pl.ds(pl.multiple_of((2 * PAIRS + g) * LANES, LANES), LANES)
        o_lanes = pl.ds(pl.multiple_of((1 + g) * LANES, LANES), LANES)
        kt_ref[...] = rot_ref[:, k_lanes].T
        dk_ref[...] = jnp.zeros_like(dk_ref)
        dv_ref[...] = jnp.zeros_like(dv_ref)
        for i in range(tiles):
            cols = pl.ds(i * TILE, TILE)

            def biases(here):
                bias = bias_ref[here, cols]
                return jnp.concatenate([bias, bias], axis=1)

            centre = jnp.concatenate([row_sums(cols, o_lanes, False), row_sums(cols, o_lanes, True)], axis=1)
            d_query = score_block(
                i + 1,
                2 * TILE,
                lambda here: rot_ref[here, k_lanes],
                lambda here: rot_ref[here, v_lanes],
                two_heads(rot_ref[cols, q_lanes]),
                two_heads(d_ref[cols, o_lanes]),
                biases,
                lse_ref[g, pl.ds(0, 1), pl.ds(i * 2 * TILE, 2 * TILE)],
                centre[0:1],
            )
            out = jnp.concatenate([d_query[:HEAD_DIM, :TILE], d_query[HEAD_DIM:, TILE:]], axis=0)
            dq_ref[cols, :] = out.T
        place(lambda here: dq_ref[here, :], q_lanes, True)
        place(lambda here: dk_ref[here, :], k_lanes, True)
        place(lambda here: dv_ref[here, :], v_lanes, False)
        return carry

    lax.fori_loop(0, PAIRS, pair, 0)
    k_lanes, v_lanes = pl.ds(6 * LANES, LANES), pl.ds(7 * LANES, LANES)
    kt_ref[...] = rot_ref[:, k_lanes].T
    dk_ref[...] = jnp.zeros_like(dk_ref)
    dv_ref[...] = jnp.zeros_like(dv_ref)
    dq_ref[...] = jnp.zeros_like(dq_ref)
    for j in range((tiles + 1) // 2):
        which = 2 * j + info[8]

        @pl.when(which < tiles)
        def _():
            cols = pl.ds(pl.multiple_of(which * TILE, TILE), TILE)
            queries = pltpu.roll(rot_ref[cols, k_lanes].astype(f32), HEAD_DIM, 1)
            queries = jnp.where(lane_mask(TILE, True), queries, 0.0).astype(bf16)
            d_rows = pltpu.roll(d_ref[cols, pl.ds(0, LANES)].astype(f32), HEAD_DIM, 1)
            d_rows = jnp.where(lane_mask(TILE, False), d_rows, 0.0).astype(bf16)
            d_query = score_block(
                min(2 * j + 2, tiles),
                TILE,
                lambda here: rot_ref[here, k_lanes],
                lambda here: rot_ref[here, v_lanes],
                queries,
                d_rows,
                lambda here: bias_ref[here, cols],
                lse_ref[PAIRS, pl.ds(0, 1), pl.ds(j * TILE, TILE)],
                row_sums(cols, pl.ds(0, LANES), True)[0:1],
            )
            out = jnp.concatenate([d_query[HEAD_DIM:], jnp.zeros((HEAD_DIM, TILE), f32)], axis=0)
            dq_ref[cols, :] = out.T

    place(lambda here: dq_ref[here, :] + dk_ref[here, :], k_lanes, True)
    place(lambda here: dv_ref[here, :], v_lanes, False)


SMEM_SPEC = pl.BlockSpec(memory_space=pltpu.SMEM)
VMEM_SPEC = pl.BlockSpec(memory_space=pltpu.VMEM)


def attention_forward(info, qkv, cosine, sine, bias):
    slot = qkv.shape[0]
    pieces = slot // TILE
    return pl.pallas_call(
        forward_kernel,
        out_shape=(
            jax.ShapeDtypeStruct((slot, 8 * LANES), bf16),
            jax.ShapeDtypeStruct((slot, 3 * LANES), bf16),
            jax.ShapeDtypeStruct((PAIRS + 1, 8, pieces * 2 * TILE), f32),
        ),
        in_specs=[SMEM_SPEC] + [VMEM_SPEC] * 4,
        out_specs=(VMEM_SPEC,) * 3,
        scratch_shapes=[
            pltpu.VMEM((slot, 2 * TILE), f32),
            pltpu.VMEM((slot, 2 * TILE), bf16),
            pltpu.VMEM((LANES, slot), bf16),
            pltpu.VMEM((slot, 3 * LANES), bf16),
        ],
        compiler_params=pltpu.CompilerParams(vmem_limit_bytes=48 << 20),
        cost_estimate=pl.CostEstimate(flops=0, bytes_accessed=1024, transcendentals=0),
        name="attention_forward",
    )(info, qkv, cosine, sine, bias)


def attention_backward(info, rotated, cosine, sine, bias, mixed, near, far, log_total):
    slot = rotated.shape[0]
    return pl.pallas_call(
        backward_kernel,
        out_shape=jax.ShapeDtypeStruct((slot, 8 * LANES), bf16),
        in_specs=[SMEM_SPEC] + [VMEM_SPEC] * 8,
        out_specs=VMEM_SPEC,
        scratch_shapes=[
            pltpu.VMEM((slot, 3 * LANES), bf16),
            pltpu.VMEM((slot, 3 * LANES), f32),
            pltpu.VMEM((slot, 2 * TILE), bf16),
            pltpu.VMEM((LANES, slot), bf16),
            pltpu.VMEM((slot, LANES), f32),
            pltpu.VMEM((slot, LANES), f32),
            pltpu.VMEM((slot, LANES), f32),
        ],
        compiler_params=pltpu.CompilerParams(vmem_limit_bytes=48 << 20),
        cost_estimate=pl.CostEstimate(flops=0, bytes_accessed=1024, transcendentals=0),
        name="attention_backward",
    )(info, rotated, cosine, sine, bias, mixed, near, far, log_total)


def whole(shape):
    return pl.BlockSpec(shape, lambda i: (0,) * len(shape), pipeline_mode=pl.Buffered(1))


FREE = pl.CostEstimate(flops=0, bytes_accessed=1024, transcendentals=0)
ROOMY = pltpu.CompilerParams(vmem_limit_bytes=52 << 20)


def tail_lanes(shape, at, size):
    lane = lax.broadcasted_iota(jnp.int32, shape, 1)
    return (lane >= at) & (lane < at + size)


def tail_parts(tail, size):
    return pltpu.roll(tail, 2 * size, 1), pltpu.roll(tail, size, 1)


def gate_kernel(size, rows_ref, w_ref, *refs):
    gate_up_ref, main_ref, tail_ref = refs[-3:]
    width = main_ref.shape[1]
    gate_up = dot(rows_ref[...], w_ref[...])
    gate_up_ref[...] = gate_up
    gate, up = gate_up[:, :width], gate_up[:, width : 2 * width]
    main_ref[...] = (gate * jax.nn.sigmoid(gate) * up).astype(bf16)
    gate, up = tail_parts(gate_up[:, 2 * width :], size)
    tail = gate * jax.nn.sigmoid(gate) * up
    tail_ref[...] = jnp.where(tail_lanes(tail.shape, 2 * size, size), tail, 0.0).astype(bf16)


def gate_half(rows, gu_w, width, size, earlier):
    count, depth = rows.shape
    cols = gu_w.shape[1]
    tile = count // 4
    at = 4 if earlier else 0
    widths = (cols, width, cols - 2 * width)
    return pl.pallas_call(
        functools.partial(gate_kernel, size),
        grid=(4,),
        out_shape=tuple(
            jax.ShapeDtypeStruct((2 * count, w), kind) for w, kind in zip(widths, (f32, bf16, bf16))
        ),
        in_specs=[pl.BlockSpec((tile, depth), lambda i: (i, 0)), whole((depth, cols))]
        + [pl.BlockSpec(memory_space=pl.ANY)] * len(earlier),
        out_specs=tuple(pl.BlockSpec((tile, w), lambda i: (i + at, 0)) for w in widths),
        input_output_aliases={2: 0, 3: 1, 4: 2} if earlier else {},
        compiler_params=ROOMY,
        cost_estimate=FREE,
        name="gate_half",
    )(rows, gu_w, *earlier)


def gate_back(d_hidden, gate, up):
    sigmoid_gate = jax.nn.sigmoid(gate)
    d_gate = d_hidden * up * sigmoid_gate * (1.0 + gate * (1.0 - sigmoid_gate))
    return d_gate, d_hidden * (gate * sigmoid_gate)


def hidden_back_kernel(size, rows_ref, w_ref, tail_w_ref, gate_up_ref, out_ref):
    width = w_ref.shape[1]
    rows = rows_ref[...]
    d_gate, d_up = gate_back(
        dot(rows, w_ref[...]), gate_up_ref[:, :width], gate_up_ref[:, width : 2 * width]
    )
    out_ref[:, :width] = d_gate.astype(bf16)
    out_ref[:, width : 2 * width] = d_up.astype(bf16)
    gate, up = tail_parts(gate_up_ref[:, 2 * width :], size)
    d_gate, d_up = gate_back(dot(rows, tail_w_ref[...]), gate, up)
    lanes = d_gate.shape[1]
    d_gate = pltpu.roll(d_gate, lanes - 2 * size, 1)
    d_up = pltpu.roll(d_up, lanes - size, 1)
    tail = jnp.where(tail_lanes(d_up.shape, size, size), d_up, 0.0)
    tail = jnp.where(tail_lanes(d_up.shape, 0, size), d_gate, tail)
    out_ref[:, 2 * width :] = tail.astype(bf16)


def hidden_back(rows, down_w, gu_w, gate_up, size):
    count, depth = rows.shape
    width, cols = down_w.shape[1], gate_up.shape[1]
    tail = cols - 2 * width
    tile = count // 4
    return pl.pallas_call(
        functools.partial(hidden_back_kernel, size),
        grid=(4,),
        out_shape=jax.ShapeDtypeStruct((count, cols), bf16),
        in_specs=[
            pl.BlockSpec((tile, depth), lambda i: (i, 0)),
            whole((depth, width)),
            pl.BlockSpec((depth, tail), lambda i: (0, 2 * width // tail), pipeline_mode=pl.Buffered(1)),
            pl.BlockSpec((tile, cols), lambda i: (i, 0)),
        ],
        out_specs=pl.BlockSpec((tile, cols), lambda i: (i, 0)),
        compiler_params=ROOMY,
        cost_estimate=FREE,
        name="hidden_back",
    )(rows, down_w, gu_w, gate_up)


def rows_kernel(rows_ref, w_ref, *refs):
    refs[-1][...] = dot(rows_ref[...], w_ref[...])


def project_half(rows, weight, cols, earlier):
    count, depth = rows.shape
    tile = count // 4
    at = 0 if earlier is None else 4
    earlier = () if earlier is None else (earlier,)
    return pl.pallas_call(
        rows_kernel,
        grid=(4,),
        out_shape=jax.ShapeDtypeStruct((2 * count, cols), f32),
        in_specs=[
            pl.BlockSpec((tile, depth), lambda i: (i, 0)),
            pl.BlockSpec((depth, cols), lambda i: (0, 0), pipeline_mode=pl.Buffered(1)),
        ]
        + [pl.BlockSpec(memory_space=pl.ANY)] * len(earlier),
        out_specs=pl.BlockSpec((tile, cols), lambda i: (i + at, 0)),
        input_output_aliases={2: 0} if earlier else {},
        compiler_params=ROOMY,
        cost_estimate=FREE,
        name="project_half",
    )(rows, weight, *earlier)


def grads_kernel(place, *refs):
    out_ref = refs[-1]
    products = []
    for near_ref, far_ref, right_ref in zip(refs[0:-1:3], refs[1:-1:3], refs[2:-1:3]):
        left = jnp.concatenate([near_ref[...], far_ref[...]], axis=0)
        products.append(dot(left, right_ref[...], TN))
    place(out_ref, *products)


def place_one(out_ref, product):
    out_ref[...] = product.astype(bf16)


def place_tail(out_ref, first, second):
    start = first.shape[1] - second.shape[1]
    out_ref[:, :start] = first[:, :start].astype(bf16)
    out_ref[:, start:] = (first[:, start:] + second).astype(bf16)


def place_heads(out_ref, first, second):
    start = first.shape[1] - LANES
    out_ref[:, :start] = first[:, :start].astype(bf16)
    out_ref[:, start : start + LANES] = (first[:, start:] + second[:, :LANES]).astype(bf16)
    out_ref[:, start + LANES :] = second[:, LANES:].astype(bf16)


def weight_grads(place, cols, tile, *triples):
    depth = triples[0][0].shape[1]
    specs, operands = [], []
    for near, far, right in triples:
        specs += [
            pl.BlockSpec((near.shape[0], tile), lambda i: (0, i)),
            pl.BlockSpec((far.shape[0], tile), lambda i: (0, i)),
            whole(right.shape),
        ]
        operands += [near, far, right]
    return pl.pallas_call(
        functools.partial(grads_kernel, place),
        grid=(depth // tile,),
        out_shape=jax.ShapeDtypeStruct((depth, cols), bf16),
        in_specs=specs,
        out_specs=pl.BlockSpec((tile, cols), lambda i: (i, 0)),
        compiler_params=ROOMY,
        cost_estimate=FREE,
        name="weight_grads",
    )(*operands)


def shards(
    tokens,
    w_query,
    w_key,
    w_value,
    w_out,
    gain_attn,
    w_gate,
    w_up,
    w_down,
    gain_mlp,
    cotangent,
    lineage,
    padding,
    positions,
):
    slot = lineage.shape[1]
    on_x, on_mp = lax.axis_index("ctx"), lax.axis_index("mp")
    on_y, on_core = on_mp // 2, on_mp % 2
    lower_x = on_x == 0
    heads = w_query.shape[1] // HEAD_DIM
    own_cols = heads // 2 * HEAD_DIM
    ff_half = w_gate.shape[1] // 2
    ff_main = ff_half // LANES * LANES
    ff_tail = ff_half - ff_main

    info, back = [], []
    for n in range(8):
        d_x, d_y, d_core = on_x ^ (n // 4), on_y ^ (n // 2 % 2), on_core ^ (n % 2)
        info.append(d_core * 4 + d_x * 2 + d_y)
        from_x, from_y, from_core = on_x ^ (n // 2 % 2), on_y ^ (n % 2), on_core ^ (n // 4)
        back.append(from_x * 4 + from_y * 2 + from_core)
    info = jnp.stack(info + [on_x] + back).astype(jnp.int32)

    gain_a = gain_attn.astype(f32)
    gain_m = gain_mlp.astype(f32)
    inputs = tokens.astype(f32)
    grad_rows = cotangent.astype(f32)

    def both_x(mine, theirs):
        got = flip_x(theirs)
        return jnp.where(lower_x, jnp.concatenate([mine, got], 0), jnp.concatenate([got, mine], 0))

    out_t = w_out.T
    a_cols = [w[:, :own_cols] for w in (w_query, w_key, w_value, out_t)]
    b_cols = [w[:, own_cols : 2 * own_cols] for w in (w_query, w_key, w_value, out_t)]
    s_cols = [w[:, 2 * own_cols :] for w in (w_query, w_key, w_value, out_t)]

    def pack(cols):
        return jnp.concatenate(cols[:3] + s_cols + cols[3:], axis=1)

    attn_a, attn_b = pack(a_cols), pack(b_cols)
    attn_mine, attn_theirs = jnp.where(lower_x, attn_a, attn_b), jnp.where(lower_x, attn_b, attn_a)

    def halves(weight):
        first, second = weight[:, :ff_half], weight[:, ff_half:]
        return jnp.where(lower_x, first, second), jnp.where(lower_x, second, first)

    def pack_hidden(gate, up, down):
        fill = jnp.zeros((gate.shape[0], 2 * LANES - 3 * ff_tail), bf16)
        tails = [w[:, ff_main:] for w in (gate, up, down)]
        return jnp.concatenate([gate[:, :ff_main], up[:, :ff_main]] + tails + [fill], axis=1)

    index = jnp.arange(slot, dtype=jnp.int32)
    own_seg = lineage[0]
    related = (
        (own_seg[:, None] == lineage[0][None, :])
        | (own_seg[:, None] == lineage[1][None, :])
        | (own_seg[:, None] == lineage[2][None, :])
    )
    live = padding == 0
    allowed = (index[:, None] == index[None, :]) | (
        related & live[:, None] & live[None, :] & (index[:, None] < index[None, :])
    )
    bias = jnp.where(allowed, 0.0, masked_value).astype(f32)
    half_dim = HEAD_DIM // 2
    inv_freq = rope_base ** (-2.0 * jnp.arange(half_dim, dtype=f32) / HEAD_DIM)
    angles = positions.astype(f32)[:, None] * inv_freq[None, :]
    cos, sin = jnp.cos(angles), jnp.sin(angles)
    cosine = jnp.concatenate([cos, cos, cos, cos], axis=1)
    sine = jnp.concatenate([-sin, sin, -sin, sin], axis=1)

    def rows_of_x(field):
        rows = field.shape[0] // 2
        mine = jnp.where(lower_x, field[:rows], field[rows:])
        return mine, flip_x(jnp.where(lower_x, field[rows:], field[:rows]))

    attn_got = flip_x(attn_theirs)
    count, on_dp = lax.axis_size("dp"), lax.axis_index("dp")

    def from_dp(field, k):
        return lax.ppermute(field, "dp", [(i, i ^ k) for i in range(count)])

    arrived = [from_dp(attn_mine, k) for k in range(1, count)]
    _, own_rows = after(attn_got, (normalize(inputs) * gain_a).astype(bf16))
    near_a, arrived[:2] = gather_near(own_rows, arrived[:2])
    near_a, arrived[2:], w_gate, w_up, w_down = after(near_a, arrived[2:], w_gate, w_up, w_down)
    gate_mine, gate_theirs = halves(w_gate)
    up_mine, up_theirs = halves(w_up)
    down_mine, down_theirs = halves(w_down.T)
    gu_part = both_x(
        pack_hidden(gate_mine, up_mine, down_mine), pack_hidden(gate_theirs, up_theirs, down_theirs)
    )
    block = (1, 1) + attn_mine.shape
    attn_w = jnp.zeros((count, 2) + attn_mine.shape, bf16)
    for k, field in enumerate([attn_mine] + arrived):
        attn_w = lax.dynamic_update_slice(attn_w, field.reshape(block), (on_dp ^ k, on_x, 0, 0))
    attn_all = lax.all_gather(attn_got, "dp", axis=0, tiled=False)
    near_a, gu_part, attn_all, attn_w, bias, cosine, sine = after(
        near_a, gu_part, attn_all, attn_w, bias, cosine, sine
    )
    far_a = flip_core(near_a)
    attn_w = lax.dynamic_update_slice(attn_w, attn_all[:, None], (0, 1 - on_x, 0, 0))
    attn_w = attn_w.reshape(count * 2 * attn_mine.shape[0], attn_mine.shape[1])
    gu_w = lax.all_gather(gu_part, "dp", axis=0, tiled=True)
    qkv_w = attn_w[:, : 8 * LANES]
    out_w = attn_w[:, 7 * LANES :]
    qkv = project_half(far_a, attn_w, 8 * LANES, project_half(near_a, attn_w, 8 * LANES, None))
    qkv, down_mine, down_theirs, grad_rows = after(
        qkv, down_mine[:, :ff_main], down_theirs[:, :ff_main], grad_rows
    )
    near_d, far_d = gather_rows((branch_scale * grad_rows).astype(bf16))
    d_mlp = jnp.concatenate([near_d, far_d], axis=0)
    down_part = both_x(down_mine, down_theirs)
    rotated, mixed, log_total = attention_forward(info, qkv, cosine, sine, bias)
    residual = inputs + branch_scale * sum_rows(mixed, out_w, NT, pieces=4)
    own_m, gu_w, d_mlp = after((normalize(residual) * gain_m).astype(bf16), gu_w, d_mlp)
    near_m = gather_near(own_m)
    down_w = lax.all_gather(down_part, "dp", axis=0, tiled=True)
    far_m = flip_core(near_m, 4)
    earlier = gate_half(near_m, gu_w, ff_main, ff_tail, ())
    gate_up, hidden, hidden_tail = gate_half(far_m, gu_w, ff_main, ff_tail, earlier)

    grad_down = weight_grads(place_one, ff_main, 6 * LANES, (near_d, far_d, hidden))
    gate_up, grad_down = after(gate_up, grad_down)
    grad_down = lax.psum_scatter(grad_down, "dp", scatter_dimension=0, tiled=True)
    d_gate_up = hidden_back(d_mlp, down_w, gu_w, gate_up, ff_tail)
    grad_gu = weight_grads(
        place_tail,
        gate_up.shape[1],
        3 * LANES,
        (near_m, far_m, d_gate_up),
        (near_d, far_d, hidden_tail),
    )
    d_gate_up, grad_gu = after(d_gate_up, grad_gu)
    grad_gu = lax.psum_scatter(grad_gu, "dp", scatter_dimension=0, tiled=True)
    d_normed_mlp, grad_down = sum_rows(d_gate_up, gu_w, NT, grad_down)
    back_mlp, gain_mlp_part = norm_back(residual, gain_m, d_normed_mlp)
    d_residual = grad_rows + back_mlp

    near_o, far_o = gather_rows((branch_scale * d_residual).astype(bf16))
    d_mixed_near, d_mixed_far = dot(near_o, out_w).astype(bf16), dot(far_o, out_w).astype(bf16)
    d_qkv = attention_backward(
        info, rotated, cosine, sine, bias, mixed, d_mixed_near, d_mixed_far, log_total
    )
    grad_attn = weight_grads(
        place_heads, 10 * LANES, 3 * LANES, (near_a, far_a, d_qkv), (near_o, far_o, mixed)
    )
    grad_attn, grad_gu, d_qkv, hidden = after(grad_attn, grad_gu, d_qkv, hidden)
    grad_attn = lax.psum_scatter(grad_attn, "dp", scatter_dimension=0, tiled=True)
    tail_mine, tail_got = rows_of_x(grad_gu[:, 2 * ff_main :])
    tail_got, d_qkv, hidden = after(tail_got, d_qkv, hidden)
    gu_mine, gu_got = rows_of_x(grad_gu[:, : 2 * ff_main])
    d_normed_attn = sum_rows(d_qkv, qkv_w, NT, pieces=4)
    back_attn, gain_attn_part = norm_back(inputs, gain_a, d_normed_attn)
    input_grad = d_residual + back_attn
    gains, grad_attn = sum_all(jnp.stack([gain_attn_part, gain_mlp_part]), grad_attn)
    hidden = jnp.concatenate([hidden, hidden_tail], axis=1)
    down_w = jnp.concatenate([down_w, gu_w[:, 2 * ff_main :]], axis=1)
    output = residual + branch_scale * sum_rows(hidden, down_w, NT, pieces=4)

    def join(mine, got):
        mine, got = mine.astype(f32), got.astype(f32)
        return jnp.where(lower_x, jnp.concatenate([mine, got], 1), jnp.concatenate([got, mine], 1))

    def join_heads(mine, got, at, shared_at):
        whole = join(mine[:, at : at + own_cols], got[:, at : at + own_cols])
        last = slice(shared_at, shared_at + HEAD_DIM)
        return jnp.concatenate([whole, mine[:, last].astype(f32) + got[:, last].astype(f32)], axis=1)

    down_mine, down_got = rows_of_x(grad_down)

    def join_hidden(mine, got, at):
        last = slice(at * ff_tail, (at + 1) * ff_tail)
        mine = jnp.concatenate([mine, tail_mine[:, last]], axis=1)
        return join(mine, jnp.concatenate([got, tail_got[:, last]], axis=1))

    grad_gate = join_hidden(gu_mine[:, :ff_main], gu_got[:, :ff_main], 0)
    up_lanes = slice(ff_main, 2 * ff_main)
    grad_up = join_hidden(gu_mine[:, up_lanes], gu_got[:, up_lanes], 1)
    grad_down = join_hidden(down_mine, down_got, 2).T
    mine, got = rows_of_x(grad_attn)
    grad_query = join_heads(mine, got, 0, 6 * LANES)
    grad_key = join_heads(mine, got, 2 * LANES, 6 * LANES + HEAD_DIM)
    grad_value = join_heads(mine, got, 4 * LANES, 7 * LANES)
    grad_out = join_heads(mine, got, 8 * LANES, 7 * LANES + HEAD_DIM).T

    return (
        output.astype(bf16),
        input_grad.astype(bf16),
        grad_query,
        grad_key,
        grad_value,
        grad_out,
        gains[0],
        grad_gate,
        grad_up,
        grad_down,
        gains[1],
    )


def solution(mesh):
    placed = (
        P(("dp", "ctx", "mp"), None),
        P(("dp", "ctx"), "mp"),
        P(("dp", "ctx"), "mp"),
        P(("dp", "ctx"), "mp"),
        P("mp", ("dp", "ctx")),
        P(),
        P(("dp", "ctx"), "mp"),
        P(("dp", "ctx"), "mp"),
        P("mp", ("dp", "ctx")),
        P(),
        P(("dp", "ctx", "mp"), None),
        P(None, "dp"),
        P("dp"),
        P("dp"),
    )
    return jax.shard_map(
        shards,
        mesh=mesh,
        in_specs=placed,
        out_specs=(
            P(("dp", "ctx", "mp"), None),
            P(("dp", "ctx", "mp"), None),
            P(("dp", "ctx"), "mp"),
            P(("dp", "ctx"), "mp"),
            P(("dp", "ctx"), "mp"),
            P("mp", ("dp", "ctx")),
            P(),
            P(("dp", "ctx"), "mp"),
            P(("dp", "ctx"), "mp"),
            P("mp", ("dp", "ctx")),
            P(),
        ),
        check_vma=False,
    )
```

```python
import functools
import math

import jax
import jax.numpy as jnp
from jax import lax
from jax.experimental import pallas as pl
from jax.experimental.pallas import tpu as pltpu
from jax.sharding import PartitionSpec as P

HEAD_DIM = 64
LANES = 128
PAIRS = 2
TILE = 128

eps = 1e-05
branch_scale = 1.4 / math.sqrt(40.0)
rope_base = 10000.0
masked_value = -1e30

f32 = jnp.float32
bf16 = jnp.bfloat16

NN = (((1,), (0,)), ((), ()))
NT = (((1,), (1,)), ((), ()))
TN = (((0,), (0,)), ((), ()))


def dot(left, right, dims=NN):
    return lax.dot_general(left, right, dims, preferred_element_type=f32)


def after(*fields):
    return lax.optimization_barrier(fields)


def normalize(field):
    return field * lax.rsqrt(jnp.mean(field * field, axis=-1, keepdims=True) + eps)


def norm_back(field, gain_f32, incoming):
    inverse = lax.rsqrt(jnp.mean(field * field, axis=-1, keepdims=True) + eps)
    scaled = gain_f32 * incoming
    along = jnp.mean(field * scaled, axis=-1, keepdims=True)
    return (
        inverse * scaled - field * inverse**3 * along,
        jnp.sum(incoming * field * inverse, axis=0),
    )


def flip_x(field):
    return lax.ppermute(field, "ctx", [(0, 1), (1, 0)])


def flip_y(field):
    return lax.ppermute(field, "mp", [(0, 2), (2, 0), (1, 3), (3, 1)])


def flip_core(field, pieces=1):
    if pieces > 1:
        size = field.shape[0] // pieces
        parts = [flip_core(field[i * size : (i + 1) * size]) for i in range(pieces)]
        return jnp.concatenate(parts, axis=0)
    return lax.ppermute(field, "mp", [(0, 1), (1, 0), (2, 3), (3, 2)])


def gather_near(own, other=None):
    half = own.shape[0] // 2
    from_x, from_y = flip_x(own), flip_y(own)
    if other is not None:
        from_x, from_y, other = after(from_x, from_y, other)
    corner = jnp.concatenate([flip_y(from_x[:half]), flip_x(from_y[half:])], axis=0)
    near = jnp.concatenate([own, from_y, from_x, corner], axis=0)
    return near if other is None else (near, other)


def gather_rows(own):
    near = gather_near(own)
    return near, flip_core(near)


def sum_rows(left, right, dims, other=None, pieces=1):
    count = left.shape[0] // 2
    block = count // 4
    half = block // 2
    away = flip_core(dot(left[count:], right, dims).astype(bf16), pieces)
    total = dot(left[:count], right, dims) + away.astype(f32)
    total = total.reshape(2, 2, block, total.shape[-1])
    got_x = flip_x(total[1, :, :half].astype(bf16)).astype(f32)
    got_y = flip_y(total[:, 1, half:].astype(bf16)).astype(f32)
    upper = total[0, :, :half] + got_x
    lower = total[:, 0, half:] + got_y
    if other is not None:
        upper, other = after(upper, other)
    upper = upper[0] + flip_y(upper[1].astype(bf16)).astype(f32)
    lower = lower[0] + flip_x(lower[1].astype(bf16)).astype(f32)
    total = jnp.concatenate([upper, lower], axis=0)
    return total if other is None else (total, other)


def sum_all(field, other):
    total = flip_core(field) + field
    total = flip_y(total) + total
    total = flip_x(total) + total
    count, step = lax.axis_size("dp"), 1
    while step < count:
        if 2 * step >= count:
            total, other = after(total, other)
        total = lax.ppermute(total, "dp", [(i, i ^ step) for i in range(count)]) + total
        step *= 2
    return total, other


def lane_mask(rows, upper):
    lane = lax.broadcasted_iota(jnp.int32, (rows, LANES), 1)
    return lane >= HEAD_DIM if upper else lane < HEAD_DIM


def swap_halves(field):
    lane = lax.broadcasted_iota(jnp.int32, field.shape, 1)
    return jnp.where(
        lane % HEAD_DIM < HEAD_DIM // 2,
        pltpu.roll(field, LANES - HEAD_DIM // 2, 1),
        pltpu.roll(field, HEAD_DIM // 2, 1),
    )


def two_heads(block):
    zero = jnp.zeros_like(block)
    return jnp.concatenate(
        [
            jnp.where(lane_mask(block.shape[0], False), block, zero),
            jnp.where(lane_mask(block.shape[0], True), block, zero),
        ],
        axis=0,
    )


def forward_kernel(
    info, qkv_ref, cos_ref, sin_ref, bias_ref, rot_ref, mixed_ref, lse_ref, s_ref, e_ref, vt_ref, o_ref
):
    slot = qkv_ref.shape[0]
    rows = slot // 8
    tiles = slot // TILE
    for n in range(8):
        here = pl.ds(n * rows, rows)
        there = pl.ds(pl.multiple_of(info[n] * rows, 16), rows)
        cosine, sine = cos_ref[here, :], sin_ref[here, :]
        for g in (0, 1, 2, 3, 6):
            lanes = pl.ds(g * LANES, LANES)
            field = qkv_ref[there, lanes]
            field = field * cosine + swap_halves(field) * sine
            if g < 2:
                field = field * (HEAD_DIM**-0.5)
            if g == 6:
                field = jnp.where(lane_mask(rows, False), field * (HEAD_DIM**-0.5), field)
            rot_ref[here, lanes] = field.astype(bf16)
        for g in (4, 5):
            lanes = pl.ds(g * LANES, LANES)
            rot_ref[here, lanes] = qkv_ref[there, lanes].astype(bf16)
        lanes = pl.ds(7 * LANES, LANES)
        field = qkv_ref[there, lanes]
        rot_ref[here, lanes] = jnp.where(lane_mask(rows, False), field, 0.0).astype(bf16)

    def softmax_block(count, width, keys, queries, biases):
        top = jnp.full((8, width), masked_value, f32)
        for t in range(count):
            scores = dot(keys(t), queries, NT) + biases(t)
            s_ref[pl.ds(t * TILE, TILE), pl.ds(0, width)] = scores
            top = jnp.maximum(top, jnp.max(scores.reshape(TILE // 8, 8, width), axis=0))
        top = jnp.max(top, axis=0, keepdims=True)
        total = jnp.zeros((8, width), f32)
        for t in range(count):
            weights = jnp.exp(s_ref[pl.ds(t * TILE, TILE), pl.ds(0, width)] - top)
            total = total + jnp.sum(weights.reshape(TILE // 8, 8, width), axis=0)
            e_ref[pl.ds(t * TILE, TILE), pl.ds(0, width)] = weights.astype(bf16)
        total = jnp.sum(total, axis=0, keepdims=True)
        depth = count * TILE
        product = dot(vt_ref[:, pl.ds(0, depth)], e_ref[pl.ds(0, depth), pl.ds(0, width)])
        return product / total, top + jnp.log(total)

    def pair(g, carry):
        q_lanes = pl.ds(pl.multiple_of(g * LANES, LANES), LANES)
        k_lanes = pl.ds(pl.multiple_of((PAIRS + g) * LANES, LANES), LANES)
        v_lanes = pl.ds(pl.multiple_of((2 * PAIRS + g) * LANES, LANES), LANES)
        o_lanes = pl.ds(pl.multiple_of((1 + g) * LANES, LANES), LANES)
        vt_ref[...] = rot_ref[:, v_lanes].T
        for i in range(tiles):
            cols = pl.ds(i * TILE, TILE)

            def biases(t):
                bias = bias_ref[pl.ds(t * TILE, TILE), cols]
                return jnp.concatenate([bias, bias], axis=1)

            product, log_total = softmax_block(
                i + 1,
                2 * TILE,
                lambda t: rot_ref[pl.ds(t * TILE, TILE), k_lanes],
                two_heads(rot_ref[cols, q_lanes]),
                biases,
            )
            lse_ref[g, :, pl.ds(i * 2 * TILE, 2 * TILE)] = jnp.broadcast_to(log_total, (8, 2 * TILE))
            out = jnp.concatenate([product[:HEAD_DIM, :TILE], product[HEAD_DIM:, TILE:]], axis=0)
            o_ref[cols, o_lanes] = out.T.astype(bf16)
        return carry

    lax.fori_loop(0, PAIRS, pair, 0)
    o_ref[:, pl.ds(0, LANES)] = jnp.zeros((slot, LANES), bf16)
    vt_ref[...] = rot_ref[:, pl.ds(7 * LANES, LANES)].T
    for j in range((tiles + 1) // 2):
        which = 2 * j + info[8]

        @pl.when(which < tiles)
        def _():
            cols = pl.ds(pl.multiple_of(which * TILE, TILE), TILE)
            queries = pltpu.roll(rot_ref[cols, pl.ds(6 * LANES, LANES)].astype(f32), HEAD_DIM, 1)
            queries = jnp.where(lane_mask(TILE, True), queries, 0.0).astype(bf16)
            product, log_total = softmax_block(
                min(2 * j + 2, tiles),
                TILE,
                lambda t: rot_ref[pl.ds(t * TILE, TILE), pl.ds(6 * LANES, LANES)],
                queries,
                lambda t: bias_ref[pl.ds(t * TILE, TILE), cols],
            )
            lse_ref[PAIRS, :, pl.ds(j * TILE, TILE)] = jnp.broadcast_to(log_total, (8, TILE))
            out = jnp.concatenate([jnp.zeros((HEAD_DIM, TILE), f32), product[:HEAD_DIM]], axis=0)
            o_ref[cols, pl.ds(0, LANES)] = out.T.astype(bf16)

    for n in range(8):
        there = pl.ds(pl.multiple_of(info[n] * rows, 16), rows)
        mixed_ref[there, :] = o_ref[pl.ds(n * rows, rows), :]


def backward_kernel(
    info, rot_ref, cos_ref, sin_ref, bias_ref, mixed_ref, near_ref, far_ref, lse_ref, out_ref,
    d_ref, p_ref, ds_ref, kt_ref, dk_ref, dv_ref, dq_ref,
):
    slot = rot_ref.shape[0]
    rows = slot // 8
    tiles = slot // TILE
    for r in range(8):
        here = pl.ds(r * rows, rows)
        there = pl.ds(pl.multiple_of(info[9 + r] * rows, 16), rows)
        d_rows = (near_ref if r < 4 else far_ref)[pl.ds(r % 4 * rows, rows), :]
        d_ref[there, :] = d_rows
        p_ref[there, :] = d_rows.astype(f32) * mixed_ref[here, :].astype(f32)

    def row_sums(cols, lanes, upper):
        product = p_ref[cols, lanes]
        high = product.astype(bf16)
        low = (product - high.astype(f32)).astype(bf16)
        ones = jnp.where(lane_mask(8, upper), 1.0, 0.0).astype(bf16)
        return dot(ones, high, NT) + dot(ones, low, NT)

    def score_block(count, width, keys, values, queries, d_rows, biases, lse, centre):
        here = pl.ds(0, count * TILE)
        probs = jnp.exp(dot(keys(here), queries, NT) + biases(here) - lse)
        d_probs = dot(values(here), d_rows, NT)
        d_scores = (probs * (d_probs - centre)).astype(bf16)
        ds_ref[here, pl.ds(0, width)] = d_scores
        dk_ref[here, :] += dot(d_scores, queries)
        dv_ref[here, :] += dot(probs.astype(bf16), d_rows)
        return dot(kt_ref[:, here], ds_ref[here, pl.ds(0, width)]) * (HEAD_DIM**-0.5)

    def place(field_of, lanes, turned):
        for n in range(8):
            here = pl.ds(n * rows, rows)
            there = pl.ds(pl.multiple_of(info[n] * rows, 16), rows)
            field = field_of(here)
            if turned:
                field = field * cos_ref[here, :] - swap_halves(field) * sin_ref[here, :]
            out_ref[there, lanes] = field.astype(bf16)

    def pair(g, carry):
        q_lanes = pl.ds(pl.multiple_of(g * LANES, LANES), LANES)
        k_lanes = pl.ds(pl.multiple_of((PAIRS + g) * LANES, LANES), LANES)
        v_lanes = pl.ds(pl.multiple_of((2 * PAIRS + g) * LANES, LANES), LANES)
        o_lanes = pl.ds(pl.multiple_of((1 + g) * LANES, LANES), LANES)
        kt_ref[...] = rot_ref[:, k_lanes].T
        dk_ref[...] = jnp.zeros_like(dk_ref)
        dv_ref[...] = jnp.zeros_like(dv_ref)
        for i in range(tiles):
            cols = pl.ds(i * TILE, TILE)

            def biases(here):
                bias = bias_ref[here, cols]
                return jnp.concatenate([bias, bias], axis=1)

            centre = jnp.concatenate([row_sums(cols, o_lanes, False), row_sums(cols, o_lanes, True)], axis=1)
            d_query = score_block(
                i + 1,
                2 * TILE,
                lambda here: rot_ref[here, k_lanes],
                lambda here: rot_ref[here, v_lanes],
                two_heads(rot_ref[cols, q_lanes]),
                two_heads(d_ref[cols, o_lanes]),
                biases,
                lse_ref[g, pl.ds(0, 1), pl.ds(i * 2 * TILE, 2 * TILE)],
                centre[0:1],
            )
            out = jnp.concatenate([d_query[:HEAD_DIM, :TILE], d_query[HEAD_DIM:, TILE:]], axis=0)
            dq_ref[cols, :] = out.T
        place(lambda here: dq_ref[here, :], q_lanes, True)
        place(lambda here: dk_ref[here, :], k_lanes, True)
        place(lambda here: dv_ref[here, :], v_lanes, False)
        return carry

    lax.fori_loop(0, PAIRS, pair, 0)
    k_lanes, v_lanes = pl.ds(6 * LANES, LANES), pl.ds(7 * LANES, LANES)
    kt_ref[...] = rot_ref[:, k_lanes].T
    dk_ref[...] = jnp.zeros_like(dk_ref)
    dv_ref[...] = jnp.zeros_like(dv_ref)
    dq_ref[...] = jnp.zeros_like(dq_ref)
    for j in range((tiles + 1) // 2):
        which = 2 * j + info[8]

        @pl.when(which < tiles)
        def _():
            cols = pl.ds(pl.multiple_of(which * TILE, TILE), TILE)
            queries = pltpu.roll(rot_ref[cols, k_lanes].astype(f32), HEAD_DIM, 1)
            queries = jnp.where(lane_mask(TILE, True), queries, 0.0).astype(bf16)
            d_rows = pltpu.roll(d_ref[cols, pl.ds(0, LANES)].astype(f32), HEAD_DIM, 1)
            d_rows = jnp.where(lane_mask(TILE, False), d_rows, 0.0).astype(bf16)
            d_query = score_block(
                min(2 * j + 2, tiles),
                TILE,
                lambda here: rot_ref[here, k_lanes],
                lambda here: rot_ref[here, v_lanes],
                queries,
                d_rows,
                lambda here: bias_ref[here, cols],
                lse_ref[PAIRS, pl.ds(0, 1), pl.ds(j * TILE, TILE)],
                row_sums(cols, pl.ds(0, LANES), True)[0:1],
            )
            out = jnp.concatenate([d_query[HEAD_DIM:], jnp.zeros((HEAD_DIM, TILE), f32)], axis=0)
            dq_ref[cols, :] = out.T

    place(lambda here: dq_ref[here, :] + dk_ref[here, :], k_lanes, True)
    place(lambda here: dv_ref[here, :], v_lanes, False)


SMEM_SPEC = pl.BlockSpec(memory_space=pltpu.SMEM)
VMEM_SPEC = pl.BlockSpec(memory_space=pltpu.VMEM)


def attention_forward(info, qkv, cosine, sine, bias):
    slot = qkv.shape[0]
    pieces = slot // TILE
    return pl.pallas_call(
        forward_kernel,
        out_shape=(
            jax.ShapeDtypeStruct((slot, 8 * LANES), bf16),
            jax.ShapeDtypeStruct((slot, 3 * LANES), bf16),
            jax.ShapeDtypeStruct((PAIRS + 1, 8, pieces * 2 * TILE), f32),
        ),
        in_specs=[SMEM_SPEC] + [VMEM_SPEC] * 4,
        out_specs=(VMEM_SPEC,) * 3,
        scratch_shapes=[
            pltpu.VMEM((slot, 2 * TILE), f32),
            pltpu.VMEM((slot, 2 * TILE), bf16),
            pltpu.VMEM((LANES, slot), bf16),
            pltpu.VMEM((slot, 3 * LANES), bf16),
        ],
        compiler_params=pltpu.CompilerParams(vmem_limit_bytes=48 << 20),
        cost_estimate=pl.CostEstimate(flops=0, bytes_accessed=1024, transcendentals=0),
        name="attention_forward",
    )(info, qkv, cosine, sine, bias)


def attention_backward(info, rotated, cosine, sine, bias, mixed, near, far, log_total):
    slot = rotated.shape[0]
    return pl.pallas_call(
        backward_kernel,
        out_shape=jax.ShapeDtypeStruct((slot, 8 * LANES), bf16),
        in_specs=[SMEM_SPEC] + [VMEM_SPEC] * 8,
        out_specs=VMEM_SPEC,
        scratch_shapes=[
            pltpu.VMEM((slot, 3 * LANES), bf16),
            pltpu.VMEM((slot, 3 * LANES), f32),
            pltpu.VMEM((slot, 2 * TILE), bf16),
            pltpu.VMEM((LANES, slot), bf16),
            pltpu.VMEM((slot, LANES), f32),
            pltpu.VMEM((slot, LANES), f32),
            pltpu.VMEM((slot, LANES), f32),
        ],
        compiler_params=pltpu.CompilerParams(vmem_limit_bytes=48 << 20),
        cost_estimate=pl.CostEstimate(flops=0, bytes_accessed=1024, transcendentals=0),
        name="attention_backward",
    )(info, rotated, cosine, sine, bias, mixed, near, far, log_total)


def whole(shape):
    return pl.BlockSpec(shape, lambda i: (0,) * len(shape), pipeline_mode=pl.Buffered(1))


FREE = pl.CostEstimate(flops=0, bytes_accessed=1024, transcendentals=0)
ROOMY = pltpu.CompilerParams(vmem_limit_bytes=52 << 20)


def tail_lanes(shape, at, size):
    lane = lax.broadcasted_iota(jnp.int32, shape, 1)
    return (lane >= at) & (lane < at + size)


def tail_parts(tail, size):
    return pltpu.roll(tail, 2 * size, 1), pltpu.roll(tail, size, 1)


def gate_kernel(size, first_ref, second_ref, w_ref, *refs):
    gate_up_ref, main_ref, tail_ref = refs[-3:]
    width = main_ref.shape[1]

    def project(rows):
        gate_up = dot(rows, w_ref[...])
        gate_up_ref[...] = gate_up
        gate, up = gate_up[:, :width], gate_up[:, width : 2 * width]
        main_ref[...] = (gate * jax.nn.sigmoid(gate) * up).astype(bf16)
        gate, up = tail_parts(gate_up[:, 2 * width :], size)
        tail = gate * jax.nn.sigmoid(gate) * up
        tail_ref[...] = jnp.where(tail_lanes(tail.shape, 2 * size, size), tail, 0.0).astype(bf16)

    pl.when(pl.program_id(0) == 0)(lambda: project(first_ref[...]))
    pl.when(pl.program_id(0) == 1)(lambda: project(second_ref[...]))


def gate_blocks(blocks, places, gu_w, width, size, earlier):
    count, depth = blocks[0].shape
    cols = gu_w.shape[1]
    at, step = places[0], places[1] - places[0]
    widths = (cols, width, cols - 2 * width)
    return pl.pallas_call(
        functools.partial(gate_kernel, size),
        grid=(2,),
        out_shape=tuple(
            jax.ShapeDtypeStruct((8 * count, w), kind) for w, kind in zip(widths, (f32, bf16, bf16))
        ),
        in_specs=[whole((count, depth))] * 2
        + [whole((depth, cols))]
        + [pl.BlockSpec(memory_space=pl.ANY)] * len(earlier),
        out_specs=tuple(pl.BlockSpec((count, w), lambda i: (at + step * i, 0)) for w in widths),
        input_output_aliases={3: 0, 4: 1, 5: 2} if earlier else {},
        compiler_params=ROOMY,
        cost_estimate=pl.CostEstimate(flops=8 * count * depth * cols, bytes_accessed=1024, transcendentals=0),
        name="gate_blocks",
    )(*blocks, gu_w, *earlier)


def gate_back(d_hidden, gate, up):
    sigmoid_gate = jax.nn.sigmoid(gate)
    d_gate = d_hidden * up * sigmoid_gate * (1.0 + gate * (1.0 - sigmoid_gate))
    return d_gate, d_hidden * (gate * sigmoid_gate)


def hidden_back_kernel(size, rows_ref, w_ref, tail_w_ref, gate_up_ref, out_ref):
    width = w_ref.shape[1]
    rows = rows_ref[...]
    d_gate, d_up = gate_back(
        dot(rows, w_ref[...]), gate_up_ref[:, :width], gate_up_ref[:, width : 2 * width]
    )
    out_ref[:, :width] = d_gate.astype(bf16)
    out_ref[:, width : 2 * width] = d_up.astype(bf16)
    gate, up = tail_parts(gate_up_ref[:, 2 * width :], size)
    d_gate, d_up = gate_back(dot(rows, tail_w_ref[...]), gate, up)
    lanes = d_gate.shape[1]
    d_gate = pltpu.roll(d_gate, lanes - 2 * size, 1)
    d_up = pltpu.roll(d_up, lanes - size, 1)
    tail = jnp.where(tail_lanes(d_up.shape, size, size), d_up, 0.0)
    tail = jnp.where(tail_lanes(d_up.shape, 0, size), d_gate, tail)
    out_ref[:, 2 * width :] = tail.astype(bf16)


def hidden_back(rows, down_w, gu_w, gate_up, size):
    count, depth = rows.shape
    width, cols = down_w.shape[1], gate_up.shape[1]
    tail = cols - 2 * width
    tile = count // 4
    return pl.pallas_call(
        functools.partial(hidden_back_kernel, size),
        grid=(4,),
        out_shape=jax.ShapeDtypeStruct((count, cols), bf16),
        in_specs=[
            pl.BlockSpec((tile, depth), lambda i: (i, 0)),
            whole((depth, width)),
            pl.BlockSpec((depth, tail), lambda i: (0, 2 * width // tail), pipeline_mode=pl.Buffered(1)),
            pl.BlockSpec((tile, cols), lambda i: (i, 0)),
        ],
        out_specs=pl.BlockSpec((tile, cols), lambda i: (i, 0)),
        compiler_params=ROOMY,
        cost_estimate=FREE,
        name="hidden_back",
    )(rows, down_w, gu_w, gate_up)


def rows_kernel(rows_ref, w_ref, *refs):
    refs[-1][...] = dot(rows_ref[...], w_ref[...])


def project_half(rows, weight, cols, earlier):
    count, depth = rows.shape
    tile = count // 4
    at = 0 if earlier is None else 4
    earlier = () if earlier is None else (earlier,)
    return pl.pallas_call(
        rows_kernel,
        grid=(4,),
        out_shape=jax.ShapeDtypeStruct((2 * count, cols), f32),
        in_specs=[
            pl.BlockSpec((tile, depth), lambda i: (i, 0)),
            pl.BlockSpec((depth, cols), lambda i: (0, 0), pipeline_mode=pl.Buffered(1)),
        ]
        + [pl.BlockSpec(memory_space=pl.ANY)] * len(earlier),
        out_specs=pl.BlockSpec((tile, cols), lambda i: (i + at, 0)),
        input_output_aliases={2: 0} if earlier else {},
        compiler_params=ROOMY,
        cost_estimate=FREE,
        name="project_half",
    )(rows, weight, *earlier)


def grads_kernel(place, counts, *refs):
    out_ref = refs[-1]
    products, at = [], 0
    for count in counts:
        left = jnp.concatenate([ref[...] for ref in refs[at : at + count]], axis=0)
        products.append(dot(left, refs[at + count][...], TN))
        at += count + 1
    place(out_ref, *products)


def place_one(out_ref, product):
    out_ref[...] = product.astype(bf16)


def place_tail(out_ref, first, second):
    start = first.shape[1] - second.shape[1]
    out_ref[:, :start] = first[:, :start].astype(bf16)
    out_ref[:, start:] = (first[:, start:] + second).astype(bf16)


def place_heads(out_ref, first, second):
    start = first.shape[1] - LANES
    out_ref[:, :start] = first[:, :start].astype(bf16)
    out_ref[:, start : start + LANES] = (first[:, start:] + second[:, :LANES]).astype(bf16)
    out_ref[:, start + LANES :] = second[:, LANES:].astype(bf16)


def weight_grads(place, cols, tile, *products):
    depth = products[0][0][0].shape[1]
    specs, operands = [], []
    for pieces, right in products:
        specs += [pl.BlockSpec((piece.shape[0], tile), lambda i: (0, i)) for piece in pieces]
        specs += [whole(right.shape)]
        operands += [*pieces, right]
    counts = [len(pieces) for pieces, _ in products]
    return pl.pallas_call(
        functools.partial(grads_kernel, place, counts),
        grid=(depth // tile,),
        out_shape=jax.ShapeDtypeStruct((depth, cols), bf16),
        in_specs=specs,
        out_specs=pl.BlockSpec((tile, cols), lambda i: (i, 0)),
        compiler_params=ROOMY,
        cost_estimate=FREE,
        name="weight_grads",
    )(*operands)


def shards(
    tokens,
    w_query,
    w_key,
    w_value,
    w_out,
    gain_attn,
    w_gate,
    w_up,
    w_down,
    gain_mlp,
    cotangent,
    lineage,
    padding,
    positions,
):
    slot = lineage.shape[1]
    on_x, on_mp = lax.axis_index("ctx"), lax.axis_index("mp")
    on_y, on_core = on_mp // 2, on_mp % 2
    lower_x = on_x == 0
    heads = w_query.shape[1] // HEAD_DIM
    own_cols = heads // 2 * HEAD_DIM
    ff_half = w_gate.shape[1] // 2
    ff_main = ff_half // LANES * LANES
    ff_tail = ff_half - ff_main

    info, back = [], []
    for n in range(8):
        d_x, d_y, d_core = on_x ^ (n // 4), on_y ^ (n // 2 % 2), on_core ^ (n % 2)
        info.append(d_core * 4 + d_x * 2 + d_y)
        from_x, from_y, from_core = on_x ^ (n // 2 % 2), on_y ^ (n % 2), on_core ^ (n // 4)
        back.append(from_x * 4 + from_y * 2 + from_core)
    info = jnp.stack(info + [on_x] + back).astype(jnp.int32)

    gain_a = gain_attn.astype(f32)
    gain_m = gain_mlp.astype(f32)
    inputs = tokens.astype(f32)
    grad_rows = cotangent.astype(f32)

    def both_x(mine, theirs):
        got = flip_x(theirs)
        return jnp.where(lower_x, jnp.concatenate([mine, got], 0), jnp.concatenate([got, mine], 0))

    out_t = w_out.T
    a_cols = [w[:, :own_cols] for w in (w_query, w_key, w_value, out_t)]
    b_cols = [w[:, own_cols : 2 * own_cols] for w in (w_query, w_key, w_value, out_t)]
    s_cols = [w[:, 2 * own_cols :] for w in (w_query, w_key, w_value, out_t)]

    def pack(cols):
        return jnp.concatenate(cols[:3] + s_cols + cols[3:], axis=1)

    attn_a, attn_b = pack(a_cols), pack(b_cols)
    attn_mine, attn_theirs = jnp.where(lower_x, attn_a, attn_b), jnp.where(lower_x, attn_b, attn_a)

    def halves(weight):
        first, second = weight[:, :ff_half], weight[:, ff_half:]
        return jnp.where(lower_x, first, second), jnp.where(lower_x, second, first)

    def pack_hidden(gate, up, down):
        fill = jnp.zeros((gate.shape[0], 2 * LANES - 3 * ff_tail), bf16)
        tails = [w[:, ff_main:] for w in (gate, up, down)]
        return jnp.concatenate([gate[:, :ff_main], up[:, :ff_main]] + tails + [fill], axis=1)

    index = jnp.arange(slot, dtype=jnp.int32)
    own_seg = lineage[0]
    related = (
        (own_seg[:, None] == lineage[0][None, :])
        | (own_seg[:, None] == lineage[1][None, :])
        | (own_seg[:, None] == lineage[2][None, :])
    )
    live = padding == 0
    allowed = (index[:, None] == index[None, :]) | (
        related & live[:, None] & live[None, :] & (index[:, None] < index[None, :])
    )
    bias = jnp.where(allowed, 0.0, masked_value).astype(f32)
    half_dim = HEAD_DIM // 2
    inv_freq = rope_base ** (-2.0 * jnp.arange(half_dim, dtype=f32) / HEAD_DIM)
    angles = positions.astype(f32)[:, None] * inv_freq[None, :]
    cos, sin = jnp.cos(angles), jnp.sin(angles)
    cosine = jnp.concatenate([cos, cos, cos, cos], axis=1)
    sine = jnp.concatenate([-sin, sin, -sin, sin], axis=1)

    def rows_of_x(field):
        rows = field.shape[0] // 2
        mine = jnp.where(lower_x, field[:rows], field[rows:])
        return mine, flip_x(jnp.where(lower_x, field[rows:], field[:rows]))

    attn_got = flip_x(attn_theirs)
    count, on_dp = lax.axis_size("dp"), lax.axis_index("dp")

    def from_dp(field, k):
        return lax.ppermute(field, "dp", [(i, i ^ k) for i in range(count)])

    arrived = [from_dp(attn_mine, k) for k in range(1, count)]
    _, own_rows = after(attn_got, (normalize(inputs) * gain_a).astype(bf16))
    near_a, arrived[:2] = gather_near(own_rows, arrived[:2])
    near_a, arrived[2:], w_gate, w_up, w_down = after(near_a, arrived[2:], w_gate, w_up, w_down)
    gate_mine, gate_theirs = halves(w_gate)
    up_mine, up_theirs = halves(w_up)
    down_mine, down_theirs = halves(w_down.T)
    gu_part = both_x(
        pack_hidden(gate_mine, up_mine, down_mine), pack_hidden(gate_theirs, up_theirs, down_theirs)
    )
    block = (1, 1) + attn_mine.shape
    attn_w = jnp.zeros((count, 2) + attn_mine.shape, bf16)
    for k, field in enumerate([attn_mine] + arrived):
        attn_w = lax.dynamic_update_slice(attn_w, field.reshape(block), (on_dp ^ k, on_x, 0, 0))
    attn_all = lax.all_gather(attn_got, "dp", axis=0, tiled=False)
    near_a, gu_part, attn_all, attn_w, bias, cosine, sine = after(
        near_a, gu_part, attn_all, attn_w, bias, cosine, sine
    )
    far_a = flip_core(near_a)
    attn_w = lax.dynamic_update_slice(attn_w, attn_all[:, None], (0, 1 - on_x, 0, 0))
    attn_w = attn_w.reshape(count * 2 * attn_mine.shape[0], attn_mine.shape[1])
    gu_w = lax.all_gather(gu_part, "dp", axis=0, tiled=True)
    qkv_w = attn_w[:, : 8 * LANES]
    out_w = attn_w[:, 7 * LANES :]
    qkv = project_half(far_a, attn_w, 8 * LANES, project_half(near_a, attn_w, 8 * LANES, None))
    qkv, down_mine, down_theirs, grad_rows = after(
        qkv, down_mine[:, :ff_main], down_theirs[:, :ff_main], grad_rows
    )
    near_d, far_d = gather_rows((branch_scale * grad_rows).astype(bf16))
    d_mlp = jnp.concatenate([near_d, far_d], axis=0)
    down_part = both_x(down_mine, down_theirs)
    rotated, mixed, log_total = attention_forward(info, qkv, cosine, sine, bias)
    residual = inputs + branch_scale * sum_rows(mixed, out_w, NT, pieces=4)
    own_m, gu_w, d_mlp = after((normalize(residual) * gain_m).astype(bf16), gu_w, d_mlp)
    down_w = lax.all_gather(down_part, "dp", axis=0, tiled=True)
    half = own_m.shape[0] // 2
    from_x, from_y, own_c = flip_x(own_m), flip_y(own_m), flip_core(own_m)
    gates = gate_blocks((own_m, own_c), (0, 4), gu_w, ff_main, ff_tail, ())
    from_x, from_y, gates = after(from_x, from_y, gates)
    corner = jnp.concatenate([flip_y(from_x[:half]), flip_x(from_y[half:])], axis=0)
    y_c, x_c = flip_core(from_y), flip_core(from_x)
    gates = gate_blocks((from_y, from_x), (1, 2), gu_w, ff_main, ff_tail, gates)
    corner, gates = after(corner, gates)
    corner_c = flip_core(corner)
    gates = gate_blocks((y_c, x_c), (5, 6), gu_w, ff_main, ff_tail, gates)
    gates = gate_blocks((corner, corner_c), (3, 7), gu_w, ff_main, ff_tail, gates)
    gate_up, hidden, hidden_tail = gates
    all_m = (own_m, from_y, from_x, corner, own_c, y_c, x_c, corner_c)

    grad_down = weight_grads(place_one, ff_main, 6 * LANES, ((near_d, far_d), hidden))
    gate_up, grad_down = after(gate_up, grad_down)
    grad_down = lax.psum_scatter(grad_down, "dp", scatter_dimension=0, tiled=True)
    d_gate_up = hidden_back(d_mlp, down_w, gu_w, gate_up, ff_tail)
    grad_gu = weight_grads(
        place_tail,
        gate_up.shape[1],
        3 * LANES,
        (all_m, d_gate_up),
        ((near_d, far_d), hidden_tail),
    )
    d_gate_up, grad_gu = after(d_gate_up, grad_gu)
    grad_gu = lax.psum_scatter(grad_gu, "dp", scatter_dimension=0, tiled=True)
    d_normed_mlp, grad_down = sum_rows(d_gate_up, gu_w, NT, grad_down)
    back_mlp, gain_mlp_part = norm_back(residual, gain_m, d_normed_mlp)
    d_residual = grad_rows + back_mlp

    near_o, far_o = gather_rows((branch_scale * d_residual).astype(bf16))
    d_mixed_near, d_mixed_far = dot(near_o, out_w).astype(bf16), dot(far_o, out_w).astype(bf16)
    d_qkv = attention_backward(
        info, rotated, cosine, sine, bias, mixed, d_mixed_near, d_mixed_far, log_total
    )
    grad_attn = weight_grads(
        place_heads, 10 * LANES, 3 * LANES, ((near_a, far_a), d_qkv), ((near_o, far_o), mixed)
    )
    grad_attn, grad_gu, d_qkv, hidden = after(grad_attn, grad_gu, d_qkv, hidden)
    grad_attn = lax.psum_scatter(grad_attn, "dp", scatter_dimension=0, tiled=True)
    tail_mine, tail_got = rows_of_x(grad_gu[:, 2 * ff_main :])
    tail_got, d_qkv, hidden = after(tail_got, d_qkv, hidden)
    gu_mine, gu_got = rows_of_x(grad_gu[:, : 2 * ff_main])
    d_normed_attn = sum_rows(d_qkv, qkv_w, NT, pieces=4)
    back_attn, gain_attn_part = norm_back(inputs, gain_a, d_normed_attn)
    input_grad = d_residual + back_attn
    gains, grad_attn = sum_all(jnp.stack([gain_attn_part, gain_mlp_part]), grad_attn)
    hidden = jnp.concatenate([hidden, hidden_tail], axis=1)
    down_w = jnp.concatenate([down_w, gu_w[:, 2 * ff_main :]], axis=1)
    output = residual + branch_scale * sum_rows(hidden, down_w, NT, pieces=4)

    def join(mine, got):
        mine, got = mine.astype(f32), got.astype(f32)
        return jnp.where(lower_x, jnp.concatenate([mine, got], 1), jnp.concatenate([got, mine], 1))

    def join_heads(mine, got, at, shared_at):
        whole = join(mine[:, at : at + own_cols], got[:, at : at + own_cols])
        last = slice(shared_at, shared_at + HEAD_DIM)
        return jnp.concatenate([whole, mine[:, last].astype(f32) + got[:, last].astype(f32)], axis=1)

    down_mine, down_got = rows_of_x(grad_down)

    def join_hidden(mine, got, at):
        last = slice(at * ff_tail, (at + 1) * ff_tail)
        mine = jnp.concatenate([mine, tail_mine[:, last]], axis=1)
        return join(mine, jnp.concatenate([got, tail_got[:, last]], axis=1))

    grad_gate = join_hidden(gu_mine[:, :ff_main], gu_got[:, :ff_main], 0)
    up_lanes = slice(ff_main, 2 * ff_main)
    grad_up = join_hidden(gu_mine[:, up_lanes], gu_got[:, up_lanes], 1)
    grad_down = join_hidden(down_mine, down_got, 2).T
    mine, got = rows_of_x(grad_attn)
    grad_query = join_heads(mine, got, 0, 6 * LANES)
    grad_key = join_heads(mine, got, 2 * LANES, 6 * LANES + HEAD_DIM)
    grad_value = join_heads(mine, got, 4 * LANES, 7 * LANES)
    grad_out = join_heads(mine, got, 8 * LANES, 7 * LANES + HEAD_DIM).T

    return (
        output.astype(bf16),
        input_grad.astype(bf16),
        grad_query,
        grad_key,
        grad_value,
        grad_out,
        gains[0],
        grad_gate,
        grad_up,
        grad_down,
        gains[1],
    )


def solution(mesh):
    placed = (
        P(("dp", "ctx", "mp"), None),
        P(("dp", "ctx"), "mp"),
        P(("dp", "ctx"), "mp"),
        P(("dp", "ctx"), "mp"),
        P("mp", ("dp", "ctx")),
        P(),
        P(("dp", "ctx"), "mp"),
        P(("dp", "ctx"), "mp"),
        P("mp", ("dp", "ctx")),
        P(),
        P(("dp", "ctx", "mp"), None),
        P(None, "dp"),
        P("dp"),
        P("dp"),
    )
    return jax.shard_map(
        shards,
        mesh=mesh,
        in_specs=placed,
        out_specs=(
            P(("dp", "ctx", "mp"), None),
            P(("dp", "ctx", "mp"), None),
            P(("dp", "ctx"), "mp"),
            P(("dp", "ctx"), "mp"),
            P(("dp", "ctx"), "mp"),
            P("mp", ("dp", "ctx")),
            P(),
            P(("dp", "ctx"), "mp"),
            P(("dp", "ctx"), "mp"),
            P("mp", ("dp", "ctx")),
            P(),
        ),
        check_vma=False,
    )
```

```python
import functools
import math

import jax
import jax.numpy as jnp
from jax import lax
from jax.experimental import pallas as pl
from jax.experimental.pallas import tpu as pltpu
from jax.sharding import PartitionSpec as P

HEAD_DIM = 64
LANES = 128
PAIRS = 2
TILE = 128

eps = 1e-05
branch_scale = 1.4 / math.sqrt(40.0)
rope_base = 10000.0
masked_value = -1e30

f32 = jnp.float32
bf16 = jnp.bfloat16

NN = (((1,), (0,)), ((), ()))
NT = (((1,), (1,)), ((), ()))
TN = (((0,), (0,)), ((), ()))


def dot(left, right, dims=NN):
    return lax.dot_general(left, right, dims, preferred_element_type=f32)


def after(*fields):
    return lax.optimization_barrier(fields)


def normalize(field):
    return field * lax.rsqrt(jnp.mean(field * field, axis=-1, keepdims=True) + eps)


def norm_back(field, gain_f32, incoming):
    inverse = lax.rsqrt(jnp.mean(field * field, axis=-1, keepdims=True) + eps)
    scaled = gain_f32 * incoming
    along = jnp.mean(field * scaled, axis=-1, keepdims=True)
    return (
        inverse * scaled - field * inverse**3 * along,
        jnp.sum(incoming * field * inverse, axis=0),
    )


def flip_x(field):
    return lax.ppermute(field, "ctx", [(0, 1), (1, 0)])


def flip_y(field):
    return lax.ppermute(field, "mp", [(0, 2), (2, 0), (1, 3), (3, 1)])


def flip_core(field, pieces=1):
    if pieces > 1:
        size = field.shape[0] // pieces
        parts = [flip_core(field[i * size : (i + 1) * size]) for i in range(pieces)]
        return jnp.concatenate(parts, axis=0)
    return lax.ppermute(field, "mp", [(0, 1), (1, 0), (2, 3), (3, 2)])


def gather_near(own, other=None):
    half = own.shape[0] // 2
    from_x, from_y = flip_x(own), flip_y(own)
    if other is not None:
        from_x, from_y, other = after(from_x, from_y, other)
    corner = jnp.concatenate([flip_y(from_x[:half]), flip_x(from_y[half:])], axis=0)
    near = jnp.concatenate([own, from_y, from_x, corner], axis=0)
    return near if other is None else (near, other)


def gather_rows(own):
    near = gather_near(own)
    return near, flip_core(near)


def sum_rows(left, right, dims, other=None, pieces=1):
    count = left.shape[0] // 2
    block = count // 4
    half = block // 2
    away = flip_core(dot(left[count:], right, dims).astype(bf16), pieces)
    total = dot(left[:count], right, dims) + away.astype(f32)
    total = total.reshape(2, 2, block, total.shape[-1])
    got_x = flip_x(total[1, :, :half].astype(bf16)).astype(f32)
    got_y = flip_y(total[:, 1, half:].astype(bf16)).astype(f32)
    upper = total[0, :, :half] + got_x
    lower = total[:, 0, half:] + got_y
    if other is not None:
        upper, other = after(upper, other)
    upper = upper[0] + flip_y(upper[1].astype(bf16)).astype(f32)
    lower = lower[0] + flip_x(lower[1].astype(bf16)).astype(f32)
    total = jnp.concatenate([upper, lower], axis=0)
    return total if other is None else (total, other)


def sum_all(field, other):
    total = flip_core(field) + field
    total = flip_y(total) + total
    total = flip_x(total) + total
    count, step = lax.axis_size("dp"), 1
    while step < count:
        if 2 * step >= count:
            total, other = after(total, other)
        total = lax.ppermute(total, "dp", [(i, i ^ step) for i in range(count)]) + total
        step *= 2
    return total, other


def lane_mask(rows, upper):
    lane = lax.broadcasted_iota(jnp.int32, (rows, LANES), 1)
    return lane >= HEAD_DIM if upper else lane < HEAD_DIM


def swap_halves(field):
    lane = lax.broadcasted_iota(jnp.int32, field.shape, 1)
    return jnp.where(
        lane % HEAD_DIM < HEAD_DIM // 2,
        pltpu.roll(field, LANES - HEAD_DIM // 2, 1),
        pltpu.roll(field, HEAD_DIM // 2, 1),
    )


def two_heads(block):
    zero = jnp.zeros_like(block)
    return jnp.concatenate(
        [
            jnp.where(lane_mask(block.shape[0], False), block, zero),
            jnp.where(lane_mask(block.shape[0], True), block, zero),
        ],
        axis=0,
    )


def forward_kernel(
    info, qkv_ref, cos_ref, sin_ref, bias_ref, rot_ref, mixed_ref, lse_ref, s_ref, e_ref, vt_ref, o_ref
):
    slot = qkv_ref.shape[0]
    rows = slot // 8
    tiles = slot // TILE
    for n in range(8):
        here = pl.ds(n * rows, rows)
        there = pl.ds(pl.multiple_of(info[n] * rows, 16), rows)
        cosine, sine = cos_ref[here, :], sin_ref[here, :]
        for g in (0, 1, 2, 3, 6):
            lanes = pl.ds(g * LANES, LANES)
            field = qkv_ref[there, lanes]
            field = field * cosine + swap_halves(field) * sine
            if g < 2:
                field = field * (HEAD_DIM**-0.5)
            if g == 6:
                field = jnp.where(lane_mask(rows, False), field * (HEAD_DIM**-0.5), field)
            rot_ref[here, lanes] = field.astype(bf16)
        for g in (4, 5):
            lanes = pl.ds(g * LANES, LANES)
            rot_ref[here, lanes] = qkv_ref[there, lanes].astype(bf16)
        lanes = pl.ds(7 * LANES, LANES)
        field = qkv_ref[there, lanes]
        rot_ref[here, lanes] = jnp.where(lane_mask(rows, False), field, 0.0).astype(bf16)

    def softmax_block(count, width, keys, queries, biases):
        top = jnp.full((8, width), masked_value, f32)
        for t in range(count):
            scores = dot(keys(t), queries, NT) + biases(t)
            s_ref[pl.ds(t * TILE, TILE), pl.ds(0, width)] = scores
            top = jnp.maximum(top, jnp.max(scores.reshape(TILE // 8, 8, width), axis=0))
        top = jnp.max(top, axis=0, keepdims=True)
        total = jnp.zeros((8, width), f32)
        for t in range(count):
            weights = jnp.exp(s_ref[pl.ds(t * TILE, TILE), pl.ds(0, width)] - top)
            total = total + jnp.sum(weights.reshape(TILE // 8, 8, width), axis=0)
            e_ref[pl.ds(t * TILE, TILE), pl.ds(0, width)] = weights.astype(bf16)
        total = jnp.sum(total, axis=0, keepdims=True)
        depth = count * TILE
        product = dot(vt_ref[:, pl.ds(0, depth)], e_ref[pl.ds(0, depth), pl.ds(0, width)])
        return product / total, top + jnp.log(total)

    def pair(g, carry):
        q_lanes = pl.ds(pl.multiple_of(g * LANES, LANES), LANES)
        k_lanes = pl.ds(pl.multiple_of((PAIRS + g) * LANES, LANES), LANES)
        v_lanes = pl.ds(pl.multiple_of((2 * PAIRS + g) * LANES, LANES), LANES)
        o_lanes = pl.ds(pl.multiple_of((1 + g) * LANES, LANES), LANES)
        vt_ref[...] = rot_ref[:, v_lanes].T
        for i in range(tiles):
            cols = pl.ds(i * TILE, TILE)

            def biases(t):
                bias = bias_ref[pl.ds(t * TILE, TILE), cols]
                return jnp.concatenate([bias, bias], axis=1)

            product, log_total = softmax_block(
                i + 1,
                2 * TILE,
                lambda t: rot_ref[pl.ds(t * TILE, TILE), k_lanes],
                two_heads(rot_ref[cols, q_lanes]),
                biases,
            )
            lse_ref[g, :, pl.ds(i * 2 * TILE, 2 * TILE)] = jnp.broadcast_to(log_total, (8, 2 * TILE))
            out = jnp.concatenate([product[:HEAD_DIM, :TILE], product[HEAD_DIM:, TILE:]], axis=0)
            o_ref[cols, o_lanes] = out.T.astype(bf16)
        return carry

    lax.fori_loop(0, PAIRS, pair, 0)
    o_ref[:, pl.ds(0, LANES)] = jnp.zeros((slot, LANES), bf16)
    vt_ref[...] = rot_ref[:, pl.ds(7 * LANES, LANES)].T
    for j in range((tiles + 1) // 2):
        which = 2 * j + info[8]

        @pl.when(which < tiles)
        def _():
            cols = pl.ds(pl.multiple_of(which * TILE, TILE), TILE)
            queries = pltpu.roll(rot_ref[cols, pl.ds(6 * LANES, LANES)].astype(f32), HEAD_DIM, 1)
            queries = jnp.where(lane_mask(TILE, True), queries, 0.0).astype(bf16)
            product, log_total = softmax_block(
                min(2 * j + 2, tiles),
                TILE,
                lambda t: rot_ref[pl.ds(t * TILE, TILE), pl.ds(6 * LANES, LANES)],
                queries,
                lambda t: bias_ref[pl.ds(t * TILE, TILE), cols],
            )
            lse_ref[PAIRS, :, pl.ds(j * TILE, TILE)] = jnp.broadcast_to(log_total, (8, TILE))
            out = jnp.concatenate([jnp.zeros((HEAD_DIM, TILE), f32), product[:HEAD_DIM]], axis=0)
            o_ref[cols, pl.ds(0, LANES)] = out.T.astype(bf16)

    for n in range(8):
        there = pl.ds(pl.multiple_of(info[n] * rows, 16), rows)
        mixed_ref[there, :] = o_ref[pl.ds(n * rows, rows), :]


def backward_kernel(
    info, rot_ref, cos_ref, sin_ref, bias_ref, mixed_ref, near_ref, far_ref, lse_ref, out_ref,
    d_ref, p_ref, ds_ref, kt_ref, dk_ref, dv_ref, dq_ref,
):
    slot = rot_ref.shape[0]
    rows = slot // 8
    tiles = slot // TILE
    for r in range(8):
        here = pl.ds(r * rows, rows)
        there = pl.ds(pl.multiple_of(info[9 + r] * rows, 16), rows)
        d_rows = (near_ref if r < 4 else far_ref)[pl.ds(r % 4 * rows, rows), :]
        d_ref[there, :] = d_rows
        p_ref[there, :] = d_rows.astype(f32) * mixed_ref[here, :].astype(f32)

    def row_sums(cols, lanes, upper):
        product = p_ref[cols, lanes]
        high = product.astype(bf16)
        low = (product - high.astype(f32)).astype(bf16)
        ones = jnp.where(lane_mask(8, upper), 1.0, 0.0).astype(bf16)
        return dot(ones, high, NT) + dot(ones, low, NT)

    def score_block(count, width, keys, values, queries, d_rows, biases, lse, centre):
        here = pl.ds(0, count * TILE)
        probs = jnp.exp(dot(keys(here), queries, NT) + biases(here) - lse)
        d_probs = dot(values(here), d_rows, NT)
        d_scores = (probs * (d_probs - centre)).astype(bf16)
        ds_ref[here, pl.ds(0, width)] = d_scores
        dk_ref[here, :] += dot(d_scores, queries)
        dv_ref[here, :] += dot(probs.astype(bf16), d_rows)
        return dot(kt_ref[:, here], ds_ref[here, pl.ds(0, width)]) * (HEAD_DIM**-0.5)

    def place(field_of, lanes, turned):
        for n in range(8):
            here = pl.ds(n * rows, rows)
            there = pl.ds(pl.multiple_of(info[n] * rows, 16), rows)
            field = field_of(here)
            if turned:
                field = field * cos_ref[here, :] - swap_halves(field) * sin_ref[here, :]
            out_ref[there, lanes] = field.astype(bf16)

    def pair(g, carry):
        q_lanes = pl.ds(pl.multiple_of(g * LANES, LANES), LANES)
        k_lanes = pl.ds(pl.multiple_of((PAIRS + g) * LANES, LANES), LANES)
        v_lanes = pl.ds(pl.multiple_of((2 * PAIRS + g) * LANES, LANES), LANES)
        o_lanes = pl.ds(pl.multiple_of((1 + g) * LANES, LANES), LANES)
        kt_ref[...] = rot_ref[:, k_lanes].T
        dk_ref[...] = jnp.zeros_like(dk_ref)
        dv_ref[...] = jnp.zeros_like(dv_ref)
        for i in range(tiles):
            cols = pl.ds(i * TILE, TILE)

            def biases(here):
                bias = bias_ref[here, cols]
                return jnp.concatenate([bias, bias], axis=1)

            centre = jnp.concatenate([row_sums(cols, o_lanes, False), row_sums(cols, o_lanes, True)], axis=1)
            d_query = score_block(
                i + 1,
                2 * TILE,
                lambda here: rot_ref[here, k_lanes],
                lambda here: rot_ref[here, v_lanes],
                two_heads(rot_ref[cols, q_lanes]),
                two_heads(d_ref[cols, o_lanes]),
                biases,
                lse_ref[g, pl.ds(0, 1), pl.ds(i * 2 * TILE, 2 * TILE)],
                centre[0:1],
            )
            out = jnp.concatenate([d_query[:HEAD_DIM, :TILE], d_query[HEAD_DIM:, TILE:]], axis=0)
            dq_ref[cols, :] = out.T
        place(lambda here: dq_ref[here, :], q_lanes, True)
        place(lambda here: dk_ref[here, :], k_lanes, True)
        place(lambda here: dv_ref[here, :], v_lanes, False)
        return carry

    lax.fori_loop(0, PAIRS, pair, 0)
    k_lanes, v_lanes = pl.ds(6 * LANES, LANES), pl.ds(7 * LANES, LANES)
    kt_ref[...] = rot_ref[:, k_lanes].T
    dk_ref[...] = jnp.zeros_like(dk_ref)
    dv_ref[...] = jnp.zeros_like(dv_ref)
    dq_ref[...] = jnp.zeros_like(dq_ref)
    for j in range((tiles + 1) // 2):
        which = 2 * j + info[8]

        @pl.when(which < tiles)
        def _():
            cols = pl.ds(pl.multiple_of(which * TILE, TILE), TILE)
            queries = pltpu.roll(rot_ref[cols, k_lanes].astype(f32), HEAD_DIM, 1)
            queries = jnp.where(lane_mask(TILE, True), queries, 0.0).astype(bf16)
            d_rows = pltpu.roll(d_ref[cols, pl.ds(0, LANES)].astype(f32), HEAD_DIM, 1)
            d_rows = jnp.where(lane_mask(TILE, False), d_rows, 0.0).astype(bf16)
            d_query = score_block(
                min(2 * j + 2, tiles),
                TILE,
                lambda here: rot_ref[here, k_lanes],
                lambda here: rot_ref[here, v_lanes],
                queries,
                d_rows,
                lambda here: bias_ref[here, cols],
                lse_ref[PAIRS, pl.ds(0, 1), pl.ds(j * TILE, TILE)],
                row_sums(cols, pl.ds(0, LANES), True)[0:1],
            )
            out = jnp.concatenate([d_query[HEAD_DIM:], jnp.zeros((HEAD_DIM, TILE), f32)], axis=0)
            dq_ref[cols, :] = out.T

    place(lambda here: dq_ref[here, :] + dk_ref[here, :], k_lanes, True)
    place(lambda here: dv_ref[here, :], v_lanes, False)


FREE = pl.CostEstimate(flops=0, bytes_accessed=1024, transcendentals=0)
SMEM_SPEC = pl.BlockSpec(memory_space=pltpu.SMEM)
VMEM_SPEC = pl.BlockSpec(memory_space=pltpu.VMEM)


def attention_forward(info, qkv, cosine, sine, bias):
    slot = qkv.shape[0]
    pieces = slot // TILE
    return pl.pallas_call(
        forward_kernel,
        out_shape=(
            jax.ShapeDtypeStruct((slot, 8 * LANES), bf16),
            jax.ShapeDtypeStruct((slot, 3 * LANES), bf16),
            jax.ShapeDtypeStruct((PAIRS + 1, 8, pieces * 2 * TILE), f32),
        ),
        in_specs=[SMEM_SPEC] + [VMEM_SPEC] * 4,
        out_specs=(VMEM_SPEC,) * 3,
        scratch_shapes=[
            pltpu.VMEM((slot, 2 * TILE), f32),
            pltpu.VMEM((slot, 2 * TILE), bf16),
            pltpu.VMEM((LANES, slot), bf16),
            pltpu.VMEM((slot, 3 * LANES), bf16),
        ],
        compiler_params=pltpu.CompilerParams(vmem_limit_bytes=48 << 20),
        cost_estimate=pl.CostEstimate(flops=0, bytes_accessed=1024, transcendentals=0),
        name="attention_forward",
    )(info, qkv, cosine, sine, bias)


def attention_backward(info, rotated, cosine, sine, bias, mixed, near, far, log_total):
    slot = rotated.shape[0]
    return pl.pallas_call(
        backward_kernel,
        out_shape=jax.ShapeDtypeStruct((slot, 8 * LANES), bf16),
        in_specs=[SMEM_SPEC] + [VMEM_SPEC] * 8,
        out_specs=VMEM_SPEC,
        scratch_shapes=[
            pltpu.VMEM((slot, 3 * LANES), bf16),
            pltpu.VMEM((slot, 3 * LANES), f32),
            pltpu.VMEM((slot, 2 * TILE), bf16),
            pltpu.VMEM((LANES, slot), bf16),
            pltpu.VMEM((slot, LANES), f32),
            pltpu.VMEM((slot, LANES), f32),
            pltpu.VMEM((slot, LANES), f32),
        ],
        compiler_params=pltpu.CompilerParams(vmem_limit_bytes=48 << 20),
        cost_estimate=pl.CostEstimate(flops=0, bytes_accessed=1024, transcendentals=0),
        name="attention_backward",
    )(info, rotated, cosine, sine, bias, mixed, near, far, log_total)


def pack_kernel(info, q_ref, k_ref, v_ref, o_ref, mine_ref, theirs_ref):
    count, cols = q_ref.shape
    own = cols // (2 * HEAD_DIM) * HEAD_DIM
    fields = [q_ref[...], k_ref[...], v_ref[...], o_ref[...].astype(f32).T.astype(bf16)]
    lower = info[8] == 0
    for n, field in enumerate(fields):
        lanes = pl.ds((n if n < 3 else 3 + 1) * own, own)
        first, second = field[:, :own], field[:, own : 2 * own]
        mine_ref[:, lanes] = jnp.where(lower, first, second)
        theirs_ref[:, lanes] = jnp.where(lower, second, first)
    for n in range(2):
        left, right = fields[2 * n][:, 2 * own :], fields[2 * n + 1][:, 2 * own :]
        shared = jnp.concatenate([left.astype(f32), right.astype(f32)], axis=1).astype(bf16)
        lanes = pl.ds(3 * own + n * LANES, LANES)
        mine_ref[:, lanes] = shared
        theirs_ref[:, lanes] = shared


def pack_heads(info, w_query, w_key, w_value, w_out):
    count, cols = w_query.shape
    shape = jax.ShapeDtypeStruct((count, 10 * LANES), bf16)
    return pl.pallas_call(
        pack_kernel,
        out_shape=(shape, shape),
        in_specs=[SMEM_SPEC] + [VMEM_SPEC] * 4,
        out_specs=(VMEM_SPEC, VMEM_SPEC),
        compiler_params=pltpu.CompilerParams(vmem_limit_bytes=24 << 20),
        cost_estimate=FREE,
        name="pack_heads",
    )(info, w_query, w_key, w_value, w_out)


def whole(shape):
    return pl.BlockSpec(shape, lambda i: (0,) * len(shape), pipeline_mode=pl.Buffered(1))


ROOMY = pltpu.CompilerParams(vmem_limit_bytes=52 << 20)


def tail_lanes(shape, at, size):
    lane = lax.broadcasted_iota(jnp.int32, shape, 1)
    return (lane >= at) & (lane < at + size)


def tail_parts(tail, size):
    return pltpu.roll(tail, 2 * size, 1), pltpu.roll(tail, size, 1)


def gate_kernel(size, first_ref, second_ref, w_ref, *refs):
    gate_up_ref, main_ref, tail_ref = refs[-3:]
    width = main_ref.shape[1]

    def project(rows):
        gate_up = dot(rows, w_ref[...])
        gate_up_ref[...] = gate_up
        gate, up = gate_up[:, :width], gate_up[:, width : 2 * width]
        main_ref[...] = (gate * jax.nn.sigmoid(gate) * up).astype(bf16)
        gate, up = tail_parts(gate_up[:, 2 * width :], size)
        tail = gate * jax.nn.sigmoid(gate) * up
        tail_ref[...] = jnp.where(tail_lanes(tail.shape, 2 * size, size), tail, 0.0).astype(bf16)

    pl.when(pl.program_id(0) == 0)(lambda: project(first_ref[...]))
    pl.when(pl.program_id(0) == 1)(lambda: project(second_ref[...]))


def gate_blocks(blocks, places, gu_w, width, size, earlier):
    count, depth = blocks[0].shape
    cols = gu_w.shape[1]
    at, step = places[0], places[1] - places[0]
    widths = (cols, width, cols - 2 * width)
    return pl.pallas_call(
        functools.partial(gate_kernel, size),
        grid=(2,),
        out_shape=tuple(
            jax.ShapeDtypeStruct((8 * count, w), kind) for w, kind in zip(widths, (f32, bf16, bf16))
        ),
        in_specs=[whole((count, depth))] * 2
        + [whole((depth, cols))]
        + [pl.BlockSpec(memory_space=pl.ANY)] * len(earlier),
        out_specs=tuple(pl.BlockSpec((count, w), lambda i: (at + step * i, 0)) for w in widths),
        input_output_aliases={3: 0, 4: 1, 5: 2} if earlier else {},
        compiler_params=ROOMY,
        cost_estimate=pl.CostEstimate(flops=8 * count * depth * cols, bytes_accessed=1024, transcendentals=0),
        name="gate_blocks",
    )(*blocks, gu_w, *earlier)


def gate_back(d_hidden, gate, up):
    sigmoid_gate = jax.nn.sigmoid(gate)
    d_gate = d_hidden * up * sigmoid_gate * (1.0 + gate * (1.0 - sigmoid_gate))
    return d_gate, d_hidden * (gate * sigmoid_gate)


def hidden_back_kernel(size, rows_ref, w_ref, tail_w_ref, gate_up_ref, out_ref):
    width = w_ref.shape[1]
    rows = rows_ref[...]
    d_gate, d_up = gate_back(
        dot(rows, w_ref[...]), gate_up_ref[:, :width], gate_up_ref[:, width : 2 * width]
    )
    out_ref[:, :width] = d_gate.astype(bf16)
    out_ref[:, width : 2 * width] = d_up.astype(bf16)
    gate, up = tail_parts(gate_up_ref[:, 2 * width :], size)
    d_gate, d_up = gate_back(dot(rows, tail_w_ref[...]), gate, up)
    lanes = d_gate.shape[1]
    d_gate = pltpu.roll(d_gate, lanes - 2 * size, 1)
    d_up = pltpu.roll(d_up, lanes - size, 1)
    tail = jnp.where(tail_lanes(d_up.shape, size, size), d_up, 0.0)
    tail = jnp.where(tail_lanes(d_up.shape, 0, size), d_gate, tail)
    out_ref[:, 2 * width :] = tail.astype(bf16)


def hidden_back(rows, down_w, gu_w, gate_up, size):
    count, depth = rows.shape
    width, cols = down_w.shape[1], gate_up.shape[1]
    tail = cols - 2 * width
    tile = count // 2
    return pl.pallas_call(
        functools.partial(hidden_back_kernel, size),
        grid=(2,),
        out_shape=jax.ShapeDtypeStruct((count, cols), bf16),
        in_specs=[
            pl.BlockSpec((tile, depth), lambda i: (i, 0)),
            whole((depth, width)),
            pl.BlockSpec((depth, tail), lambda i: (0, 2 * width // tail), pipeline_mode=pl.Buffered(1)),
            pl.BlockSpec((tile, cols), lambda i: (i, 0)),
        ],
        out_specs=pl.BlockSpec((tile, cols), lambda i: (i, 0)),
        compiler_params=ROOMY,
        cost_estimate=FREE,
        name="hidden_back",
    )(rows, down_w, gu_w, gate_up)


def rows_kernel(rows_ref, w_ref, *refs):
    refs[-1][...] = dot(rows_ref[...], w_ref[...])


def project_half(rows, weight, cols, earlier):
    count, depth = rows.shape
    tile = count // 4
    at = 0 if earlier is None else 4
    earlier = () if earlier is None else (earlier,)
    return pl.pallas_call(
        rows_kernel,
        grid=(4,),
        out_shape=jax.ShapeDtypeStruct((2 * count, cols), f32),
        in_specs=[
            pl.BlockSpec((tile, depth), lambda i: (i, 0)),
            pl.BlockSpec((depth, cols), lambda i: (0, 0), pipeline_mode=pl.Buffered(1)),
        ]
        + [pl.BlockSpec(memory_space=pl.ANY)] * len(earlier),
        out_specs=pl.BlockSpec((tile, cols), lambda i: (i + at, 0)),
        input_output_aliases={2: 0} if earlier else {},
        compiler_params=ROOMY,
        cost_estimate=FREE,
        name="project_half",
    )(rows, weight, *earlier)


def grads_kernel(place, counts, *refs):
    out_ref = refs[-1]
    products, at = [], 0
    for count in counts:
        left = jnp.concatenate([ref[...] for ref in refs[at : at + count]], axis=0)
        products.append(dot(left, refs[at + count][...], TN))
        at += count + 1
    place(out_ref, *products)


def place_one(out_ref, product):
    out_ref[...] = product.astype(bf16)


def place_tail(out_ref, first, second):
    start = first.shape[1] - second.shape[1]
    out_ref[:, :start] = first[:, :start].astype(bf16)
    out_ref[:, start:] = (first[:, start:] + second).astype(bf16)


def place_heads(out_ref, first, second):
    start = first.shape[1] - LANES
    out_ref[:, :start] = first[:, :start].astype(bf16)
    out_ref[:, start : start + LANES] = (first[:, start:] + second[:, :LANES]).astype(bf16)
    out_ref[:, start + LANES :] = second[:, LANES:].astype(bf16)


def weight_grads(place, cols, tile, *products):
    depth = products[0][0][0].shape[1]
    specs, operands = [], []
    for pieces, right in products:
        specs += [pl.BlockSpec((piece.shape[0], tile), lambda i: (0, i)) for piece in pieces]
        specs += [whole(right.shape)]
        operands += [*pieces, right]
    counts = [len(pieces) for pieces, _ in products]
    return pl.pallas_call(
        functools.partial(grads_kernel, place, counts),
        grid=(depth // tile,),
        out_shape=jax.ShapeDtypeStruct((depth, cols), bf16),
        in_specs=specs,
        out_specs=pl.BlockSpec((tile, cols), lambda i: (i, 0)),
        compiler_params=ROOMY,
        cost_estimate=FREE,
        name="weight_grads",
    )(*operands)


def shards(
    tokens,
    w_query,
    w_key,
    w_value,
    w_out,
    gain_attn,
    w_gate,
    w_up,
    w_down,
    gain_mlp,
    cotangent,
    lineage,
    padding,
    positions,
):
    slot = lineage.shape[1]
    on_x, on_mp = lax.axis_index("ctx"), lax.axis_index("mp")
    on_y, on_core = on_mp // 2, on_mp % 2
    lower_x = on_x == 0
    heads = w_query.shape[1] // HEAD_DIM
    own_cols = heads // 2 * HEAD_DIM
    ff_half = w_gate.shape[1] // 2
    ff_main = ff_half // LANES * LANES
    ff_tail = ff_half - ff_main

    info, back = [], []
    for n in range(8):
        d_x, d_y, d_core = on_x ^ (n // 4), on_y ^ (n // 2 % 2), on_core ^ (n % 2)
        info.append(d_core * 4 + d_x * 2 + d_y)
        from_x, from_y, from_core = on_x ^ (n // 2 % 2), on_y ^ (n % 2), on_core ^ (n // 4)
        back.append(from_x * 4 + from_y * 2 + from_core)
    info = jnp.stack(info + [on_x] + back).astype(jnp.int32)

    gain_a = gain_attn.astype(f32)
    gain_m = gain_mlp.astype(f32)
    inputs = tokens.astype(f32)
    grad_rows = cotangent.astype(f32)

    def both_x(mine, theirs):
        got = flip_x(theirs)
        return jnp.where(lower_x, jnp.concatenate([mine, got], 0), jnp.concatenate([got, mine], 0))

    attn_mine, attn_theirs = pack_heads(info, w_query, w_key, w_value, w_out)

    def halves(weight):
        first, second = weight[:, :ff_half], weight[:, ff_half:]
        return jnp.where(lower_x, first, second), jnp.where(lower_x, second, first)

    def pack_hidden(gate, up, down):
        fill = jnp.zeros((gate.shape[0], 2 * LANES - 3 * ff_tail), bf16)
        tails = [w[:, ff_main:] for w in (gate, up, down)]
        return jnp.concatenate([gate[:, :ff_main], up[:, :ff_main]] + tails + [fill], axis=1)

    index = jnp.arange(slot, dtype=jnp.int32)
    own_seg = lineage[0]
    related = (
        (own_seg[:, None] == lineage[0][None, :])
        | (own_seg[:, None] == lineage[1][None, :])
        | (own_seg[:, None] == lineage[2][None, :])
    )
    live = padding == 0
    allowed = (index[:, None] == index[None, :]) | (
        related & live[:, None] & live[None, :] & (index[:, None] < index[None, :])
    )
    bias = jnp.where(allowed, 0.0, masked_value).astype(f32)
    half_dim = HEAD_DIM // 2
    inv_freq = rope_base ** (-2.0 * jnp.arange(half_dim, dtype=f32) / HEAD_DIM)
    angles = positions.astype(f32)[:, None] * inv_freq[None, :]
    cos, sin = jnp.cos(angles), jnp.sin(angles)
    cosine = jnp.concatenate([cos, cos, cos, cos], axis=1)
    sine = jnp.concatenate([-sin, sin, -sin, sin], axis=1)

    def rows_of_x(field):
        rows = field.shape[0] // 2
        mine = jnp.where(lower_x, field[:rows], field[rows:])
        return mine, flip_x(jnp.where(lower_x, field[rows:], field[:rows]))

    attn_got = flip_x(attn_theirs)
    count, on_dp = lax.axis_size("dp"), lax.axis_index("dp")

    def from_dp(field, k):
        return lax.ppermute(field, "dp", [(i, i ^ k) for i in range(count)])

    arrived = [from_dp(attn_mine, k) for k in range(1, count)]
    _, own_rows = after(attn_got, (normalize(inputs) * gain_a).astype(bf16))
    near_a, arrived[:2] = gather_near(own_rows, arrived[:2])
    near_a, arrived[2:], w_gate, w_up, w_down = after(near_a, arrived[2:], w_gate, w_up, w_down)
    gate_mine, gate_theirs = halves(w_gate)
    up_mine, up_theirs = halves(w_up)
    down_mine, down_theirs = halves(w_down.T)
    gu_part = both_x(
        pack_hidden(gate_mine, up_mine, down_mine), pack_hidden(gate_theirs, up_theirs, down_theirs)
    )
    block = (1, 1) + attn_mine.shape
    attn_w = jnp.zeros((count, 2) + attn_mine.shape, bf16)
    for k, field in enumerate([attn_mine] + arrived):
        attn_w = lax.dynamic_update_slice(attn_w, field.reshape(block), (on_dp ^ k, on_x, 0, 0))
    attn_all = lax.all_gather(attn_got, "dp", axis=0, tiled=False)
    near_a, gu_part, attn_all, attn_w, bias, cosine, sine = after(
        near_a, gu_part, attn_all, attn_w, bias, cosine, sine
    )
    far_a = flip_core(near_a)
    attn_w = lax.dynamic_update_slice(attn_w, attn_all[:, None], (0, 1 - on_x, 0, 0))
    attn_w = attn_w.reshape(count * 2 * attn_mine.shape[0], attn_mine.shape[1])
    gu_w = lax.all_gather(gu_part, "dp", axis=0, tiled=True)
    qkv_w = attn_w[:, : 8 * LANES]
    out_w = attn_w[:, 7 * LANES :]
    qkv = project_half(far_a, attn_w, 8 * LANES, project_half(near_a, attn_w, 8 * LANES, None))
    qkv, down_mine, down_theirs, grad_rows = after(
        qkv, down_mine[:, :ff_main], down_theirs[:, :ff_main], grad_rows
    )
    near_d, far_d = gather_rows((branch_scale * grad_rows).astype(bf16))
    d_mlp = jnp.concatenate([near_d, far_d], axis=0)
    down_part = both_x(down_mine, down_theirs)
    rotated, mixed, log_total = attention_forward(info, qkv, cosine, sine, bias)
    residual = inputs + branch_scale * sum_rows(mixed, out_w, NT, pieces=4)
    own_m, gu_w, d_mlp = after((normalize(residual) * gain_m).astype(bf16), gu_w, d_mlp)
    down_w = lax.all_gather(down_part, "dp", axis=0, tiled=True)
    half = own_m.shape[0] // 2
    from_x, from_y, own_c = flip_x(own_m), flip_y(own_m), flip_core(own_m)
    gates = gate_blocks((own_m, own_c), (0, 4), gu_w, ff_main, ff_tail, ())
    from_x, from_y, gates = after(from_x, from_y, gates)
    corner = jnp.concatenate([flip_y(from_x[:half]), flip_x(from_y[half:])], axis=0)
    y_c, x_c = flip_core(from_y), flip_core(from_x)
    gates = gate_blocks((from_y, from_x), (1, 2), gu_w, ff_main, ff_tail, gates)
    corner, gates = after(corner, gates)
    corner_c = flip_core(corner)
    gates = gate_blocks((y_c, x_c), (5, 6), gu_w, ff_main, ff_tail, gates)
    gates = gate_blocks((corner, corner_c), (3, 7), gu_w, ff_main, ff_tail, gates)
    gate_up, hidden, hidden_tail = gates
    all_m = (own_m, from_y, from_x, corner, own_c, y_c, x_c, corner_c)

    grad_down = weight_grads(place_one, ff_main, 6 * LANES, ((near_d, far_d), hidden))
    gate_up, grad_down = after(gate_up, grad_down)
    grad_down = lax.psum_scatter(grad_down, "dp", scatter_dimension=0, tiled=True)
    d_gate_up = hidden_back(d_mlp, down_w, gu_w, gate_up, ff_tail)
    grad_gu = weight_grads(
        place_tail,
        gate_up.shape[1],
        3 * LANES,
        (all_m, d_gate_up),
        ((near_d, far_d), hidden_tail),
    )
    d_gate_up, grad_gu = after(d_gate_up, grad_gu)
    grad_gu = lax.psum_scatter(grad_gu, "dp", scatter_dimension=0, tiled=True)
    d_normed_mlp, grad_down = sum_rows(d_gate_up, gu_w, NT, grad_down)
    back_mlp, gain_mlp_part = norm_back(residual, gain_m, d_normed_mlp)
    d_residual = grad_rows + back_mlp

    near_o, far_o = gather_rows((branch_scale * d_residual).astype(bf16))
    d_mixed_near, d_mixed_far = dot(near_o, out_w).astype(bf16), dot(far_o, out_w).astype(bf16)
    d_qkv = attention_backward(
        info, rotated, cosine, sine, bias, mixed, d_mixed_near, d_mixed_far, log_total
    )
    grad_attn = weight_grads(
        place_heads, 10 * LANES, 3 * LANES, ((near_a, far_a), d_qkv), ((near_o, far_o), mixed)
    )
    grad_attn, grad_gu, d_qkv, hidden = after(grad_attn, grad_gu, d_qkv, hidden)
    grad_attn = lax.psum_scatter(grad_attn, "dp", scatter_dimension=0, tiled=True)
    tail_mine, tail_got = rows_of_x(grad_gu[:, 2 * ff_main :])
    tail_got, d_qkv, hidden = after(tail_got, d_qkv, hidden)
    gu_mine, gu_got = rows_of_x(grad_gu[:, : 2 * ff_main])
    d_normed_attn = sum_rows(d_qkv, qkv_w, NT, pieces=4)
    back_attn, gain_attn_part = norm_back(inputs, gain_a, d_normed_attn)
    input_grad = d_residual + back_attn
    gains, grad_attn = sum_all(jnp.stack([gain_attn_part, gain_mlp_part]), grad_attn)
    hidden = jnp.concatenate([hidden, hidden_tail], axis=1)
    down_w = jnp.concatenate([down_w, gu_w[:, 2 * ff_main :]], axis=1)
    output = residual + branch_scale * sum_rows(hidden, down_w, NT, pieces=4)

    def join(mine, got):
        mine, got = mine.astype(f32), got.astype(f32)
        return jnp.where(lower_x, jnp.concatenate([mine, got], 1), jnp.concatenate([got, mine], 1))

    def join_heads(mine, got, at, shared_at):
        whole = join(mine[:, at : at + own_cols], got[:, at : at + own_cols])
        last = slice(shared_at, shared_at + HEAD_DIM)
        return jnp.concatenate([whole, mine[:, last].astype(f32) + got[:, last].astype(f32)], axis=1)

    down_mine, down_got = rows_of_x(grad_down)

    def join_hidden(mine, got, at):
        last = slice(at * ff_tail, (at + 1) * ff_tail)
        mine = jnp.concatenate([mine, tail_mine[:, last]], axis=1)
        return join(mine, jnp.concatenate([got, tail_got[:, last]], axis=1))

    grad_gate = join_hidden(gu_mine[:, :ff_main], gu_got[:, :ff_main], 0)
    up_lanes = slice(ff_main, 2 * ff_main)
    grad_up = join_hidden(gu_mine[:, up_lanes], gu_got[:, up_lanes], 1)
    grad_down = join_hidden(down_mine, down_got, 2).T
    mine, got = rows_of_x(grad_attn)
    grad_query = join_heads(mine, got, 0, 6 * LANES)
    grad_key = join_heads(mine, got, 2 * LANES, 6 * LANES + HEAD_DIM)
    grad_value = join_heads(mine, got, 4 * LANES, 7 * LANES)
    grad_out = join_heads(mine, got, 8 * LANES, 7 * LANES + HEAD_DIM).T

    return (
        output.astype(bf16),
        input_grad.astype(bf16),
        grad_query,
        grad_key,
        grad_value,
        grad_out,
        gains[0],
        grad_gate,
        grad_up,
        grad_down,
        gains[1],
    )


def solution(mesh):
    placed = (
        P(("dp", "ctx", "mp"), None),
        P(("dp", "ctx"), "mp"),
        P(("dp", "ctx"), "mp"),
        P(("dp", "ctx"), "mp"),
        P("mp", ("dp", "ctx")),
        P(),
        P(("dp", "ctx"), "mp"),
        P(("dp", "ctx"), "mp"),
        P("mp", ("dp", "ctx")),
        P(),
        P(("dp", "ctx", "mp"), None),
        P(None, "dp"),
        P("dp"),
        P("dp"),
    )
    return jax.shard_map(
        shards,
        mesh=mesh,
        in_specs=placed,
        out_specs=(
            P(("dp", "ctx", "mp"), None),
            P(("dp", "ctx", "mp"), None),
            P(("dp", "ctx"), "mp"),
            P(("dp", "ctx"), "mp"),
            P(("dp", "ctx"), "mp"),
            P("mp", ("dp", "ctx")),
            P(),
            P(("dp", "ctx"), "mp"),
            P(("dp", "ctx"), "mp"),
            P("mp", ("dp", "ctx")),
            P(),
        ),
        check_vma=False,
    )
```

```python
import functools
import math

import jax
import jax.numpy as jnp
from jax import lax
from jax.experimental import pallas as pl
from jax.experimental.pallas import tpu as pltpu
from jax.sharding import PartitionSpec as P

HEAD_DIM = 64
LANES = 128
PAIRS = 2
TILE = 128

eps = 1e-05
branch_scale = 1.4 / math.sqrt(40.0)
rope_base = 10000.0
masked_value = -1e30

f32 = jnp.float32
bf16 = jnp.bfloat16

NN = (((1,), (0,)), ((), ()))
NT = (((1,), (1,)), ((), ()))
TN = (((0,), (0,)), ((), ()))


def dot(left, right, dims=NN):
    return lax.dot_general(left, right, dims, preferred_element_type=f32)


def after(*fields):
    return lax.optimization_barrier(fields)


def normalize(field):
    return field * lax.rsqrt(jnp.mean(field * field, axis=-1, keepdims=True) + eps)


def norm_back(field, gain_f32, incoming):
    inverse = lax.rsqrt(jnp.mean(field * field, axis=-1, keepdims=True) + eps)
    scaled = gain_f32 * incoming
    along = jnp.mean(field * scaled, axis=-1, keepdims=True)
    return (
        inverse * scaled - field * inverse**3 * along,
        jnp.sum(incoming * field * inverse, axis=0),
    )


def flip_x(field):
    return lax.ppermute(field, "ctx", [(0, 1), (1, 0)])


def flip_y(field):
    return lax.ppermute(field, "mp", [(0, 2), (2, 0), (1, 3), (3, 1)])


def flip_core(field, pieces=1):
    if pieces > 1:
        size = field.shape[0] // pieces
        parts = [flip_core(field[i * size : (i + 1) * size]) for i in range(pieces)]
        return jnp.concatenate(parts, axis=0)
    return lax.ppermute(field, "mp", [(0, 1), (1, 0), (2, 3), (3, 2)])


def gather_near(own, other=None):
    half = own.shape[0] // 2
    from_x, from_y = flip_x(own), flip_y(own)
    if other is not None:
        from_x, from_y, other = after(from_x, from_y, other)
    corner = jnp.concatenate([flip_y(from_x[:half]), flip_x(from_y[half:])], axis=0)
    near = jnp.concatenate([own, from_y, from_x, corner], axis=0)
    return near if other is None else (near, other)


def gather_rows(own):
    near = gather_near(own)
    return near, flip_core(near)


def sum_rows(left, right, dims, other=None, pieces=1):
    count = left.shape[0] // 2
    block = count // 4
    half = block // 2
    away = flip_core(dot(left[count:], right, dims).astype(bf16), pieces)
    total = dot(left[:count], right, dims) + away.astype(f32)
    total = total.reshape(2, 2, block, total.shape[-1])
    got_x = flip_x(total[1, :, :half].astype(bf16)).astype(f32)
    got_y = flip_y(total[:, 1, half:].astype(bf16)).astype(f32)
    upper = total[0, :, :half] + got_x
    lower = total[:, 0, half:] + got_y
    if other is not None:
        upper, other = after(upper, other)
    upper = upper[0] + flip_y(upper[1].astype(bf16)).astype(f32)
    lower = lower[0] + flip_x(lower[1].astype(bf16)).astype(f32)
    total = jnp.concatenate([upper, lower], axis=0)
    return total if other is None else (total, other)


def sum_all(field, other):
    total = flip_core(field) + field
    total = flip_y(total) + total
    total = flip_x(total) + total
    count, step = lax.axis_size("dp"), 1
    while step < count:
        if 2 * step >= count:
            total, other = after(total, other)
        total = lax.ppermute(total, "dp", [(i, i ^ step) for i in range(count)]) + total
        step *= 2
    return total, other


def lane_mask(rows, upper):
    lane = lax.broadcasted_iota(jnp.int32, (rows, LANES), 1)
    return lane >= HEAD_DIM if upper else lane < HEAD_DIM


def swap_halves(field):
    lane = lax.broadcasted_iota(jnp.int32, field.shape, 1)
    return jnp.where(
        lane % HEAD_DIM < HEAD_DIM // 2,
        pltpu.roll(field, LANES - HEAD_DIM // 2, 1),
        pltpu.roll(field, HEAD_DIM // 2, 1),
    )


def two_heads(block):
    zero = jnp.zeros_like(block)
    return jnp.concatenate(
        [
            jnp.where(lane_mask(block.shape[0], False), block, zero),
            jnp.where(lane_mask(block.shape[0], True), block, zero),
        ],
        axis=0,
    )


def forward_kernel(
    info, qkv_ref, cos_ref, sin_ref, bias_ref, rot_ref, mixed_ref, lse_ref, s_ref, e_ref, vt_ref, o_ref
):
    slot = qkv_ref.shape[0]
    rows = slot // 8
    tiles = slot // TILE
    for n in range(8):
        here = pl.ds(n * rows, rows)
        there = pl.ds(pl.multiple_of(info[n] * rows, 16), rows)
        cosine, sine = cos_ref[here, :], sin_ref[here, :]
        for g in (0, 1, 2, 3, 6):
            lanes = pl.ds(g * LANES, LANES)
            field = qkv_ref[there, lanes]
            field = field * cosine + swap_halves(field) * sine
            if g < 2:
                field = field * (HEAD_DIM**-0.5)
            if g == 6:
                field = jnp.where(lane_mask(rows, False), field * (HEAD_DIM**-0.5), field)
            rot_ref[here, lanes] = field.astype(bf16)
        for g in (4, 5):
            lanes = pl.ds(g * LANES, LANES)
            rot_ref[here, lanes] = qkv_ref[there, lanes].astype(bf16)
        lanes = pl.ds(7 * LANES, LANES)
        field = qkv_ref[there, lanes]
        rot_ref[here, lanes] = jnp.where(lane_mask(rows, False), field, 0.0).astype(bf16)

    def softmax_block(count, width, keys, queries, biases):
        top = jnp.full((8, width), masked_value, f32)
        for t in range(count):
            scores = dot(keys(t), queries, NT) + biases(t)
            s_ref[pl.ds(t * TILE, TILE), pl.ds(0, width)] = scores
            top = jnp.maximum(top, jnp.max(scores.reshape(TILE // 8, 8, width), axis=0))
        top = jnp.max(top, axis=0, keepdims=True)
        total = jnp.zeros((8, width), f32)
        for t in range(count):
            weights = jnp.exp(s_ref[pl.ds(t * TILE, TILE), pl.ds(0, width)] - top)
            total = total + jnp.sum(weights.reshape(TILE // 8, 8, width), axis=0)
            e_ref[pl.ds(t * TILE, TILE), pl.ds(0, width)] = weights.astype(bf16)
        total = jnp.sum(total, axis=0, keepdims=True)
        depth = count * TILE
        product = dot(vt_ref[:, pl.ds(0, depth)], e_ref[pl.ds(0, depth), pl.ds(0, width)])
        return product / total, top + jnp.log(total)

    def pair(g, carry):
        q_lanes = pl.ds(pl.multiple_of(g * LANES, LANES), LANES)
        k_lanes = pl.ds(pl.multiple_of((PAIRS + g) * LANES, LANES), LANES)
        v_lanes = pl.ds(pl.multiple_of((2 * PAIRS + g) * LANES, LANES), LANES)
        o_lanes = pl.ds(pl.multiple_of((1 + g) * LANES, LANES), LANES)
        vt_ref[...] = rot_ref[:, v_lanes].T
        for i in range(tiles):
            cols = pl.ds(i * TILE, TILE)

            def biases(t):
                bias = bias_ref[pl.ds(t * TILE, TILE), cols]
                return jnp.concatenate([bias, bias], axis=1)

            product, log_total = softmax_block(
                i + 1,
                2 * TILE,
                lambda t: rot_ref[pl.ds(t * TILE, TILE), k_lanes],
                two_heads(rot_ref[cols, q_lanes]),
                biases,
            )
            lse_ref[g, :, pl.ds(i * 2 * TILE, 2 * TILE)] = jnp.broadcast_to(log_total, (8, 2 * TILE))
            out = jnp.concatenate([product[:HEAD_DIM, :TILE], product[HEAD_DIM:, TILE:]], axis=0)
            o_ref[cols, o_lanes] = out.T.astype(bf16)
        return carry

    lax.fori_loop(0, PAIRS, pair, 0)
    o_ref[:, pl.ds(0, LANES)] = jnp.zeros((slot, LANES), bf16)
    vt_ref[...] = rot_ref[:, pl.ds(7 * LANES, LANES)].T
    for j in range((tiles + 1) // 2):
        which = 2 * j + info[8]

        @pl.when(which < tiles)
        def _():
            cols = pl.ds(pl.multiple_of(which * TILE, TILE), TILE)
            queries = pltpu.roll(rot_ref[cols, pl.ds(6 * LANES, LANES)].astype(f32), HEAD_DIM, 1)
            queries = jnp.where(lane_mask(TILE, True), queries, 0.0).astype(bf16)
            product, log_total = softmax_block(
                min(2 * j + 2, tiles),
                TILE,
                lambda t: rot_ref[pl.ds(t * TILE, TILE), pl.ds(6 * LANES, LANES)],
                queries,
                lambda t: bias_ref[pl.ds(t * TILE, TILE), cols],
            )
            lse_ref[PAIRS, :, pl.ds(j * TILE, TILE)] = jnp.broadcast_to(log_total, (8, TILE))
            out = jnp.concatenate([jnp.zeros((HEAD_DIM, TILE), f32), product[:HEAD_DIM]], axis=0)
            o_ref[cols, pl.ds(0, LANES)] = out.T.astype(bf16)

    for n in range(8):
        there = pl.ds(pl.multiple_of(info[n] * rows, 16), rows)
        mixed_ref[there, :] = o_ref[pl.ds(n * rows, rows), :]


def backward_kernel(
    info, rot_ref, cos_ref, sin_ref, bias_ref, mixed_ref, near_ref, far_ref, lse_ref, out_ref,
    d_ref, p_ref, ds_ref, kt_ref, dk_ref, dv_ref, dq_ref,
):
    slot = rot_ref.shape[0]
    rows = slot // 8
    tiles = slot // TILE
    for r in range(8):
        here = pl.ds(r * rows, rows)
        there = pl.ds(pl.multiple_of(info[9 + r] * rows, 16), rows)
        d_rows = (near_ref if r < 4 else far_ref)[pl.ds(r % 4 * rows, rows), :]
        d_ref[there, :] = d_rows
        p_ref[there, :] = d_rows.astype(f32) * mixed_ref[here, :].astype(f32)

    def row_sums(cols, lanes, upper):
        product = p_ref[cols, lanes]
        high = product.astype(bf16)
        low = (product - high.astype(f32)).astype(bf16)
        ones = jnp.where(lane_mask(8, upper), 1.0, 0.0).astype(bf16)
        return dot(ones, high, NT) + dot(ones, low, NT)

    def score_block(count, width, keys, values, queries, d_rows, biases, lse, centre):
        here = pl.ds(0, count * TILE)
        probs = jnp.exp(dot(keys(here), queries, NT) + biases(here) - lse)
        d_probs = dot(values(here), d_rows, NT)
        d_scores = (probs * (d_probs - centre)).astype(bf16)
        ds_ref[here, pl.ds(0, width)] = d_scores
        dk_ref[here, :] += dot(d_scores, queries)
        dv_ref[here, :] += dot(probs.astype(bf16), d_rows)
        return dot(kt_ref[:, here], ds_ref[here, pl.ds(0, width)]) * (HEAD_DIM**-0.5)

    def place(field_of, lanes, turned):
        for n in range(8):
            here = pl.ds(n * rows, rows)
            there = pl.ds(pl.multiple_of(info[n] * rows, 16), rows)
            field = field_of(here)
            if turned:
                field = field * cos_ref[here, :] - swap_halves(field) * sin_ref[here, :]
            out_ref[there, lanes] = field.astype(bf16)

    def pair(g, carry):
        q_lanes = pl.ds(pl.multiple_of(g * LANES, LANES), LANES)
        k_lanes = pl.ds(pl.multiple_of((PAIRS + g) * LANES, LANES), LANES)
        v_lanes = pl.ds(pl.multiple_of((2 * PAIRS + g) * LANES, LANES), LANES)
        o_lanes = pl.ds(pl.multiple_of((1 + g) * LANES, LANES), LANES)
        kt_ref[...] = rot_ref[:, k_lanes].T
        dk_ref[...] = jnp.zeros_like(dk_ref)
        dv_ref[...] = jnp.zeros_like(dv_ref)
        for i in range(tiles):
            cols = pl.ds(i * TILE, TILE)

            def biases(here):
                bias = bias_ref[here, cols]
                return jnp.concatenate([bias, bias], axis=1)

            centre = jnp.concatenate([row_sums(cols, o_lanes, False), row_sums(cols, o_lanes, True)], axis=1)
            d_query = score_block(
                i + 1,
                2 * TILE,
                lambda here: rot_ref[here, k_lanes],
                lambda here: rot_ref[here, v_lanes],
                two_heads(rot_ref[cols, q_lanes]),
                two_heads(d_ref[cols, o_lanes]),
                biases,
                lse_ref[g, pl.ds(0, 1), pl.ds(i * 2 * TILE, 2 * TILE)],
                centre[0:1],
            )
            out = jnp.concatenate([d_query[:HEAD_DIM, :TILE], d_query[HEAD_DIM:, TILE:]], axis=0)
            dq_ref[cols, :] = out.T
        place(lambda here: dq_ref[here, :], q_lanes, True)
        place(lambda here: dk_ref[here, :], k_lanes, True)
        place(lambda here: dv_ref[here, :], v_lanes, False)
        return carry

    lax.fori_loop(0, PAIRS, pair, 0)
    k_lanes, v_lanes = pl.ds(6 * LANES, LANES), pl.ds(7 * LANES, LANES)
    kt_ref[...] = rot_ref[:, k_lanes].T
    dk_ref[...] = jnp.zeros_like(dk_ref)
    dv_ref[...] = jnp.zeros_like(dv_ref)
    dq_ref[...] = jnp.zeros_like(dq_ref)
    for j in range((tiles + 1) // 2):
        which = 2 * j + info[8]

        @pl.when(which < tiles)
        def _():
            cols = pl.ds(pl.multiple_of(which * TILE, TILE), TILE)
            queries = pltpu.roll(rot_ref[cols, k_lanes].astype(f32), HEAD_DIM, 1)
            queries = jnp.where(lane_mask(TILE, True), queries, 0.0).astype(bf16)
            d_rows = pltpu.roll(d_ref[cols, pl.ds(0, LANES)].astype(f32), HEAD_DIM, 1)
            d_rows = jnp.where(lane_mask(TILE, False), d_rows, 0.0).astype(bf16)
            d_query = score_block(
                min(2 * j + 2, tiles),
                TILE,
                lambda here: rot_ref[here, k_lanes],
                lambda here: rot_ref[here, v_lanes],
                queries,
                d_rows,
                lambda here: bias_ref[here, cols],
                lse_ref[PAIRS, pl.ds(0, 1), pl.ds(j * TILE, TILE)],
                row_sums(cols, pl.ds(0, LANES), True)[0:1],
            )
            out = jnp.concatenate([d_query[HEAD_DIM:], jnp.zeros((HEAD_DIM, TILE), f32)], axis=0)
            dq_ref[cols, :] = out.T

    place(lambda here: dq_ref[here, :] + dk_ref[here, :], k_lanes, True)
    place(lambda here: dv_ref[here, :], v_lanes, False)


FREE = pl.CostEstimate(flops=0, bytes_accessed=1024, transcendentals=0)
SMEM_SPEC = pl.BlockSpec(memory_space=pltpu.SMEM)
VMEM_SPEC = pl.BlockSpec(memory_space=pltpu.VMEM)


def attention_forward(info, qkv, cosine, sine, bias):
    slot = qkv.shape[0]
    pieces = slot // TILE
    return pl.pallas_call(
        forward_kernel,
        out_shape=(
            jax.ShapeDtypeStruct((slot, 8 * LANES), bf16),
            jax.ShapeDtypeStruct((slot, 3 * LANES), bf16),
            jax.ShapeDtypeStruct((PAIRS + 1, 8, pieces * 2 * TILE), f32),
        ),
        in_specs=[SMEM_SPEC] + [VMEM_SPEC] * 4,
        out_specs=(VMEM_SPEC,) * 3,
        scratch_shapes=[
            pltpu.VMEM((slot, 2 * TILE), f32),
            pltpu.VMEM((slot, 2 * TILE), bf16),
            pltpu.VMEM((LANES, slot), bf16),
            pltpu.VMEM((slot, 3 * LANES), bf16),
        ],
        compiler_params=pltpu.CompilerParams(vmem_limit_bytes=48 << 20),
        cost_estimate=pl.CostEstimate(flops=0, bytes_accessed=1024, transcendentals=0),
        name="attention_forward",
    )(info, qkv, cosine, sine, bias)


def attention_backward(info, rotated, cosine, sine, bias, mixed, near, far, log_total):
    slot = rotated.shape[0]
    return pl.pallas_call(
        backward_kernel,
        out_shape=jax.ShapeDtypeStruct((slot, 8 * LANES), bf16),
        in_specs=[SMEM_SPEC] + [VMEM_SPEC] * 8,
        out_specs=VMEM_SPEC,
        scratch_shapes=[
            pltpu.VMEM((slot, 3 * LANES), bf16),
            pltpu.VMEM((slot, 3 * LANES), f32),
            pltpu.VMEM((slot, 2 * TILE), bf16),
            pltpu.VMEM((LANES, slot), bf16),
            pltpu.VMEM((slot, LANES), f32),
            pltpu.VMEM((slot, LANES), f32),
            pltpu.VMEM((slot, LANES), f32),
        ],
        compiler_params=pltpu.CompilerParams(vmem_limit_bytes=48 << 20),
        cost_estimate=pl.CostEstimate(flops=0, bytes_accessed=1024, transcendentals=0),
        name="attention_backward",
    )(info, rotated, cosine, sine, bias, mixed, near, far, log_total)


def pack_kernel(info, q_ref, k_ref, v_ref, o_ref, mine_ref, theirs_ref):
    count, cols = q_ref.shape
    own = cols // (2 * HEAD_DIM) * HEAD_DIM
    fields = [q_ref[...], k_ref[...], v_ref[...], o_ref[...].astype(f32).T.astype(bf16)]
    lower = info[8] == 0
    for n, field in enumerate(fields):
        lanes = pl.ds((n if n < 3 else 3 + 1) * own, own)
        first, second = field[:, :own], field[:, own : 2 * own]
        mine_ref[:, lanes] = jnp.where(lower, first, second)
        theirs_ref[:, lanes] = jnp.where(lower, second, first)
    for n in range(2):
        left, right = fields[2 * n][:, 2 * own :], fields[2 * n + 1][:, 2 * own :]
        shared = jnp.concatenate([left.astype(f32), right.astype(f32)], axis=1).astype(bf16)
        lanes = pl.ds(3 * own + n * LANES, LANES)
        mine_ref[:, lanes] = shared
        theirs_ref[:, lanes] = shared


def pack_heads(info, w_query, w_key, w_value, w_out):
    count, cols = w_query.shape
    shape = jax.ShapeDtypeStruct((count, 10 * LANES), bf16)
    return pl.pallas_call(
        pack_kernel,
        out_shape=(shape, shape),
        in_specs=[SMEM_SPEC] + [VMEM_SPEC] * 4,
        out_specs=(VMEM_SPEC, VMEM_SPEC),
        compiler_params=pltpu.CompilerParams(vmem_limit_bytes=24 << 20),
        cost_estimate=FREE,
        name="pack_heads",
    )(info, w_query, w_key, w_value, w_out)


def whole(shape):
    return pl.BlockSpec(shape, lambda i: (0,) * len(shape), pipeline_mode=pl.Buffered(1))


ROOMY = pltpu.CompilerParams(vmem_limit_bytes=52 << 20)


def tail_lanes(shape, at, size):
    lane = lax.broadcasted_iota(jnp.int32, shape, 1)
    return (lane >= at) & (lane < at + size)


def tail_parts(tail, size):
    return pltpu.roll(tail, 2 * size, 1), pltpu.roll(tail, size, 1)


def gate_kernel(size, first_ref, second_ref, w_ref, *refs):
    gate_up_ref, main_ref, tail_ref = refs[-3:]
    width = main_ref.shape[1]

    def project(rows):
        gate_up = dot(rows, w_ref[...])
        gate_up_ref[...] = gate_up
        gate, up = gate_up[:, :width], gate_up[:, width : 2 * width]
        main_ref[...] = (gate * jax.nn.sigmoid(gate) * up).astype(bf16)
        gate, up = tail_parts(gate_up[:, 2 * width :], size)
        tail = gate * jax.nn.sigmoid(gate) * up
        tail_ref[...] = jnp.where(tail_lanes(tail.shape, 2 * size, size), tail, 0.0).astype(bf16)

    pl.when(pl.program_id(0) == 0)(lambda: project(first_ref[...]))
    pl.when(pl.program_id(0) == 1)(lambda: project(second_ref[...]))


def gate_blocks(blocks, places, gu_w, width, size, earlier):
    count, depth = blocks[0].shape
    cols = gu_w.shape[1]
    at, step = places[0], places[1] - places[0]
    widths = (cols, width, cols - 2 * width)
    return pl.pallas_call(
        functools.partial(gate_kernel, size),
        grid=(2,),
        out_shape=tuple(
            jax.ShapeDtypeStruct((8 * count, w), kind) for w, kind in zip(widths, (f32, bf16, bf16))
        ),
        in_specs=[whole((count, depth))] * 2
        + [whole((depth, cols))]
        + [pl.BlockSpec(memory_space=pl.ANY)] * len(earlier),
        out_specs=tuple(pl.BlockSpec((count, w), lambda i: (at + step * i, 0)) for w in widths),
        input_output_aliases={3: 0, 4: 1, 5: 2} if earlier else {},
        compiler_params=ROOMY,
        cost_estimate=pl.CostEstimate(flops=8 * count * depth * cols, bytes_accessed=1024, transcendentals=0),
        name="gate_blocks",
    )(*blocks, gu_w, *earlier)


def gate_back(d_hidden, gate, up):
    sigmoid_gate = jax.nn.sigmoid(gate)
    d_gate = d_hidden * up * sigmoid_gate * (1.0 + gate * (1.0 - sigmoid_gate))
    return d_gate, d_hidden * (gate * sigmoid_gate)


def hidden_back_kernel(size, rows_ref, w_ref, tail_w_ref, gate_up_ref, out_ref):
    width = w_ref.shape[1]
    rows = rows_ref[...]
    d_gate, d_up = gate_back(
        dot(rows, w_ref[...]), gate_up_ref[:, :width], gate_up_ref[:, width : 2 * width]
    )
    out_ref[:, :width] = d_gate.astype(bf16)
    out_ref[:, width : 2 * width] = d_up.astype(bf16)
    gate, up = tail_parts(gate_up_ref[:, 2 * width :], size)
    d_gate, d_up = gate_back(dot(rows, tail_w_ref[...]), gate, up)
    lanes = d_gate.shape[1]
    d_gate = pltpu.roll(d_gate, lanes - 2 * size, 1)
    d_up = pltpu.roll(d_up, lanes - size, 1)
    tail = jnp.where(tail_lanes(d_up.shape, size, size), d_up, 0.0)
    tail = jnp.where(tail_lanes(d_up.shape, 0, size), d_gate, tail)
    out_ref[:, 2 * width :] = tail.astype(bf16)


def hidden_back(rows, down_w, gu_w, gate_up, size):
    count, depth = rows.shape
    width, cols = down_w.shape[1], gate_up.shape[1]
    tail = cols - 2 * width
    tile = count // 2
    return pl.pallas_call(
        functools.partial(hidden_back_kernel, size),
        grid=(2,),
        out_shape=jax.ShapeDtypeStruct((count, cols), bf16),
        in_specs=[
            pl.BlockSpec((tile, depth), lambda i: (i, 0)),
            whole((depth, width)),
            pl.BlockSpec((depth, tail), lambda i: (0, 2 * width // tail), pipeline_mode=pl.Buffered(1)),
            pl.BlockSpec((tile, cols), lambda i: (i, 0)),
        ],
        out_specs=pl.BlockSpec((tile, cols), lambda i: (i, 0)),
        compiler_params=ROOMY,
        cost_estimate=FREE,
        name="hidden_back",
    )(rows, down_w, gu_w, gate_up)


def rows_kernel(rows_ref, w_ref, *refs):
    refs[-1][...] = dot(rows_ref[...], w_ref[...])


def project_half(rows, weight, cols, earlier):
    count, depth = rows.shape
    tile = count // 4
    at = 0 if earlier is None else 4
    earlier = () if earlier is None else (earlier,)
    return pl.pallas_call(
        rows_kernel,
        grid=(4,),
        out_shape=jax.ShapeDtypeStruct((2 * count, cols), f32),
        in_specs=[
            pl.BlockSpec((tile, depth), lambda i: (i, 0)),
            pl.BlockSpec((depth, cols), lambda i: (0, 0), pipeline_mode=pl.Buffered(1)),
        ]
        + [pl.BlockSpec(memory_space=pl.ANY)] * len(earlier),
        out_specs=pl.BlockSpec((tile, cols), lambda i: (i + at, 0)),
        input_output_aliases={2: 0} if earlier else {},
        compiler_params=ROOMY,
        cost_estimate=FREE,
        name="project_half",
    )(rows, weight, *earlier)


def grads_kernel(place, counts, *refs):
    out_ref = refs[-1]
    products, at = [], 0
    for count in counts:
        left = jnp.concatenate([ref[...] for ref in refs[at : at + count]], axis=0)
        products.append(dot(left, refs[at + count][...], TN))
        at += count + 1
    place(out_ref, *products)


def place_one(out_ref, product):
    out_ref[...] = product.astype(bf16)


def place_tail(out_ref, first, second):
    start = first.shape[1] - second.shape[1]
    out_ref[:, :start] = first[:, :start].astype(bf16)
    out_ref[:, start:] = (first[:, start:] + second).astype(bf16)


def place_heads(out_ref, first, second):
    start = first.shape[1] - LANES
    out_ref[:, :start] = first[:, :start].astype(bf16)
    out_ref[:, start : start + LANES] = (first[:, start:] + second[:, :LANES]).astype(bf16)
    out_ref[:, start + LANES :] = second[:, LANES:].astype(bf16)


def weight_grads(place, cols, tile, *products):
    depth = products[0][0][0].shape[1]
    specs, operands = [], []
    for pieces, right in products:
        specs += [pl.BlockSpec((piece.shape[0], tile), lambda i: (0, i)) for piece in pieces]
        specs += [whole(right.shape)]
        operands += [*pieces, right]
    counts = [len(pieces) for pieces, _ in products]
    return pl.pallas_call(
        functools.partial(grads_kernel, place, counts),
        grid=(depth // tile,),
        out_shape=jax.ShapeDtypeStruct((depth, cols), bf16),
        in_specs=specs,
        out_specs=pl.BlockSpec((tile, cols), lambda i: (i, 0)),
        compiler_params=ROOMY,
        cost_estimate=FREE,
        name="weight_grads",
    )(*operands)


def shards(
    tokens,
    w_query,
    w_key,
    w_value,
    w_out,
    gain_attn,
    w_gate,
    w_up,
    w_down,
    gain_mlp,
    cotangent,
    lineage,
    padding,
    positions,
):
    slot = lineage.shape[1]
    on_x, on_mp = lax.axis_index("ctx"), lax.axis_index("mp")
    on_y, on_core = on_mp // 2, on_mp % 2
    lower_x = on_x == 0
    heads = w_query.shape[1] // HEAD_DIM
    own_cols = heads // 2 * HEAD_DIM
    ff_half = w_gate.shape[1] // 2
    ff_main = ff_half // LANES * LANES
    ff_tail = ff_half - ff_main

    info, back = [], []
    for n in range(8):
        d_x, d_y, d_core = on_x ^ (n // 4), on_y ^ (n // 2 % 2), on_core ^ (n % 2)
        info.append(d_core * 4 + d_x * 2 + d_y)
        from_x, from_y, from_core = on_x ^ (n // 2 % 2), on_y ^ (n % 2), on_core ^ (n // 4)
        back.append(from_x * 4 + from_y * 2 + from_core)
    info = jnp.stack(info + [on_x] + back).astype(jnp.int32)

    gain_a = gain_attn.astype(f32)
    gain_m = gain_mlp.astype(f32)
    inputs = tokens.astype(f32)
    grad_rows = cotangent.astype(f32)

    def both_x(mine, theirs):
        got = flip_x(theirs)
        return jnp.where(lower_x, jnp.concatenate([mine, got], 0), jnp.concatenate([got, mine], 0))

    attn_mine, attn_theirs = pack_heads(info, w_query, w_key, w_value, w_out)

    def halves(weight):
        first, second = weight[:, :ff_half], weight[:, ff_half:]
        return jnp.where(lower_x, first, second), jnp.where(lower_x, second, first)

    def pack_hidden(gate, up, down):
        fill = jnp.zeros((gate.shape[0], 2 * LANES - 3 * ff_tail), bf16)
        tails = [w[:, ff_main:] for w in (gate, up, down)]
        return jnp.concatenate([gate[:, :ff_main], up[:, :ff_main]] + tails + [fill], axis=1)

    index = jnp.arange(slot, dtype=jnp.int32)
    own_seg = lineage[0]
    related = (
        (own_seg[:, None] == lineage[0][None, :])
        | (own_seg[:, None] == lineage[1][None, :])
        | (own_seg[:, None] == lineage[2][None, :])
    )
    live = padding == 0
    allowed = (index[:, None] == index[None, :]) | (
        related & live[:, None] & live[None, :] & (index[:, None] < index[None, :])
    )
    bias = jnp.where(allowed, 0.0, masked_value).astype(f32)
    half_dim = HEAD_DIM // 2
    inv_freq = rope_base ** (-2.0 * jnp.arange(half_dim, dtype=f32) / HEAD_DIM)
    angles = positions.astype(f32)[:, None] * inv_freq[None, :]
    cos, sin = jnp.cos(angles), jnp.sin(angles)
    cosine = jnp.concatenate([cos, cos, cos, cos], axis=1)
    sine = jnp.concatenate([-sin, sin, -sin, sin], axis=1)

    def rows_of_x(field):
        rows = field.shape[0] // 2
        mine = jnp.where(lower_x, field[:rows], field[rows:])
        return mine, flip_x(jnp.where(lower_x, field[rows:], field[:rows]))

    attn_got = flip_x(attn_theirs)
    count, on_dp = lax.axis_size("dp"), lax.axis_index("dp")

    def from_dp(field, k):
        return lax.ppermute(field, "dp", [(i, i ^ k) for i in range(count)])

    arrived = [from_dp(attn_mine, k) for k in range(1, count)]
    _, own_rows = after(attn_got, (normalize(inputs) * gain_a).astype(bf16))
    near_a, arrived[:2] = gather_near(own_rows, arrived[:2])
    near_a, arrived[2:], w_gate, w_up, w_down = after(near_a, arrived[2:], w_gate, w_up, w_down)
    gate_mine, gate_theirs = halves(w_gate)
    up_mine, up_theirs = halves(w_up)
    down_mine, down_theirs = halves(w_down.T)
    gu_part = both_x(
        pack_hidden(gate_mine, up_mine, down_mine), pack_hidden(gate_theirs, up_theirs, down_theirs)
    )
    block = (1, 1) + attn_mine.shape
    attn_w = jnp.zeros((count, 2) + attn_mine.shape, bf16)
    for k, field in enumerate([attn_mine] + arrived):
        attn_w = lax.dynamic_update_slice(attn_w, field.reshape(block), (on_dp ^ k, on_x, 0, 0))
    attn_all = lax.all_gather(attn_got, "dp", axis=0, tiled=False)
    near_a, gu_part, attn_all, attn_w, bias, cosine, sine = after(
        near_a, gu_part, attn_all, attn_w, bias, cosine, sine
    )
    far_a = flip_core(near_a)
    attn_w = lax.dynamic_update_slice(attn_w, attn_all[:, None], (0, 1 - on_x, 0, 0))
    attn_w = attn_w.reshape(count * 2 * attn_mine.shape[0], attn_mine.shape[1])
    gu_w = lax.all_gather(gu_part, "dp", axis=0, tiled=True)
    qkv_w = attn_w[:, : 8 * LANES]
    out_w = attn_w[:, 7 * LANES :]
    qkv = project_half(far_a, attn_w, 8 * LANES, project_half(near_a, attn_w, 8 * LANES, None))
    qkv, down_mine, down_theirs, grad_rows = after(
        qkv, down_mine[:, :ff_main], down_theirs[:, :ff_main], grad_rows
    )
    near_d, far_d = gather_rows((branch_scale * grad_rows).astype(bf16))
    d_mlp = jnp.concatenate([near_d, far_d], axis=0)
    down_part = both_x(down_mine, down_theirs)
    rotated, mixed, log_total = attention_forward(info, qkv, cosine, sine, bias)
    residual = inputs + branch_scale * sum_rows(mixed, out_w, NT, pieces=4)
    own_m, gu_w, d_mlp = after((normalize(residual) * gain_m).astype(bf16), gu_w, d_mlp)
    down_w = lax.all_gather(down_part, "dp", axis=0, tiled=True)
    half = own_m.shape[0] // 2
    from_x, from_y, own_c = flip_x(own_m), flip_y(own_m), flip_core(own_m)
    gates = gate_blocks((own_m, own_c), (0, 4), gu_w, ff_main, ff_tail, ())
    from_x, from_y, gates = after(from_x, from_y, gates)
    corner = jnp.concatenate([flip_y(from_x[:half]), flip_x(from_y[half:])], axis=0)
    y_c, x_c = flip_core(from_y), flip_core(from_x)
    gates = gate_blocks((from_y, from_x), (1, 2), gu_w, ff_main, ff_tail, gates)
    corner, gates = after(corner, gates)
    corner_c = flip_core(corner)
    gates = gate_blocks((y_c, x_c), (5, 6), gu_w, ff_main, ff_tail, gates)
    gates = gate_blocks((corner, corner_c), (3, 7), gu_w, ff_main, ff_tail, gates)
    gate_up, hidden, hidden_tail = gates
    all_m = (own_m, from_y, from_x, corner, own_c, y_c, x_c, corner_c)

    grad_down = weight_grads(place_one, ff_main, 6 * LANES, ((near_d, far_d), hidden))
    gate_up, grad_down = after(gate_up, grad_down)
    grad_down = lax.psum_scatter(grad_down, "dp", scatter_dimension=0, tiled=True)
    d_gate_up = hidden_back(d_mlp, down_w, gu_w, gate_up, ff_tail)
    grad_gu = weight_grads(
        place_tail,
        gate_up.shape[1],
        3 * LANES,
        (all_m, d_gate_up),
        ((near_d, far_d), hidden_tail),
    )
    d_gate_up, grad_gu = after(d_gate_up, grad_gu)
    grad_gu = lax.psum_scatter(grad_gu, "dp", scatter_dimension=0, tiled=True)
    d_normed_mlp, grad_down = sum_rows(d_gate_up, gu_w, NT, grad_down)
    back_mlp, gain_mlp_part = norm_back(residual, gain_m, d_normed_mlp)
    d_residual = grad_rows + back_mlp

    near_o, far_o = gather_rows((branch_scale * d_residual).astype(bf16))
    d_mixed_near, d_mixed_far = dot(near_o, out_w).astype(bf16), dot(far_o, out_w).astype(bf16)
    d_qkv = attention_backward(
        info, rotated, cosine, sine, bias, mixed, d_mixed_near, d_mixed_far, log_total
    )
    grad_attn = weight_grads(
        place_heads, 10 * LANES, 3 * LANES, ((near_a, far_a), d_qkv), ((near_o, far_o), mixed)
    )
    grad_attn, grad_gu, d_qkv, hidden = after(grad_attn, grad_gu, d_qkv, hidden)
    grad_attn = lax.psum_scatter(grad_attn, "dp", scatter_dimension=0, tiled=True)
    tail_mine, tail_got = rows_of_x(grad_gu[:, 2 * ff_main :])
    tail_got, d_qkv, hidden, grad_gu = after(tail_got, d_qkv, hidden, grad_gu)
    gu_mine, gu_got = rows_of_x(grad_gu[:, : 2 * ff_main])
    d_normed_attn = sum_rows(d_qkv, qkv_w, NT, pieces=4)
    back_attn, gain_attn_part = norm_back(inputs, gain_a, d_normed_attn)
    input_grad = d_residual + back_attn
    gains, grad_attn = sum_all(jnp.stack([gain_attn_part, gain_mlp_part]), grad_attn)
    hidden = jnp.concatenate([hidden, hidden_tail], axis=1)
    down_w = jnp.concatenate([down_w, gu_w[:, 2 * ff_main :]], axis=1)
    output = residual + branch_scale * sum_rows(hidden, down_w, NT, pieces=4)

    def join(mine, got):
        mine, got = mine.astype(f32), got.astype(f32)
        return jnp.where(lower_x, jnp.concatenate([mine, got], 1), jnp.concatenate([got, mine], 1))

    def join_heads(mine, got, at, shared_at):
        whole = join(mine[:, at : at + own_cols], got[:, at : at + own_cols])
        last = slice(shared_at, shared_at + HEAD_DIM)
        return jnp.concatenate([whole, mine[:, last].astype(f32) + got[:, last].astype(f32)], axis=1)

    down_mine, down_got = rows_of_x(grad_down)

    def join_hidden(mine, got, at):
        last = slice(at * ff_tail, (at + 1) * ff_tail)
        mine = jnp.concatenate([mine, tail_mine[:, last]], axis=1)
        return join(mine, jnp.concatenate([got, tail_got[:, last]], axis=1))

    grad_gate = join_hidden(gu_mine[:, :ff_main], gu_got[:, :ff_main], 0)
    up_lanes = slice(ff_main, 2 * ff_main)
    grad_up = join_hidden(gu_mine[:, up_lanes], gu_got[:, up_lanes], 1)
    grad_down = join_hidden(down_mine, down_got, 2).T
    mine, got = rows_of_x(grad_attn)
    grad_query = join_heads(mine, got, 0, 6 * LANES)
    grad_key = join_heads(mine, got, 2 * LANES, 6 * LANES + HEAD_DIM)
    grad_value = join_heads(mine, got, 4 * LANES, 7 * LANES)
    grad_out = join_heads(mine, got, 8 * LANES, 7 * LANES + HEAD_DIM).T

    return (
        output.astype(bf16),
        input_grad.astype(bf16),
        grad_query,
        grad_key,
        grad_value,
        grad_out,
        gains[0],
        grad_gate,
        grad_up,
        grad_down,
        gains[1],
    )


def solution(mesh):
    placed = (
        P(("dp", "ctx", "mp"), None),
        P(("dp", "ctx"), "mp"),
        P(("dp", "ctx"), "mp"),
        P(("dp", "ctx"), "mp"),
        P("mp", ("dp", "ctx")),
        P(),
        P(("dp", "ctx"), "mp"),
        P(("dp", "ctx"), "mp"),
        P("mp", ("dp", "ctx")),
        P(),
        P(("dp", "ctx", "mp"), None),
        P(None, "dp"),
        P("dp"),
        P("dp"),
    )
    return jax.shard_map(
        shards,
        mesh=mesh,
        in_specs=placed,
        out_specs=(
            P(("dp", "ctx", "mp"), None),
            P(("dp", "ctx", "mp"), None),
            P(("dp", "ctx"), "mp"),
            P(("dp", "ctx"), "mp"),
            P(("dp", "ctx"), "mp"),
            P("mp", ("dp", "ctx")),
            P(),
            P(("dp", "ctx"), "mp"),
            P(("dp", "ctx"), "mp"),
            P("mp", ("dp", "ctx")),
            P(),
        ),
        check_vma=False,
    )
```
